32 devices in a mesh: row: 8 (over y, x, core), col: 4 (over z).
Axes of the slice: x: 2, y: 2, z: 4, core: 2. Of those that a mesh axis runs over, the one named last changes fastest.
Arguments:
- features: bfloat16 [16384, 256], P('row', 'col'), may hold values from -12 to 12
- tile_vals: bfloat16 [1024, 512, 128], P('row', 'col'), may hold values from 0 to 4, as said below
- tile_src: int32 [8, 512], P('row', 'col'), may hold values from 0 to 15
- row_counts: int32 [8, 128], P('row', 'col'), may hold values from 1 to 6, as said below
Outputs:
- propagated: bfloat16 [16384, 256], P(('row', 'col'))
The draws below stay inside these ranges and needn't reach their ends.
Inputs may be any that keep to these rules, and one draw needn't show every extreme that they name: `tile_vals`: each entry is zero or a weight between 0.25 and 4. `row_counts`: on every group the 32 counts sum to at most 128; some groups reach 128 exactly.
All inputs are finite; a program needn't handle non-finite values.
Results may differ from the reference program's by a relative error of at most 0.009.
Values may be sent and summed in bfloat16 or wider, within the bound.
No kernel may reach another device: no remote copies, remote signals or barrier semaphores. Data moves between devices by JAX's collectives and lax.ppermute only.
A program may use at most 128 MiB of HBM per device.

```python
import math
import jax
import jax.numpy as jnp
from jax import lax

F = 256
S = 512
TILE = 128
ITERS = 3
DT = 32
ST = 16
TILE_MAX = 128
NODES = 16384
N_ROW = 8
N_COL = 4


def draw_tile_vals(key, part):
    key_edges, key_weights = jax.random.split(key)
    shape_all = (N_ROW * TILE_MAX, N_COL * TILE, TILE)
    edge_mask = jax.random.randint(key_edges, shape_all, 0, TILE) == 0
    weights = jnp.exp(jax.random.uniform(key_weights, shape_all, jnp.float32, math.log(0.25), math.log(4.0)))
    return jnp.where(edge_mask, weights, 0.0).astype(jnp.bfloat16)


def draw_row_counts(key, part):
    devices = N_ROW * N_COL
    half_rows = DT // 2
    key_light, key_base, key_shuffle, key_pick = jax.random.split(key, 4)
    lighter = jax.random.randint(key_light, (devices, DT), 1, 4)
    base_counts = jax.random.randint(key_base, (devices, half_rows), 2, 7)
    heavier = jnp.concatenate([base_counts, 8 - base_counts], axis=1)
    shuffle = jax.vmap(lambda one_key: jax.random.permutation(one_key, DT))(jax.random.split(key_shuffle, devices))
    heavier = jnp.take_along_axis(heavier, shuffle, axis=1)
    ranking = jax.random.permutation(key_pick, devices)
    chosen = (ranking < 4)[:, None]
    counts = jnp.where(chosen, heavier, lighter)
    return counts.reshape(N_ROW, N_COL * DT).astype(jnp.int32)


def place_ends(values, rng, least, top_value):
    longest = values.shape.index(max(values.shape))
    spots = []
    for shift in (0, 1):
        where = [jax.random.randint(jax.random.fold_in(rng, axis), (), 0, length) for axis, length in enumerate(values.shape)]
        where[longest] = (where[longest] + shift) % values.shape[longest]
        spots.append(tuple(where))
    return values.at[spots[0]].set(least).at[spots[1]].set(top_value)


def level_of(own_key, dims, pieces, least, top_value):
    def one(position, shards_of):
        draws = jax.random.uniform(jax.random.fold_in(jax.random.fold_in(own_key, 6), position), (shards_of,), jnp.float32, least / len(pieces), top_value / len(pieces))
        return jnp.repeat(jnp.exp(draws), dims[position] // shards_of).reshape((-1,) + (1,) * (len(dims) - position - 1))

    gain = one(*pieces[0])
    for cut in pieces[1:]:
        gain = gain * one(*cut)
    return gain


def noise(stream_key, dims, deviation, bound, cuts=(), held_as=jnp.bfloat16):
    level = level_of(stream_key, dims, cuts, -0.22, 0.18) if cuts else 1.0
    values = jax.random.normal(stream_key, dims, jnp.float32) * deviation * level
    return jnp.minimum(jnp.maximum(values, -bound), bound).astype(held_as)


def setup_inputs(seed: int = 0) -> dict:
    seeds = jax.random.split(jax.random.key(seed), 5)
    features = noise(seeds[0], (NODES, F), 2.0, 12.0, ((0, 8), (1, 4)))
    tile_vals = draw_tile_vals(jax.random.fold_in(seeds[4], 71), 0)
    tile_src = place_ends(jax.random.randint(seeds[2], (N_ROW, N_COL * TILE_MAX), 0, ST), jax.random.fold_in(seeds[2], 1), 0, ST - 1).astype(jnp.int32)
    row_counts = draw_row_counts(jax.random.fold_in(seeds[4], 71), 0)
    return {"features": features, "tile_vals": tile_vals, "tile_src": tile_src, "row_counts": row_counts}


TELEPORT = 0.1


def slot_layout(counts):
    row_ends = jnp.cumsum(counts, dtype=jnp.int32)
    slot_ids = jnp.arange(TILE_MAX, dtype=jnp.int32)
    dest_tiles = jnp.sum((row_ends[None, :] <= slot_ids[:, None]).astype(jnp.int32), axis=1, dtype=jnp.int32)
    live_slots = slot_ids < row_ends[DT - 1]
    return dest_tiles, live_slots


def group_inputs(group, tile_vals, tile_src, row_counts):
    group = group.astype(jnp.int32)
    row_index = group // N_COL
    col_index = group % N_COL
    tile_block = lax.dynamic_slice_in_dim(tile_vals, (row_index * TILE_MAX).astype(jnp.int32), TILE_MAX, 0)
    tile_block = lax.dynamic_slice_in_dim(tile_block, (col_index * TILE).astype(jnp.int32), TILE, 1)
    src_line = lax.dynamic_index_in_dim(tile_src, row_index, 0, keepdims=False)
    sources = lax.dynamic_slice_in_dim(src_line, (col_index * TILE_MAX).astype(jnp.int32), TILE_MAX, 0)
    count_line = lax.dynamic_index_in_dim(row_counts, row_index, 0, keepdims=False)
    counts = lax.dynamic_slice_in_dim(count_line, (col_index * DT).astype(jnp.int32), DT, 0)
    return row_index, col_index, tile_block, sources, counts


def reference(features, tile_vals, tile_src, row_counts):
    groups = N_ROW * N_COL

    def degree_step(group, running):
        row_index, col_index, tile_block, sources, counts = group_inputs(group, tile_vals, tile_src, row_counts)
        dest_tiles, live_slots = slot_layout(counts)
        column_sums = jnp.sum(tile_block.astype(jnp.float32), axis=1)
        column_sums = jnp.where(live_slots[:, None], column_sums, 0.0)
        weight_sums = jnp.zeros((DT, TILE), jnp.float32).at[dest_tiles].add(column_sums, mode="drop")
        return running.at[:, col_index].add(weight_sums.reshape(N_ROW, S))

    weight_total = lax.fori_loop(0, groups, degree_step, jnp.zeros((N_ROW, N_COL, S), jnp.float32))
    degree = 1.0 + weight_total.reshape(NODES)
    restart = TELEPORT * features.astype(jnp.float32)
    iterate = features
    for iteration in range(ITERS):
        def product_step(group, running, iterate=iterate):
            row_index, col_index, tile_block, sources, counts = group_inputs(group, tile_vals, tile_src, row_counts)
            dest_tiles, live_slots = slot_layout(counts)
            source_rows = lax.dynamic_slice_in_dim(iterate, (row_index * (N_COL * S)).astype(jnp.int32), N_COL * S, 0)
            grouped = source_rows.reshape(ST, TILE, F)
            picked = jnp.take(grouped, sources, axis=0).astype(jnp.float32)
            products = jnp.einsum("tsd,tsf->tdf", tile_block.astype(jnp.float32), picked, precision=lax.Precision.HIGHEST)
            products = jnp.where(live_slots[:, None, None], products, 0.0)
            summed_tiles = jnp.zeros((DT, TILE, F), jnp.float32).at[dest_tiles].add(products, mode="drop")
            rounded = lax.optimization_barrier(summed_tiles.astype(jnp.bfloat16)).astype(jnp.float32)
            return running.at[:, col_index].add(rounded.reshape(N_ROW, S, F))

        summed = lax.fori_loop(0, groups, product_step, jnp.zeros((N_ROW, N_COL, S, F), jnp.float32)).reshape(NODES, F)
        iterate = ((1.0 - TELEPORT) * (summed + iterate.astype(jnp.float32)) / degree[:, None] + restart).astype(jnp.bfloat16)
    return iterate
```

```python
import functools

import jax
import jax.numpy as jnp
from jax import lax
from jax.experimental import pallas as pl
from jax.experimental.pallas import tpu as pltpu
from jax.sharding import PartitionSpec as P

ITERS = 3


TELEPORT = 0.1


CHUNKS = 2


UNROLL = 8


def vmem(count):
    return [pl.BlockSpec(memory_space=pltpu.VMEM)] * count


def smem(count):
    return [pl.BlockSpec(memory_space=pltpu.SMEM)] * count


def pair_capacity(tile_max, dest_count):
    most = (tile_max + dest_count // 2) // 2
    return -(-most // UNROLL) * UNROLL


def prepare_kernel(
    tiles_per_owner,
    place_ref,
    src_ref,
    count_ref,
    tile_ref,
    turned_ref,
    weight_ref,
    slot_ref,
    first_ref,
    second_ref,
    row_ref,
    go_on_ref,
    turns_ref,
):
    tile_max, tile_size, _ = tile_ref.shape
    dest_count = count_ref.shape[1]
    capacity = slot_ref.shape[1]
    zero_tile = place_ref[2]
    my_row = place_ref[0]

    for half in range(2):

        def one_dest(dest, carry, half=half):
            start, used = carry
            owner = dest // tiles_per_owner
            relative = lax.bitwise_xor(owner, my_row)
            count = count_ref[0, dest]
            mine = lax.bitwise_and(relative, 1) == half
            pairs = jnp.where(mine, (count + 1) // 2, 0)
            out_row = (
                (relative // 2) * tiles_per_owner + dest - owner * tiles_per_owner
            ) * tile_size

            def one_pair(pair, carry):
                at = used + pair
                slot = start + 2 * pair
                next_slot = jnp.minimum(slot + 1, tile_max - 1)
                slot_ref[half, at] = slot
                first_ref[half, at] = src_ref[0, slot] * tile_size
                second_ref[half, at] = (
                    jnp.where(2 * pair + 1 < count, src_ref[0, next_slot], zero_tile) * tile_size
                )
                row_ref[half, at] = out_row
                go_on_ref[half, at] = jnp.where(pair > 0, 1, 0)
                return carry

            lax.fori_loop(0, pairs, one_pair, 0)
            return start + count, used + pairs

        _, used = lax.fori_loop(0, dest_count, one_dest, (jnp.int32(0), jnp.int32(0)))
        turns = (used + UNROLL - 1) // UNROLL
        last_row = row_ref[half, used - 1]

        def one_pad(at, carry, half=half, last_row=last_row):
            slot_ref[half, at] = 0
            first_ref[half, at] = zero_tile * tile_size
            second_ref[half, at] = zero_tile * tile_size
            row_ref[half, at] = last_row
            go_on_ref[half, at] = 1
            return carry

        lax.fori_loop(used, turns * UNROLL, one_pad, 0)
        turns_ref[half] = turns

    def one_turn(dest, start):
        count = count_ref[0, dest]
        owner = dest // tiles_per_owner
        relative = lax.bitwise_xor(owner, my_row)

        def one_slot(slot, running):
            tile = tile_ref[slot]
            turned_ref[slot] = tile.T
            return running + jnp.sum(tile.astype(jnp.float32), axis=0, keepdims=True)

        total = lax.fori_loop(
            start, start + count, one_slot, jnp.zeros((1, tile_size), jnp.float32)
        )
        weight_ref[relative, pl.ds(dest - owner * tiles_per_owner, 1), :] = total
        return start + count

    live = lax.fori_loop(0, dest_count, one_turn, jnp.int32(0))

    def one_dead(slot, carry):
        turned_ref[slot] = jnp.zeros((tile_size, tile_size), turned_ref.dtype)
        return carry

    lax.fori_loop(live, tile_max, one_dead, 0)


def prepare(place, tile_src, row_counts, tile_vals, row_size, tiles_per_owner):
    tile_max, tile_size, _ = tile_vals.shape
    capacity = pair_capacity(tile_max, row_counts.shape[1])
    listing = jax.ShapeDtypeStruct((2, capacity), jnp.int32)
    return pl.pallas_call(
        functools.partial(prepare_kernel, tiles_per_owner),
        out_shape=[
            jax.ShapeDtypeStruct(tile_vals.shape, tile_vals.dtype),
            jax.ShapeDtypeStruct((row_size, tiles_per_owner, tile_size), jnp.float32),
            listing,
            listing,
            listing,
            listing,
            listing,
            jax.ShapeDtypeStruct((2,), jnp.int32),
        ],
        in_specs=smem(3) + vmem(1),
        out_specs=vmem(2) + smem(6),
        compiler_params=pltpu.CompilerParams(vmem_limit_bytes=24 * 2**20),
        name="prepare",
    )(place, tile_src, row_counts, tile_vals)


def product_kernel(
    half,
    packed,
    blocks,
    place_ref,
    slot_ref,
    first_ref,
    second_ref,
    row_ref,
    go_on_ref,
    turns_ref,
    turned_ref,
    *refs,
):
    block_refs = refs[: 2 * blocks - 1]
    out_ref = refs[2 * blocks - 1]
    own_ref = refs[2 * blocks] if packed else None
    held_ref = refs[-2 if packed else -1]
    staged_ref = refs[-1] if packed else held_ref
    col = place_ref[1]
    rows, width = block_refs[0].shape
    tile_size = turned_ref.shape[1]

    def put(block, ref):
        staged_ref[pl.ds(pl.multiple_of(block * rows, rows), rows), :] = ref[...]

    put(col, block_refs[0])
    for step in range(1, blocks):
        pl.when(col >= step)(functools.partial(put, col - step, block_refs[2 * step - 1]))
        pl.when(col + step < blocks)(functools.partial(put, col + step, block_refs[2 * step]))
    if packed:
        piece = width // blocks
        for group in range(blocks):
            lanes = slice(group * piece, (group + 1) * piece)
            held_ref[group * rows : (group + 1) * rows, :] = jnp.concatenate(
                [staged_ref[b * rows : (b + 1) * rows, lanes] for b in range(blocks)], axis=1
            )
        own_ref[...] = held_ref[pl.ds(pl.multiple_of(col * rows, rows), rows), :]
    held_ref[blocks * rows :, :] = jnp.zeros((tile_size, width), held_ref.dtype)

    tile_max = turned_ref.shape[0]

    def one_turn(turn, running):
        for step in range(UNROLL):
            at = turn * UNROLL + step
            slot = slot_ref[half, at]
            left = jnp.concatenate(
                [turned_ref[slot], turned_ref[jnp.minimum(slot + 1, tile_max - 1)]], axis=1
            )
            first = pl.multiple_of(first_ref[half, at], tile_size)
            second = pl.multiple_of(second_ref[half, at], tile_size)
            right = jnp.concatenate(
                [held_ref[pl.ds(first, tile_size), :], held_ref[pl.ds(second, tile_size), :]],
                axis=0,
            )
            term = jnp.dot(left, right, preferred_element_type=jnp.float32)
            running = running * go_on_ref[half, at].astype(jnp.float32) + term
            out_row = pl.multiple_of(row_ref[half, at], tile_size)
            out_ref[pl.ds(out_row, tile_size), :] = running.astype(out_ref.dtype)
        return running

    lax.fori_loop(0, turns_ref[half], one_turn, jnp.zeros((tile_size, width), jnp.float32))


def product(half, place, lists, turned, gathered, blocks, row_size, packed):
    rows, width = gathered[0].shape
    tile_size = turned.shape[1]
    out_shape = [jax.ShapeDtypeStruct((row_size // 2 * rows, width), jnp.bfloat16)]
    scratch = [pltpu.VMEM((blocks * rows + tile_size, width), jnp.bfloat16)]
    if packed:
        out_shape.append(jax.ShapeDtypeStruct((rows, width), jnp.bfloat16))
        scratch.append(pltpu.VMEM((blocks * rows, width), jnp.bfloat16))
    return pl.pallas_call(
        functools.partial(product_kernel, half, packed, blocks),
        out_shape=out_shape,
        in_specs=smem(1 + len(lists)) + vmem(1 + len(gathered)),
        out_specs=vmem(len(out_shape)),
        scratch_shapes=scratch,
        compiler_params=pltpu.CompilerParams(vmem_limit_bytes=24 * 2**20),
        name="product",
    )(place, *lists, turned, *gathered)


def gather_line(block, size):
    found = [block]
    from_left = from_right = block
    for step in range(1, size):
        from_left = lax.ppermute(from_left, "col", [(i, i + 1) for i in range(step - 1, size - 1)])
        from_right = lax.ppermute(from_right, "col", [(i, i - 1) for i in range(1, size - step + 1)])
        found += [from_left, from_right]
    return found


def swap(block, bit, row_size):
    return lax.ppermute(block, "row", [(i, i ^ (1 << bit)) for i in range(row_size)])


def halve(state, bits, order, row_size):
    bits = list(bits)
    for bit in order:
        axis = bits.index(bit)
        send = lax.index_in_dim(state, 1, axis, keepdims=False).astype(jnp.bfloat16)
        keep = lax.index_in_dim(state, 0, axis, keepdims=False)
        state = keep + swap(send, bit, row_size).astype(jnp.float32)
        bits.remove(bit)
    return state


def on_device(features, tile_vals, tile_src, row_counts):
    row_size = lax.axis_size("row")
    blocks = lax.axis_size("col")
    my_row = lax.axis_index("row").astype(jnp.int32)
    my_col = lax.axis_index("col").astype(jnp.int32)
    tile_size = tile_vals.shape[1]
    dest_count = row_counts.shape[1]
    rows = features.shape[0] // blocks
    source_tiles = features.shape[0] // tile_size
    width = features.shape[1] * blocks // CHUNKS
    piece = features.shape[1] // CHUNKS
    tiles_per_owner = dest_count // row_size
    row_bits = row_size.bit_length() - 1
    chip_bits = list(range(row_bits - 1, 0, -1))
    place = jnp.stack([my_row, my_col, jnp.int32(source_tiles)])

    parts = features.reshape(blocks, rows, CHUNKS, piece).transpose(2, 1, 0, 3)
    parts = parts.reshape(CHUNKS, rows, blocks * piece)
    gathered = [gather_line(parts[chunk], blocks) for chunk in range(CHUNKS)]

    turned, weight_sums, *lists = prepare(
        place, tile_src, row_counts, tile_vals, row_size, tiles_per_owner
    )
    all_bits = [0] + chip_bits
    weights = weight_sums
    state = weights.reshape((2,) * row_bits + (tiles_per_owner, tile_size))
    bits = list(range(row_bits - 1, -1, -1))
    for bit in [0] + chip_bits:
        axis = bits.index(bit)
        send = lax.index_in_dim(state, 1, axis, keepdims=False)
        state = lax.index_in_dim(state, 0, axis, keepdims=False) + swap(send, bit, row_size)
        bits.remove(bit)
    scale = ((1.0 - TELEPORT) / (1.0 + state)).reshape(rows, 1)
    scale = jnp.broadcast_to(scale, (rows, width))

    iterates = [None] * CHUNKS
    restarts = [None] * CHUNKS
    for iteration in range(ITERS):
        for chunk in range(CHUNKS):
            packed = iteration == 0
            sent, *rest = product(
                1, place, lists, turned, gathered[chunk], blocks, row_size, packed
            )
            if packed:
                iterates[chunk] = rest[0]
                restarts[chunk] = TELEPORT * rest[0].astype(jnp.float32)
            other = swap(sent, 0, row_size)
            kept = product(0, place, lists, turned, gathered[chunk], blocks, row_size, packed)[0]
            shape = (2,) * len(chip_bits) + (2, rows // 2, width)
            state = kept.astype(jnp.float32) + other.astype(jnp.float32)
            state = state.reshape(shape)
            summed = []
            for half in range(2):
                turn = half % max(len(chip_bits), 1)
                order = chip_bits[turn:] + chip_bits[:turn]
                summed.append(
                    halve(state[..., half, :, :], chip_bits, order, row_size)
                )
            summed = jnp.concatenate(summed, axis=0)
            iterates[chunk] = (
                scale * (summed + iterates[chunk].astype(jnp.float32)) + restarts[chunk]
            ).astype(jnp.bfloat16)
            if iteration + 1 < ITERS:
                gathered[chunk] = gather_line(iterates[chunk], blocks)
    out = jnp.stack(iterates).reshape(CHUNKS, rows, blocks, piece).transpose(1, 2, 0, 3)
    return out.reshape(rows, CHUNKS * width)


def solution(mesh):
    placed = (P("row", "col"), P("row", "col", None), P("row", "col"), P("row", "col"))
    return jax.shard_map(
        on_device, mesh=mesh, in_specs=placed, out_specs=P(("row", "col"), None), check_vma=False
    )
```

```python
import functools

import jax
import jax.numpy as jnp
from jax import lax
from jax.experimental import pallas as pl
from jax.experimental.pallas import tpu as pltpu
from jax.sharding import PartitionSpec as P

ITERS = 3


TELEPORT = 0.1


CHUNKS = 2


UNROLL = 8


def vmem(count):
    return [pl.BlockSpec(memory_space=pltpu.VMEM)] * count


def smem(count):
    return [pl.BlockSpec(memory_space=pltpu.SMEM)] * count


def pair_capacity(tile_max, dest_count):
    most = (tile_max + dest_count // 2) // 2
    return -(-most // UNROLL) * UNROLL


def prepare_kernel(
    tiles_per_owner,
    place_ref,
    src_ref,
    count_ref,
    tile_ref,
    turned_ref,
    weight_ref,
    slot_ref,
    first_ref,
    second_ref,
    row_ref,
    go_on_ref,
    turns_ref,
):
    tile_max, tile_size, _ = tile_ref.shape
    dest_count = count_ref.shape[1]
    capacity = slot_ref.shape[1]
    zero_tile = place_ref[2]
    my_row = place_ref[0]

    for half in range(2):

        def one_dest(dest, carry, half=half):
            start, used = carry
            owner = dest // tiles_per_owner
            relative = lax.bitwise_xor(owner, my_row)
            count = count_ref[0, dest]
            mine = lax.bitwise_and(relative, 1) == half
            pairs = jnp.where(mine, (count + 1) // 2, 0)
            out_row = (
                (relative // 2) * tiles_per_owner + dest - owner * tiles_per_owner
            ) * tile_size

            def one_pair(pair, carry):
                at = used + pair
                slot = start + 2 * pair
                next_slot = jnp.minimum(slot + 1, tile_max - 1)
                slot_ref[half, at] = slot
                first_ref[half, at] = src_ref[0, slot] * tile_size
                second_ref[half, at] = (
                    jnp.where(2 * pair + 1 < count, src_ref[0, next_slot], zero_tile) * tile_size
                )
                row_ref[half, at] = out_row
                go_on_ref[half, at] = jnp.where(pair > 0, 1, 0)
                return carry

            lax.fori_loop(0, pairs, one_pair, 0)
            return start + count, used + pairs

        _, used = lax.fori_loop(0, dest_count, one_dest, (jnp.int32(0), jnp.int32(0)))
        turns = (used + UNROLL - 1) // UNROLL
        last_row = row_ref[half, used - 1]

        def one_pad(at, carry, half=half, last_row=last_row):
            slot_ref[half, at] = 0
            first_ref[half, at] = zero_tile * tile_size
            second_ref[half, at] = zero_tile * tile_size
            row_ref[half, at] = last_row
            go_on_ref[half, at] = 1
            return carry

        lax.fori_loop(used, turns * UNROLL, one_pad, 0)
        turns_ref[half] = turns

    def one_turn(dest, start):
        count = count_ref[0, dest]
        owner = dest // tiles_per_owner
        relative = lax.bitwise_xor(owner, my_row)

        def one_slot(slot, running):
            tile = tile_ref[slot]
            turned_ref[slot] = tile.T
            return running + jnp.sum(tile.astype(jnp.float32), axis=0, keepdims=True)

        total = lax.fori_loop(
            start, start + count, one_slot, jnp.zeros((1, tile_size), jnp.float32)
        )
        weight_ref[relative, pl.ds(dest - owner * tiles_per_owner, 1), :] = total
        return start + count

    live = lax.fori_loop(0, dest_count, one_turn, jnp.int32(0))

    def one_dead(slot, carry):
        turned_ref[slot] = jnp.zeros((tile_size, tile_size), turned_ref.dtype)
        return carry

    lax.fori_loop(live, tile_max, one_dead, 0)


def prepare(place, tile_src, row_counts, tile_vals, row_size, tiles_per_owner):
    tile_max, tile_size, _ = tile_vals.shape
    capacity = pair_capacity(tile_max, row_counts.shape[1])
    listing = jax.ShapeDtypeStruct((2, capacity), jnp.int32)
    return pl.pallas_call(
        functools.partial(prepare_kernel, tiles_per_owner),
        out_shape=[
            jax.ShapeDtypeStruct(tile_vals.shape, tile_vals.dtype),
            jax.ShapeDtypeStruct((row_size, tiles_per_owner, tile_size), jnp.float32),
            listing,
            listing,
            listing,
            listing,
            listing,
            jax.ShapeDtypeStruct((2,), jnp.int32),
        ],
        in_specs=smem(3) + vmem(1),
        out_specs=vmem(2) + smem(6),
        compiler_params=pltpu.CompilerParams(vmem_limit_bytes=24 * 2**20),
        name="prepare",
    )(place, tile_src, row_counts, tile_vals)


def product_kernel(
    half,
    packed,
    blocks,
    place_ref,
    slot_ref,
    first_ref,
    second_ref,
    row_ref,
    go_on_ref,
    turns_ref,
    turned_ref,
    *refs,
):
    block_refs = refs[:blocks]
    out_ref = refs[blocks]
    own_ref = refs[blocks + 1] if packed else None
    held_ref = refs[-2 if packed else -1]
    staged_ref = refs[-1] if packed else held_ref
    col = place_ref[1]
    rows, width = block_refs[0].shape
    tile_size = turned_ref.shape[1]

    def put(block, ref):
        staged_ref[pl.ds(pl.multiple_of(block * rows, rows), rows), :] = ref[...]

    for mask in range(blocks):
        put(lax.bitwise_xor(col, mask), block_refs[mask])
    if packed:
        piece = width // blocks
        for group in range(blocks):
            lanes = slice(group * piece, (group + 1) * piece)
            held_ref[group * rows : (group + 1) * rows, :] = jnp.concatenate(
                [staged_ref[b * rows : (b + 1) * rows, lanes] for b in range(blocks)], axis=1
            )
        own_ref[...] = held_ref[pl.ds(pl.multiple_of(col * rows, rows), rows), :]
    held_ref[blocks * rows :, :] = jnp.zeros((tile_size, width), held_ref.dtype)

    tile_max = turned_ref.shape[0]

    def one_turn(turn, running):
        for step in range(UNROLL):
            at = turn * UNROLL + step
            slot = slot_ref[half, at]
            left = jnp.concatenate(
                [turned_ref[slot], turned_ref[jnp.minimum(slot + 1, tile_max - 1)]], axis=1
            )
            first = pl.multiple_of(first_ref[half, at], tile_size)
            second = pl.multiple_of(second_ref[half, at], tile_size)
            right = jnp.concatenate(
                [held_ref[pl.ds(first, tile_size), :], held_ref[pl.ds(second, tile_size), :]],
                axis=0,
            )
            term = jnp.dot(left, right, preferred_element_type=jnp.float32)
            running = running * go_on_ref[half, at].astype(jnp.float32) + term
            out_row = pl.multiple_of(row_ref[half, at], tile_size)
            out_ref[pl.ds(out_row, tile_size), :] = running.astype(out_ref.dtype)
        return running

    lax.fori_loop(0, turns_ref[half], one_turn, jnp.zeros((tile_size, width), jnp.float32))


def product(half, place, lists, turned, gathered, blocks, row_size, packed):
    rows, width = gathered[0].shape
    tile_size = turned.shape[1]
    out_shape = [jax.ShapeDtypeStruct((row_size // 2 * rows, width), jnp.bfloat16)]
    scratch = [pltpu.VMEM((blocks * rows + tile_size, width), jnp.bfloat16)]
    if packed:
        out_shape.append(jax.ShapeDtypeStruct((rows, width), jnp.bfloat16))
        scratch.append(pltpu.VMEM((blocks * rows, width), jnp.bfloat16))
    return pl.pallas_call(
        functools.partial(product_kernel, half, packed, blocks),
        out_shape=out_shape,
        in_specs=smem(1 + len(lists)) + vmem(1 + len(gathered)),
        out_specs=vmem(len(out_shape)),
        scratch_shapes=scratch,
        compiler_params=pltpu.CompilerParams(vmem_limit_bytes=4 * 2**20),
        name="product",
    )(place, *lists, turned, *gathered)


def exchange(block, axis, mask, size):
    return lax.ppermute(block, axis, [(i, i ^ mask) for i in range(size)])


def gather_line(block, size):
    return [block] + [exchange(block, "col", mask, size) for mask in range(size - 1, 0, -1)][::-1]


def on_device(features, tile_vals, tile_src, row_counts):
    row_size = lax.axis_size("row")
    blocks = lax.axis_size("col")
    my_row = lax.axis_index("row").astype(jnp.int32)
    my_col = lax.axis_index("col").astype(jnp.int32)
    tile_size = tile_vals.shape[1]
    dest_count = row_counts.shape[1]
    rows = features.shape[0] // blocks
    source_tiles = features.shape[0] // tile_size
    width = features.shape[1] * blocks // CHUNKS
    piece = features.shape[1] // CHUNKS
    tiles_per_owner = dest_count // row_size
    chips = row_size // 2
    place = jnp.stack([my_row, my_col, jnp.int32(source_tiles)])

    parts = features.reshape(blocks, rows, CHUNKS, piece).transpose(2, 1, 0, 3)
    parts = parts.reshape(CHUNKS, rows, blocks * piece)

    turned, weight_sums, *lists = prepare(
        place, tile_src, row_counts, tile_vals, row_size, tiles_per_owner
    )
    other = exchange(weight_sums.reshape(row_size // 2, 2, tiles_per_owner, tile_size)[:, 1], "row", 1, row_size)
    weights = weight_sums.reshape(row_size // 2, 2, tiles_per_owner, tile_size)[:, 0] + other
    weight_total = 1.0 + weights[0]
    for mask in range(1, chips):
        weight_total = weight_total + exchange(weights[mask], "row", 2 * mask, row_size)
    scale = ((1.0 - TELEPORT) / weight_total).reshape(rows, 1)
    scale = jnp.broadcast_to(scale, (rows, width))

    gathered = [None] * CHUNKS
    iterates = [None] * CHUNKS
    restarts = [None] * CHUNKS
    gathered[0] = gather_line(parts[0], blocks)
    for iteration in range(ITERS):
        for chunk in range(CHUNKS):
            packed = iteration == 0
            after = (chunk + 1) % CHUNKS
            source = parts[1] if packed and chunk == 0 else iterates[after]
            if iteration + 1 < ITERS or chunk == 0:
                held, source = lax.optimization_barrier((gathered[chunk], source))
                gathered[chunk] = held
                gathered[after] = gather_line(source, blocks)
            sent, *rest = product(
                1, place, lists, turned, gathered[chunk], blocks, row_size, packed
            )
            if packed:
                iterates[chunk] = rest[0]
                restarts[chunk] = TELEPORT * rest[0].astype(jnp.float32)
            other = exchange(sent, "row", 1, row_size)
            kept = product(0, place, lists, turned, gathered[chunk], blocks, row_size, packed)[0]
            both = (kept.astype(jnp.float32) + other.astype(jnp.float32)).reshape(
                chips, rows, width
            )
            summed = both[0]
            for mask in range(1, chips):
                summed = summed + exchange(
                    both[mask].astype(jnp.bfloat16), "row", 2 * mask, row_size
                ).astype(jnp.float32)
            iterates[chunk] = (
                scale * (summed + iterates[chunk].astype(jnp.float32)) + restarts[chunk]
            ).astype(jnp.bfloat16)
    out = jnp.stack(iterates).reshape(CHUNKS, rows, blocks, piece).transpose(1, 2, 0, 3)
    return out.reshape(rows, CHUNKS * width)


def solution(mesh):
    placed = (P("row", "col"), P("row", "col", None), P("row", "col"), P("row", "col"))
    return jax.shard_map(
        on_device, mesh=mesh, in_specs=placed, out_specs=P(("row", "col"), None), check_vma=False
    )
```

```python
import functools

import jax
import jax.numpy as jnp
from jax import lax
from jax.experimental import pallas as pl
from jax.experimental.pallas import tpu as pltpu
from jax.sharding import PartitionSpec as P

ITERS = 3


TELEPORT = 0.1


CHUNKS = 2


UNROLL = 8


def vmem(count):
    return [pl.BlockSpec(memory_space=pltpu.VMEM)] * count


def smem(count):
    return [pl.BlockSpec(memory_space=pltpu.SMEM)] * count


def pair_capacity(tile_max, dest_count):
    most = (tile_max + dest_count // 2) // 2
    return -(-most // UNROLL) * UNROLL


def prepare_kernel(
    tiles_per_owner,
    place_ref,
    src_ref,
    count_ref,
    tile_ref,
    turned_ref,
    weight_ref,
    slot_ref,
    first_ref,
    second_ref,
    row_ref,
    go_on_ref,
    turns_ref,
):
    tile_max, tile_size, _ = tile_ref.shape
    dest_count = count_ref.shape[1]
    capacity = slot_ref.shape[1]
    zero_tile = place_ref[2]
    my_row = place_ref[0]

    for half in range(2):

        def one_dest(dest, carry, half=half):
            start, used = carry
            owner = dest // tiles_per_owner
            relative = lax.bitwise_xor(owner, my_row)
            count = count_ref[0, dest]
            mine = lax.bitwise_and(relative, 1) == half
            pairs = jnp.where(mine, (count + 1) // 2, 0)
            out_row = (
                (relative // 2) * tiles_per_owner + dest - owner * tiles_per_owner
            ) * tile_size

            def one_pair(pair, carry):
                at = used + pair
                slot = start + 2 * pair
                next_slot = jnp.minimum(slot + 1, tile_max - 1)
                slot_ref[half, at] = slot
                first_ref[half, at] = src_ref[0, slot] * tile_size
                second_ref[half, at] = (
                    jnp.where(2 * pair + 1 < count, src_ref[0, next_slot], zero_tile) * tile_size
                )
                row_ref[half, at] = out_row
                go_on_ref[half, at] = jnp.where(pair > 0, 1, 0)
                return carry

            lax.fori_loop(0, pairs, one_pair, 0)
            return start + count, used + pairs

        _, used = lax.fori_loop(0, dest_count, one_dest, (jnp.int32(0), jnp.int32(0)))
        turns = (used + UNROLL - 1) // UNROLL
        last_row = row_ref[half, used - 1]

        def one_pad(at, carry, half=half, last_row=last_row):
            slot_ref[half, at] = 0
            first_ref[half, at] = zero_tile * tile_size
            second_ref[half, at] = zero_tile * tile_size
            row_ref[half, at] = last_row
            go_on_ref[half, at] = 1
            return carry

        lax.fori_loop(used, turns * UNROLL, one_pad, 0)
        turns_ref[half] = turns

    def one_turn(dest, start):
        count = count_ref[0, dest]
        owner = dest // tiles_per_owner
        relative = lax.bitwise_xor(owner, my_row)

        def one_slot(slot, running):
            tile = tile_ref[slot]
            turned_ref[slot] = tile.T
            return running + jnp.sum(tile.astype(jnp.float32), axis=0, keepdims=True)

        total = lax.fori_loop(
            start, start + count, one_slot, jnp.zeros((1, tile_size), jnp.float32)
        )
        weight_ref[relative, pl.ds(dest - owner * tiles_per_owner, 1), :] = total
        return start + count

    live = lax.fori_loop(0, dest_count, one_turn, jnp.int32(0))

    def one_dead(slot, carry):
        turned_ref[slot] = jnp.zeros((tile_size, tile_size), turned_ref.dtype)
        return carry

    lax.fori_loop(live, tile_max, one_dead, 0)


def prepare(place, tile_src, row_counts, tile_vals, row_size, tiles_per_owner):
    tile_max, tile_size, _ = tile_vals.shape
    capacity = pair_capacity(tile_max, row_counts.shape[1])
    listing = jax.ShapeDtypeStruct((2, capacity), jnp.int32)
    return pl.pallas_call(
        functools.partial(prepare_kernel, tiles_per_owner),
        out_shape=[
            jax.ShapeDtypeStruct(tile_vals.shape, tile_vals.dtype),
            jax.ShapeDtypeStruct((row_size, tiles_per_owner, tile_size), jnp.float32),
            listing,
            listing,
            listing,
            listing,
            listing,
            jax.ShapeDtypeStruct((2,), jnp.int32),
        ],
        in_specs=smem(3) + vmem(1),
        out_specs=vmem(2) + smem(6),
        compiler_params=pltpu.CompilerParams(vmem_limit_bytes=4 * 2**20),
        name="prepare",
    )(place, tile_src, row_counts, tile_vals)


def product_kernel(
    half,
    packed,
    blocks,
    arrays,
    place_ref,
    slot_ref,
    first_ref,
    second_ref,
    row_ref,
    go_on_ref,
    turns_ref,
    turned_ref,
    *refs,
):
    block_refs = refs[:arrays]
    out_ref = refs[arrays]
    own_ref = refs[arrays + 1] if packed else None
    held_ref = refs[-2 if packed else -1]
    staged_ref = refs[-1] if packed else held_ref
    col = place_ref[1]
    rows, width = block_refs[0].shape
    tile_size = turned_ref.shape[1]

    def put(block, ref):
        staged_ref[pl.ds(pl.multiple_of(block * rows, rows), rows), :] = ref[...]

    for mask in range(blocks - 1):
        put(lax.bitwise_xor(col, mask), block_refs[mask])
    last = lax.bitwise_xor(col, blocks - 1)
    if len(block_refs) == blocks:
        put(last, block_refs[-1])
    else:
        inside = jnp.logical_and(col > 0, col < blocks - 1)
        pl.when(inside)(functools.partial(put, last, block_refs[-2]))
        pl.when(jnp.logical_not(inside))(functools.partial(put, last, block_refs[-1]))
    if packed:
        piece = width // blocks
        for group in range(blocks):
            lanes = slice(group * piece, (group + 1) * piece)
            held_ref[group * rows : (group + 1) * rows, :] = jnp.concatenate(
                [staged_ref[b * rows : (b + 1) * rows, lanes] for b in range(blocks)], axis=1
            )
        own_ref[...] = held_ref[pl.ds(pl.multiple_of(col * rows, rows), rows), :]
    held_ref[blocks * rows :, :] = jnp.zeros((tile_size, width), held_ref.dtype)

    tile_max = turned_ref.shape[0]

    def one_turn(turn, running):
        for step in range(UNROLL):
            at = turn * UNROLL + step
            slot = slot_ref[half, at]
            left = jnp.concatenate(
                [turned_ref[slot], turned_ref[jnp.minimum(slot + 1, tile_max - 1)]], axis=1
            )
            first = pl.multiple_of(first_ref[half, at], tile_size)
            second = pl.multiple_of(second_ref[half, at], tile_size)
            right = jnp.concatenate(
                [held_ref[pl.ds(first, tile_size), :], held_ref[pl.ds(second, tile_size), :]],
                axis=0,
            )
            term = jnp.dot(left, right, preferred_element_type=jnp.float32)
            running = running * go_on_ref[half, at].astype(jnp.float32) + term
            out_row = pl.multiple_of(row_ref[half, at], tile_size)
            out_ref[pl.ds(out_row, tile_size), :] = running.astype(out_ref.dtype)
        return running

    lax.fori_loop(0, turns_ref[half], one_turn, jnp.zeros((tile_size, width), jnp.float32))


def product(half, place, lists, turned, gathered, blocks, row_size, packed):
    rows, width = gathered[0].shape
    tile_size = turned.shape[1]
    out_shape = [jax.ShapeDtypeStruct((row_size // 2 * rows, width), jnp.bfloat16)]
    scratch = [pltpu.VMEM((blocks * rows + tile_size, width), jnp.bfloat16)]
    if packed:
        out_shape.append(jax.ShapeDtypeStruct((rows, width), jnp.bfloat16))
        scratch.append(pltpu.VMEM((blocks * rows, width), jnp.bfloat16))
    return pl.pallas_call(
        functools.partial(product_kernel, half, packed, blocks, len(gathered)),
        out_shape=out_shape,
        in_specs=smem(1 + len(lists)) + vmem(1 + len(gathered)),
        out_specs=vmem(len(out_shape)),
        scratch_shapes=scratch,
        compiler_params=pltpu.CompilerParams(vmem_limit_bytes=4 * 2**20),
        name="product",
    )(place, *lists, turned, *gathered)


def exchange(block, axis, mask, size):
    return lax.ppermute(block, axis, [(i, i ^ mask) for i in range(size)])


def gather_line(block, size):
    if size != 4:
        return [block] + [exchange(block, "col", mask, size) for mask in range(1, size)]
    across = exchange(block, "col", 2, size)
    beside = exchange(block, "col", 1, size)
    inner = lax.ppermute(block, "col", [(0, 0), (1, 2), (2, 1), (3, 3)])
    outer = exchange(across, "col", 1, size)
    return [block, beside, across, inner, outer]


def on_device(features, tile_vals, tile_src, row_counts):
    row_size = lax.axis_size("row")
    blocks = lax.axis_size("col")
    my_row = lax.axis_index("row").astype(jnp.int32)
    my_col = lax.axis_index("col").astype(jnp.int32)
    tile_size = tile_vals.shape[1]
    dest_count = row_counts.shape[1]
    rows = features.shape[0] // blocks
    source_tiles = features.shape[0] // tile_size
    width = features.shape[1] * blocks // CHUNKS
    piece = features.shape[1] // CHUNKS
    tiles_per_owner = dest_count // row_size
    chips = row_size // 2
    place = jnp.stack([my_row, my_col, jnp.int32(source_tiles)])

    parts = features.reshape(blocks, rows, CHUNKS, piece).transpose(2, 1, 0, 3)
    parts = parts.reshape(CHUNKS, rows, blocks * piece)

    turned, weight_sums, *lists = prepare(
        place, tile_src, row_counts, tile_vals, row_size, tiles_per_owner
    )
    other = exchange(weight_sums.reshape(row_size // 2, 2, tiles_per_owner, tile_size)[:, 1], "row", 1, row_size)
    weights = weight_sums.reshape(row_size // 2, 2, tiles_per_owner, tile_size)[:, 0] + other
    weight_total = 1.0 + weights[0]
    for mask in range(1, chips):
        weight_total = weight_total + exchange(weights[mask], "row", 2 * mask, row_size)
    scale = ((1.0 - TELEPORT) / weight_total).reshape(rows, 1)
    scale = jnp.broadcast_to(scale, (rows, width))

    gathered = [None] * CHUNKS
    iterates = [None] * CHUNKS
    restarts = [None] * CHUNKS
    gathered[0] = gather_line(parts[0], blocks)
    for iteration in range(ITERS):
        for chunk in range(CHUNKS):
            packed = iteration == 0
            after = (chunk + 1) % CHUNKS
            source = parts[1] if packed and chunk == 0 else iterates[after]
            if iteration + 1 < ITERS or chunk == 0:
                held, source = lax.optimization_barrier((gathered[chunk], source))
                gathered[chunk] = held
                gathered[after] = gather_line(source, blocks)
            sent, *rest = product(
                1, place, lists, turned, gathered[chunk], blocks, row_size, packed
            )
            if packed:
                iterates[chunk] = rest[0]
                restarts[chunk] = TELEPORT * rest[0].astype(jnp.float32)
            other = exchange(sent, "row", 1, row_size)
            kept = product(0, place, lists, turned, gathered[chunk], blocks, row_size, packed)[0]
            both = (kept.astype(jnp.float32) + other.astype(jnp.float32)).reshape(
                chips, rows, width
            )
            summed = both[0]
            for mask in range(1, chips):
                summed = summed + exchange(
                    both[mask].astype(jnp.bfloat16), "row", 2 * mask, row_size
                ).astype(jnp.float32)
            iterates[chunk] = (
                scale * (summed + iterates[chunk].astype(jnp.float32)) + restarts[chunk]
            ).astype(jnp.bfloat16)
    out = jnp.stack(iterates).reshape(CHUNKS, rows, blocks, piece).transpose(1, 2, 0, 3)
    return out.reshape(rows, CHUNKS * width)


def solution(mesh):
    placed = (P("row", "col"), P("row", "col", None), P("row", "col"), P("row", "col"))
    return jax.shard_map(
        on_device, mesh=mesh, in_specs=placed, out_specs=P(("row", "col"), None), check_vma=False
    )
```

```python
import functools

import jax
import jax.numpy as jnp
from jax import lax
from jax.experimental import pallas as pl
from jax.experimental.pallas import tpu as pltpu
from jax.sharding import PartitionSpec as P

ITERS = 3


TELEPORT = 0.1


CHUNKS = 2


UNROLL = 8


def vmem(count):
    return [pl.BlockSpec(memory_space=pltpu.VMEM)] * count


def smem(count):
    return [pl.BlockSpec(memory_space=pltpu.SMEM)] * count


def pair_capacity(tile_max, dest_count):
    most = (tile_max + dest_count // 2) // 2
    return -(-most // UNROLL) * UNROLL


def prepare_kernel(
    tiles_per_owner,
    place_ref,
    src_ref,
    count_ref,
    tile_ref,
    turned_ref,
    weight_ref,
    slot_ref,
    first_ref,
    second_ref,
    row_ref,
    go_on_ref,
    turns_ref,
):
    tile_max, tile_size, _ = tile_ref.shape
    dest_count = count_ref.shape[1]
    capacity = slot_ref.shape[1]
    zero_tile = place_ref[2]
    my_row = place_ref[0]

    for half in range(2):

        def one_dest(dest, carry, half=half):
            start, used = carry
            owner = dest // tiles_per_owner
            relative = lax.bitwise_xor(owner, my_row)
            count = count_ref[0, dest]
            mine = lax.bitwise_and(relative, 1) == half
            pairs = jnp.where(mine, (count + 1) // 2, 0)
            out_row = (
                (relative // 2) * tiles_per_owner + dest - owner * tiles_per_owner
            ) * tile_size

            def one_pair(pair, carry):
                at = used + pair
                slot = start + 2 * pair
                next_slot = jnp.minimum(slot + 1, tile_max - 1)
                slot_ref[half, at] = slot
                first_ref[half, at] = src_ref[0, slot] * tile_size
                second_ref[half, at] = (
                    jnp.where(2 * pair + 1 < count, src_ref[0, next_slot], zero_tile) * tile_size
                )
                row_ref[half, at] = out_row
                go_on_ref[half, at] = jnp.where(pair > 0, 1, 0)
                return carry

            lax.fori_loop(0, pairs, one_pair, 0)
            return start + count, used + pairs

        _, used = lax.fori_loop(0, dest_count, one_dest, (jnp.int32(0), jnp.int32(0)))
        turns = (used + UNROLL - 1) // UNROLL
        last_row = row_ref[half, used - 1]

        def one_pad(at, carry, half=half, last_row=last_row):
            slot_ref[half, at] = 0
            first_ref[half, at] = zero_tile * tile_size
            second_ref[half, at] = zero_tile * tile_size
            row_ref[half, at] = last_row
            go_on_ref[half, at] = 1
            return carry

        lax.fori_loop(used, turns * UNROLL, one_pad, 0)
        turns_ref[half] = turns

    def one_turn(dest, start):
        count = count_ref[0, dest]
        owner = dest // tiles_per_owner
        relative = lax.bitwise_xor(owner, my_row)

        def one_slot(slot, running):
            tile = tile_ref[slot]
            turned_ref[slot] = tile.T
            return running + jnp.sum(tile.astype(jnp.float32), axis=0, keepdims=True)

        total = lax.fori_loop(
            start, start + count, one_slot, jnp.zeros((1, tile_size), jnp.float32)
        )
        weight_ref[relative, pl.ds(dest - owner * tiles_per_owner, 1), :] = total
        return start + count

    live = lax.fori_loop(0, dest_count, one_turn, jnp.int32(0))

    def one_dead(slot, carry):
        turned_ref[slot] = jnp.zeros((tile_size, tile_size), turned_ref.dtype)
        return carry

    lax.fori_loop(live, tile_max, one_dead, 0)


def prepare(place, tile_src, row_counts, tile_vals, row_size, tiles_per_owner):
    tile_max, tile_size, _ = tile_vals.shape
    capacity = pair_capacity(tile_max, row_counts.shape[1])
    listing = jax.ShapeDtypeStruct((2, capacity), jnp.int32)
    return pl.pallas_call(
        functools.partial(prepare_kernel, tiles_per_owner),
        out_shape=[
            jax.ShapeDtypeStruct(tile_vals.shape, tile_vals.dtype),
            jax.ShapeDtypeStruct((row_size, tiles_per_owner, tile_size), jnp.float32),
            listing,
            listing,
            listing,
            listing,
            listing,
            jax.ShapeDtypeStruct((2,), jnp.int32),
        ],
        in_specs=smem(3) + vmem(1),
        out_specs=vmem(2) + smem(6),
        compiler_params=pltpu.CompilerParams(vmem_limit_bytes=4 * 2**20),
        name="prepare",
    )(place, tile_src, row_counts, tile_vals)


def product_kernel(
    half,
    packed,
    blocks,
    arrays,
    place_ref,
    slot_ref,
    first_ref,
    second_ref,
    row_ref,
    go_on_ref,
    turns_ref,
    turned_ref,
    *refs,
):
    block_refs = refs[:arrays]
    out_ref = refs[arrays]
    own_ref = refs[arrays + 1] if packed else None
    held_ref = refs[-2 if packed else -1]
    staged_ref = refs[-1] if packed else held_ref
    col = place_ref[1]
    rows, width = block_refs[0].shape
    rows = rows // blocks
    tile_size = turned_ref.shape[1]

    def put(block, ref):
        staged_ref[pl.ds(pl.multiple_of(block * rows, rows), rows), :] = ref[...]

    staged_ref[: blocks * rows, :] = block_refs[0][...]
    if packed:
        piece = width // blocks
        for group in range(blocks):
            lanes = slice(group * piece, (group + 1) * piece)
            held_ref[group * rows : (group + 1) * rows, :] = jnp.concatenate(
                [staged_ref[b * rows : (b + 1) * rows, lanes] for b in range(blocks)], axis=1
            )
        own_ref[...] = held_ref[pl.ds(pl.multiple_of(col * rows, rows), rows), :]
    held_ref[blocks * rows :, :] = jnp.zeros((tile_size, width), held_ref.dtype)

    tile_max = turned_ref.shape[0]

    def one_turn(turn, running):
        for step in range(UNROLL):
            at = turn * UNROLL + step
            slot = slot_ref[half, at]
            left = jnp.concatenate(
                [turned_ref[slot], turned_ref[jnp.minimum(slot + 1, tile_max - 1)]], axis=1
            )
            first = pl.multiple_of(first_ref[half, at], tile_size)
            second = pl.multiple_of(second_ref[half, at], tile_size)
            right = jnp.concatenate(
                [held_ref[pl.ds(first, tile_size), :], held_ref[pl.ds(second, tile_size), :]],
                axis=0,
            )
            term = jnp.dot(left, right, preferred_element_type=jnp.float32)
            running = running * go_on_ref[half, at].astype(jnp.float32) + term
            out_row = pl.multiple_of(row_ref[half, at], tile_size)
            out_ref[pl.ds(out_row, tile_size), :] = running.astype(out_ref.dtype)
        return running

    lax.fori_loop(0, turns_ref[half], one_turn, jnp.zeros((tile_size, width), jnp.float32))


def product(half, place, lists, turned, gathered, blocks, row_size, packed):
    rows, width = gathered[0].shape
    rows = rows // blocks
    tile_size = turned.shape[1]
    out_shape = [jax.ShapeDtypeStruct((row_size // 2 * rows, width), jnp.bfloat16)]
    scratch = [pltpu.VMEM((blocks * rows + tile_size, width), jnp.bfloat16)]
    if packed:
        out_shape.append(jax.ShapeDtypeStruct((rows, width), jnp.bfloat16))
        scratch.append(pltpu.VMEM((blocks * rows, width), jnp.bfloat16))
    return pl.pallas_call(
        functools.partial(product_kernel, half, packed, blocks, len(gathered)),
        out_shape=out_shape,
        in_specs=smem(1 + len(lists)) + vmem(1 + len(gathered)),
        out_specs=vmem(len(out_shape)),
        scratch_shapes=scratch,
        compiler_params=pltpu.CompilerParams(vmem_limit_bytes=4 * 2**20),
        name="product",
        cost_estimate=pl.CostEstimate(
            flops=600000000, bytes_accessed=6000000, transcendentals=0
        ),
    )(place, *lists, turned, *gathered)


def exchange(block, axis, mask, size):
    return lax.ppermute(block, axis, [(i, i ^ mask) for i in range(size)])


def gather_line(block, size):
    return [lax.all_gather(block, "col", axis=0, tiled=True)]
    if size != 4:
        return [block] + [exchange(block, "col", mask, size) for mask in range(1, size)]
    across = exchange(block, "col", 2, size)
    beside = exchange(block, "col", 1, size)
    inner = lax.ppermute(block, "col", [(0, 0), (1, 2), (2, 1), (3, 3)])
    outer = exchange(across, "col", 1, size)
    return [block, beside, across, inner, outer]


def on_device(features, tile_vals, tile_src, row_counts):
    row_size = lax.axis_size("row")
    blocks = lax.axis_size("col")
    my_row = lax.axis_index("row").astype(jnp.int32)
    my_col = lax.axis_index("col").astype(jnp.int32)
    tile_size = tile_vals.shape[1]
    dest_count = row_counts.shape[1]
    rows = features.shape[0] // blocks
    source_tiles = features.shape[0] // tile_size
    width = features.shape[1] * blocks // CHUNKS
    piece = features.shape[1] // CHUNKS
    tiles_per_owner = dest_count // row_size
    chips = row_size // 2
    place = jnp.stack([my_row, my_col, jnp.int32(source_tiles)])

    parts = features.reshape(blocks, rows, CHUNKS, piece).transpose(2, 1, 0, 3)
    parts = parts.reshape(CHUNKS, rows, blocks * piece)

    turned, weight_sums, *lists = prepare(
        place, tile_src, row_counts, tile_vals, row_size, tiles_per_owner
    )
    other = exchange(weight_sums.reshape(row_size // 2, 2, tiles_per_owner, tile_size)[:, 1], "row", 1, row_size)
    weights = weight_sums.reshape(row_size // 2, 2, tiles_per_owner, tile_size)[:, 0] + other
    weight_total = 1.0 + weights[0]
    for mask in range(1, chips):
        weight_total = weight_total + exchange(weights[mask], "row", 2 * mask, row_size)
    scale = ((1.0 - TELEPORT) / weight_total).reshape(rows, 1)
    scale = jnp.broadcast_to(scale, (rows, width))

    gathered = [None] * CHUNKS
    iterates = [None] * CHUNKS
    restarts = [None] * CHUNKS
    gathered[0] = gather_line(parts[0], blocks)
    for iteration in range(ITERS):
        for chunk in range(CHUNKS):
            packed = iteration == 0
            after = (chunk + 1) % CHUNKS
            source = parts[1] if packed and chunk == 0 else iterates[after]
            if iteration + 1 < ITERS or chunk == 0:
                held, source = lax.optimization_barrier((gathered[chunk], source))
                gathered[chunk] = held
                gathered[after] = gather_line(source, blocks)
            sent, *rest = product(
                1, place, lists, turned, gathered[chunk], blocks, row_size, packed
            )
            if packed:
                iterates[chunk] = rest[0]
                restarts[chunk] = TELEPORT * rest[0].astype(jnp.float32)
            other = exchange(sent, "row", 1, row_size)
            kept = product(0, place, lists, turned, gathered[chunk], blocks, row_size, packed)[0]
            both = (kept.astype(jnp.float32) + other.astype(jnp.float32)).reshape(
                chips, rows, width
            )
            summed = both[0]
            for mask in range(1, chips):
                summed = summed + exchange(
                    both[mask].astype(jnp.bfloat16), "row", 2 * mask, row_size
                ).astype(jnp.float32)
            iterates[chunk] = (
                scale * (summed + iterates[chunk].astype(jnp.float32)) + restarts[chunk]
            ).astype(jnp.bfloat16)
    out = jnp.stack(iterates).reshape(CHUNKS, rows, blocks, piece).transpose(1, 2, 0, 3)
    return out.reshape(rows, CHUNKS * width)


def solution(mesh):
    placed = (P("row", "col"), P("row", "col", None), P("row", "col"), P("row", "col"))
    return jax.shard_map(
        on_device, mesh=mesh, in_specs=placed, out_specs=P(("row", "col"), None), check_vma=False
    )
```

```python
import functools

import jax
import jax.numpy as jnp
from jax import lax
from jax.experimental import pallas as pl
from jax.experimental.pallas import tpu as pltpu
from jax.sharding import PartitionSpec as P

ITERS = 3


TELEPORT = 0.1


CHUNKS = 2


UNROLL = 8


EXTRA = 16


MOST = 8


def vmem(count):
    return [pl.BlockSpec(memory_space=pltpu.VMEM)] * count


def smem(count):
    return [pl.BlockSpec(memory_space=pltpu.SMEM)] * count


def anywhere(count):
    return [pl.BlockSpec(memory_space=pl.ANY)] * count


def pair_capacity(tile_max, dest_count):
    most = (tile_max + dest_count // 2) // 2
    return -(-most // UNROLL) * UNROLL


def prepare_kernel(
    tiles_per_owner,
    place_ref,
    src_ref,
    count_ref,
    tile_ref,
    turned_ref,
    weight_ref,
    slot_ref,
    first_ref,
    second_ref,
    row_ref,
    go_on_ref,
    turns_ref,
    held_ref,
    sum_ref,
    sems,
):
    tile_max, tile_size, _ = tile_ref.shape
    dest_count = count_ref.shape[1]
    zero_tile = place_ref[2]
    my_row = place_ref[0]
    pieces = sems.shape[0]
    piece = tile_max // pieces
    copies = []
    for index in range(pieces):
        span = pl.ds(index * piece, piece)
        copies.append(
            pltpu.make_async_copy(tile_ref.at[span], held_ref.at[span], sems.at[index])
        )
        copies[-1].start()

    for half in range(2):

        def one_dest(dest, carry, half=half):
            start, used = carry
            owner = lax.div(dest, tiles_per_owner)
            relative = lax.bitwise_xor(owner, my_row)
            count = count_ref[0, dest]
            mine = lax.bitwise_and(relative, 1) == half
            pairs = jnp.where(mine, lax.div(count + 1, 2), 0)
            out_row = (
                lax.div(relative, 2) * tiles_per_owner + dest - owner * tiles_per_owner
            ) * tile_size

            def one_pair(pair, carry):
                at = used + pair
                slot = start + 2 * pair
                next_slot = jnp.minimum(slot + 1, tile_max - 1)
                slot_ref[half, at] = slot
                first_ref[half, at] = src_ref[0, slot] * tile_size
                second_ref[half, at] = (
                    jnp.where(2 * pair + 1 < count, src_ref[0, next_slot], zero_tile) * tile_size
                )
                row_ref[half, at] = out_row
                go_on_ref[half, at] = jnp.where(pair > 0, 1, 0)
                return carry

            lax.fori_loop(0, pairs, one_pair, 0)
            return start + count, used + pairs

        _, used = lax.fori_loop(0, dest_count, one_dest, (jnp.int32(0), jnp.int32(0)))
        turns = lax.div(used + UNROLL - 1, UNROLL)
        last_row = row_ref[half, used - 1]

        def one_pad(at, carry, half=half, last_row=last_row):
            slot_ref[half, at] = 0
            first_ref[half, at] = zero_tile * tile_size
            second_ref[half, at] = zero_tile * tile_size
            row_ref[half, at] = last_row
            go_on_ref[half, at] = 1
            return carry

        lax.fori_loop(used, turns * UNROLL, one_pad, 0)
        turns_ref[half] = turns

    group = min(8, piece)
    for index in range(pieces):
        copies[index].wait()

        def one_group(at, carry, index=index):
            for step in range(group):
                slot = index * piece + at * group + step
                tile = held_ref[slot]
                turned_ref[slot] = tile.T
                sum_ref[pl.ds(slot, 1), :] = jnp.sum(
                    tile.astype(jnp.float32), axis=0, keepdims=True
                )
            return carry

        lax.fori_loop(0, piece // group, one_group, 0)

    sum_ref[tile_max:, :] = jnp.zeros((MOST, tile_size), jnp.float32)
    weight_ref[...] = jnp.zeros(weight_ref.shape, weight_ref.dtype)
    places = lax.broadcasted_iota(jnp.int32, (MOST, tile_size), 0)

    def weigh(at, start):
        for step in range(tiles_per_owner):
            count = count_ref[0, at * tiles_per_owner + step]
            sums = jnp.where(places < count, sum_ref[pl.ds(start, MOST), :], 0.0)
            weight_ref[lax.bitwise_xor(at, my_row), step : step + 1, :] = jnp.sum(
                sums, axis=0, keepdims=True
            )
            start = start + count
        return start

    lax.fori_loop(0, dest_count // tiles_per_owner, weigh, jnp.int32(0))


def prepare(place, tile_src, row_counts, tile_vals, row_size, tiles_per_owner):
    tile_max, tile_size, _ = tile_vals.shape
    capacity = pair_capacity(tile_max, row_counts.shape[1])
    listing = jax.ShapeDtypeStruct((2, capacity), jnp.int32)
    return pl.pallas_call(
        functools.partial(prepare_kernel, tiles_per_owner),
        out_shape=[
            jax.ShapeDtypeStruct(tile_vals.shape, tile_vals.dtype),
            jax.ShapeDtypeStruct((row_size, EXTRA, tile_size), jnp.float32),
            listing,
            listing,
            listing,
            listing,
            listing,
            jax.ShapeDtypeStruct((2,), jnp.int32),
        ],
        in_specs=smem(3) + anywhere(1),
        out_specs=vmem(2) + smem(6),
        scratch_shapes=[
            pltpu.VMEM(tile_vals.shape, tile_vals.dtype),
            pltpu.VMEM((tile_max + MOST, tile_size), jnp.float32),
            pltpu.SemaphoreType.DMA((8,)),
        ],
        compiler_params=pltpu.CompilerParams(vmem_limit_bytes=24 * 2**20),
        name="prepare",
    )(place, tile_src, row_counts, tile_vals)


def assemble_kernel(packed, blocks, arrays, place_ref, *refs):
    block_refs = refs[:arrays]
    held_ref = refs[arrays + 1]
    staged_ref = refs[-1] if packed else held_ref
    col = place_ref[1]
    rows, width = block_refs[0].shape

    def put(mask, ref):
        first = pl.multiple_of(lax.bitwise_xor(col, mask) * rows, rows)
        staged_ref[pl.ds(first, rows), :] = ref[...]

    for mask in range(blocks - 1):
        put(mask, block_refs[mask])
    if arrays == blocks:
        put(blocks - 1, block_refs[-1])
    else:
        inside = jnp.logical_and(col > 0, col < blocks - 1)
        pl.when(inside)(functools.partial(put, blocks - 1, block_refs[-2]))
        pl.when(jnp.logical_not(inside))(functools.partial(put, blocks - 1, block_refs[-1]))
    if packed:
        piece = width // blocks
        for group in range(blocks):
            lanes = slice(group * piece, (group + 1) * piece)
            held_ref[group * rows : (group + 1) * rows, :] = jnp.concatenate(
                [staged_ref[b * rows : (b + 1) * rows, lanes] for b in range(blocks)], axis=1
            )
        own_ref = refs[arrays + 2]
        own_ref[...] = held_ref[pl.ds(pl.multiple_of(col * rows, rows), rows), :]
    zeros = held_ref.shape[0] - blocks * rows
    held_ref[blocks * rows :, :] = jnp.zeros((zeros, width), held_ref.dtype)


def assemble(place, gathered, after, blocks, tile_size, packed):
    arrays = len(gathered)
    rows, width = gathered[0].shape
    out_shape = [jax.ShapeDtypeStruct((blocks * rows + tile_size, width), jnp.bfloat16)]
    scratch = []
    if packed:
        out_shape.append(jax.ShapeDtypeStruct((rows, width), jnp.bfloat16))
        scratch.append(pltpu.VMEM((blocks * rows, width), jnp.bfloat16))
    return pl.pallas_call(
        functools.partial(assemble_kernel, packed, blocks, arrays),
        out_shape=out_shape,
        in_specs=smem(1) + vmem(arrays) + anywhere(1),
        out_specs=vmem(len(out_shape)),
        scratch_shapes=scratch,
        compiler_params=pltpu.CompilerParams(vmem_limit_bytes=4 * 2**20),
        cost_estimate=pl.CostEstimate(flops=0, bytes_accessed=4 * 2**20, transcendentals=0),
        name="assemble",
    )(place, *gathered, after)


def product_kernel(
    half,
    rows,
    slot_ref,
    first_ref,
    second_ref,
    row_ref,
    go_on_ref,
    turns_ref,
    turned_ref,
    held_ref,
    weight_ref,
    out_ref,
):
    tile_max, tile_size, _ = turned_ref.shape
    chips, out_rows, width = out_ref.shape
    if out_rows > rows:
        for chip in range(chips):
            out_ref[chip, rows:, :] = weight_ref[2 * chip + half].astype(out_ref.dtype)

    def one_turn(turn, running):
        for step in range(UNROLL):
            at = turn * UNROLL + step
            slot = slot_ref[half, at]
            left = jnp.concatenate(
                [turned_ref[slot], turned_ref[jnp.minimum(slot + 1, tile_max - 1)]], axis=1
            )
            first = pl.multiple_of(first_ref[half, at], tile_size)
            second = pl.multiple_of(second_ref[half, at], tile_size)
            right = jnp.concatenate(
                [held_ref[pl.ds(first, tile_size), :], held_ref[pl.ds(second, tile_size), :]],
                axis=0,
            )
            term = jnp.dot(left, right, preferred_element_type=jnp.float32)
            running = running * go_on_ref[half, at].astype(jnp.float32) + term
            out_row = row_ref[half, at]
            chip = lax.div(out_row, rows)
            out_row = pl.multiple_of(out_row - chip * rows, tile_size)
            out_ref[chip, pl.ds(out_row, tile_size), :] = running.astype(out_ref.dtype)
        return running

    lax.fori_loop(0, turns_ref[half], one_turn, jnp.zeros((tile_size, width), jnp.float32))


def product(half, lists, turned, held, weights, rows, chips, extra):
    return pl.pallas_call(
        functools.partial(product_kernel, half, rows),
        out_shape=jax.ShapeDtypeStruct((chips, rows + extra, held.shape[1]), jnp.bfloat16),
        in_specs=smem(len(lists)) + vmem(3),
        out_specs=vmem(1)[0],
        compiler_params=pltpu.CompilerParams(vmem_limit_bytes=4 * 2**20),
        cost_estimate=pl.CostEstimate(
            flops=600000000, bytes_accessed=6000000, transcendentals=0
        ),
        name="product",
    )(*lists, turned, held, weights)


def update_kernel(parts, *refs):
    kept_refs = refs[:parts]
    arrived_refs = refs[parts : 2 * parts]
    iterate_ref, restart_ref, scale_ref, out_ref = refs[2 * parts :]
    rows = out_ref.shape[0] // parts
    for part in range(parts):
        span = slice(part * rows, (part + 1) * rows)
        summed = kept_refs[part][:rows, :] + arrived_refs[part][:rows, :].astype(jnp.float32)
        out_ref[span, :] = (
            scale_ref[span, :] * (summed + iterate_ref[span, :].astype(jnp.float32))
            + TELEPORT * restart_ref[span, :].astype(jnp.float32)
        ).astype(out_ref.dtype)


def update(kept, arrived, iterate, restart, scale):
    return pl.pallas_call(
        functools.partial(update_kernel, len(kept)),
        out_shape=jax.ShapeDtypeStruct(iterate.shape, iterate.dtype),
        in_specs=vmem(2 * len(kept) + 3),
        out_specs=vmem(1)[0],
        compiler_params=pltpu.CompilerParams(vmem_limit_bytes=4 * 2**20),
        cost_estimate=pl.CostEstimate(flops=0, bytes_accessed=1, transcendentals=0),
        name="update",
    )(*kept, *arrived, iterate, restart, scale)


def exchange(block, axis, mask, size):
    return lax.ppermute(block, axis, [(i, i ^ mask) for i in range(size)])


def gather_first(block, size):
    masks = (1, 2) if size == 4 else range(1, size)
    return [block] + [exchange(block, "col", mask, size) for mask in masks]


def gather_second(found, size):
    if size != 4:
        return found
    inner = lax.ppermute(found[0], "col", [(0, 0), (1, 2), (2, 1), (3, 3)])
    return found + [inner, exchange(found[2], "col", 1, size)]


def halve(state, bits, bit, row_size):
    axis = bits.index(bit)
    send = lax.index_in_dim(state, 1, axis, keepdims=False).astype(jnp.bfloat16)
    keep = lax.index_in_dim(state, 0, axis, keepdims=False)
    return keep, exchange(send, "row", 1 << bit, row_size)


def on_device(features, tile_vals, tile_src, row_counts):
    row_size = lax.axis_size("row")
    blocks = lax.axis_size("col")
    my_row = lax.axis_index("row").astype(jnp.int32)
    my_col = lax.axis_index("col").astype(jnp.int32)
    tile_size = tile_vals.shape[1]
    dest_count = row_counts.shape[1]
    rows = features.shape[0] // blocks
    source_tiles = features.shape[0] // tile_size
    width = features.shape[1] * blocks // CHUNKS
    piece = features.shape[1] // CHUNKS
    tiles_per_owner = dest_count // row_size
    chips = row_size // 2
    chip_bits = list(range(row_size.bit_length() - 2, 0, -1))
    place = jnp.stack([my_row, my_col, jnp.int32(source_tiles)])

    parts = features.reshape(blocks, rows, CHUNKS, piece).transpose(2, 1, 0, 3)
    parts = parts.reshape(CHUNKS, rows, blocks * piece)

    turned, weights, *lists = prepare(
        place, tile_src, row_counts, tile_vals, row_size, tiles_per_owner
    )

    gathered = [gather_second(gather_first(parts[0], blocks), blocks), None]
    iterates = [None] * CHUNKS
    restarts = [None] * CHUNKS
    scale = None
    last = place
    for phase in range(ITERS * CHUNKS):
        chunk = phase % CHUNKS
        after = 1 - chunk
        first = phase < CHUNKS
        extra = EXTRA if phase == 0 else 0
        if phase > 0:
            iterates[after] = last = update(*pending)
        held, *own = assemble(place, gathered[chunk], last, blocks, tile_size, first)
        if first:
            iterates[chunk] = restarts[chunk] = own[0]
        if phase == 0:
            held, parts = lax.optimization_barrier((held, parts))
            found = gather_first(parts[1], blocks)
        elif phase + 1 < ITERS * CHUNKS:
            found = gather_first(iterates[after], blocks)
        else:
            found = []
        sent = product(1, lists, turned, held, weights, rows, chips, extra)
        other = exchange(sent, "row", 1, row_size)
        kept = product(0, lists, turned, held, weights, rows, chips, extra)
        both = kept.astype(jnp.float32) + other.astype(jnp.float32)
        states, arrivals, orders = [], [], []
        for half in range(2):
            state = both[:, : rows // 2] if half == 0 else both[:, rows // 2 :]
            states.append(state.reshape((2,) * len(chip_bits) + state.shape[1:]))
            arrivals.append(None)
            turn = half % len(chip_bits)
            orders.append(chip_bits[turn:] + chip_bits[:turn])
        left = [list(chip_bits), list(chip_bits)]
        for step in range(len(chip_bits)):
            for half in range(2):
                if step > 0:
                    states[half] = states[half] + arrivals[half].astype(jnp.float32)
                bit = orders[half][step]
                states[half], arrivals[half] = halve(states[half], left[half], bit, row_size)
                left[half].remove(bit)
            if step == 0:
                found, arrivals = lax.optimization_barrier((found, arrivals))
                if found:
                    gathered[after] = gather_second(found, blocks)
        sums = states
        if phase == 0:
            weight_rows = slice(rows // 2, rows // 2 + tiles_per_owner)
            total = 1.0 + sums[1][weight_rows] + arrivals[1][weight_rows].astype(jnp.float32)
            scale = jnp.broadcast_to(
                ((1.0 - TELEPORT) / total).reshape(rows, 1), (rows, width)
            )
        pending = (sums, arrivals, iterates[chunk], restarts[chunk], scale)
    iterates[chunk] = update(*pending)
    out = jnp.stack(iterates).reshape(CHUNKS, rows, blocks, piece).transpose(1, 2, 0, 3)
    return out.reshape(rows, CHUNKS * width)


def solution(mesh):
    placed = (P("row", "col"), P("row", "col", None), P("row", "col"), P("row", "col"))
    return jax.shard_map(
        on_device, mesh=mesh, in_specs=placed, out_specs=P(("row", "col"), None), check_vma=False
    )
```

```python
import functools

import jax
import jax.numpy as jnp
from jax import lax
from jax.experimental import pallas as pl
from jax.experimental.pallas import tpu as pltpu
from jax.sharding import PartitionSpec as P

ITERS = 3


TELEPORT = 0.1


CHUNKS = 2


UNROLL = 8


EXTRA = 16


MOST = 8


def vmem(count):
    return [pl.BlockSpec(memory_space=pltpu.VMEM)] * count


def smem(count):
    return [pl.BlockSpec(memory_space=pltpu.SMEM)] * count


def anywhere(count):
    return [pl.BlockSpec(memory_space=pl.ANY)] * count


def pair_capacity(tile_max, dest_count):
    most = (tile_max + dest_count // 2) // 2
    return -(-most // UNROLL) * UNROLL


def prepare_kernel(
    tiles_per_owner,
    place_ref,
    src_ref,
    count_ref,
    tile_ref,
    turned_ref,
    weight_ref,
    slot_ref,
    first_ref,
    second_ref,
    row_ref,
    go_on_ref,
    turns_ref,
    held_ref,
    sum_ref,
    sems,
):
    tile_max, tile_size, _ = tile_ref.shape
    dest_count = count_ref.shape[1]
    zero_tile = place_ref[2]
    my_row = place_ref[0]
    pieces = sems.shape[0]
    piece = tile_max // pieces
    copies = []
    for index in range(pieces):
        span = pl.ds(index * piece, piece)
        copies.append(
            pltpu.make_async_copy(tile_ref.at[span], held_ref.at[span], sems.at[index])
        )
        copies[-1].start()

    for half in range(2):

        def one_dest(dest, carry, half=half):
            start, used = carry
            owner = lax.div(dest, tiles_per_owner)
            relative = lax.bitwise_xor(owner, my_row)
            count = count_ref[0, dest]
            mine = lax.bitwise_and(relative, 1) == half
            pairs = jnp.where(mine, lax.div(count + 1, 2), 0)
            out_row = (
                lax.div(relative, 2) * tiles_per_owner + dest - owner * tiles_per_owner
            ) * tile_size

            def one_pair(pair, carry):
                at = used + pair
                slot = start + 2 * pair
                next_slot = jnp.minimum(slot + 1, tile_max - 1)
                slot_ref[half, at] = slot
                first_ref[half, at] = src_ref[0, slot] * tile_size
                second_ref[half, at] = (
                    jnp.where(2 * pair + 1 < count, src_ref[0, next_slot], zero_tile) * tile_size
                )
                row_ref[half, at] = out_row
                go_on_ref[half, at] = jnp.where(pair > 0, 1, 0)
                return carry

            lax.fori_loop(0, pairs, one_pair, 0)
            return start + count, used + pairs

        _, used = lax.fori_loop(0, dest_count, one_dest, (jnp.int32(0), jnp.int32(0)))
        turns = lax.div(used + UNROLL - 1, UNROLL)
        last_row = row_ref[half, used - 1]

        def one_pad(at, carry, half=half, last_row=last_row):
            slot_ref[half, at] = 0
            first_ref[half, at] = zero_tile * tile_size
            second_ref[half, at] = zero_tile * tile_size
            row_ref[half, at] = last_row
            go_on_ref[half, at] = 1
            return carry

        lax.fori_loop(used, turns * UNROLL, one_pad, 0)
        turns_ref[half] = turns

    group = min(8, piece)
    for index in range(pieces):
        copies[index].wait()

        def one_group(at, carry, index=index):
            for step in range(group):
                slot = index * piece + at * group + step
                tile = held_ref[slot]
                turned_ref[slot] = tile.T
                sum_ref[pl.ds(slot, 1), :] = jnp.sum(
                    tile.astype(jnp.float32), axis=0, keepdims=True
                )
            return carry

        lax.fori_loop(0, piece // group, one_group, 0)

    sum_ref[tile_max:, :] = jnp.zeros((MOST, tile_size), jnp.float32)
    weight_ref[...] = jnp.zeros(weight_ref.shape, weight_ref.dtype)
    places = lax.broadcasted_iota(jnp.int32, (MOST, tile_size), 0)

    def weigh(at, start):
        for step in range(tiles_per_owner):
            count = count_ref[0, at * tiles_per_owner + step]
            sums = jnp.where(places < count, sum_ref[pl.ds(start, MOST), :], 0.0)
            weight_ref[lax.bitwise_xor(at, my_row), step : step + 1, :] = jnp.sum(
                sums, axis=0, keepdims=True
            )
            start = start + count
        return start

    lax.fori_loop(0, dest_count // tiles_per_owner, weigh, jnp.int32(0))


def prepare(place, tile_src, row_counts, tile_vals, row_size, tiles_per_owner):
    tile_max, tile_size, _ = tile_vals.shape
    capacity = pair_capacity(tile_max, row_counts.shape[1])
    listing = jax.ShapeDtypeStruct((2, capacity), jnp.int32)
    return pl.pallas_call(
        functools.partial(prepare_kernel, tiles_per_owner),
        out_shape=[
            jax.ShapeDtypeStruct(tile_vals.shape, tile_vals.dtype),
            jax.ShapeDtypeStruct((row_size, EXTRA, tile_size), jnp.float32),
            listing,
            listing,
            listing,
            listing,
            listing,
            jax.ShapeDtypeStruct((2,), jnp.int32),
        ],
        in_specs=smem(3) + anywhere(1),
        out_specs=vmem(2) + smem(6),
        scratch_shapes=[
            pltpu.VMEM(tile_vals.shape, tile_vals.dtype),
            pltpu.VMEM((tile_max + MOST, tile_size), jnp.float32),
            pltpu.SemaphoreType.DMA((8,)),
        ],
        compiler_params=pltpu.CompilerParams(vmem_limit_bytes=24 * 2**20),
        name="prepare",
    )(place, tile_src, row_counts, tile_vals)


def assemble_kernel(packed, blocks, place_ref, *refs):
    block_refs = refs[:blocks]
    held_ref = refs[blocks + 1]
    staged_ref = refs[-1] if packed else held_ref
    col = place_ref[1]
    rows, width = block_refs[0].shape

    def put(mask, ref):
        first = pl.multiple_of(lax.bitwise_xor(col, mask) * rows, rows)
        staged_ref[pl.ds(first, rows), :] = ref[...]

    for mask in range(blocks):
        put(mask, block_refs[mask])
    if packed:
        piece = width // blocks
        for group in range(blocks):
            lanes = slice(group * piece, (group + 1) * piece)
            held_ref[group * rows : (group + 1) * rows, :] = jnp.concatenate(
                [staged_ref[b * rows : (b + 1) * rows, lanes] for b in range(blocks)], axis=1
            )
        own_ref = refs[blocks + 2]
        own_ref[...] = held_ref[pl.ds(pl.multiple_of(col * rows, rows), rows), :]
    zeros = held_ref.shape[0] - blocks * rows
    held_ref[blocks * rows :, :] = jnp.zeros((zeros, width), held_ref.dtype)


def assemble(place, gathered, after, tile_size, packed):
    blocks = len(gathered)
    rows, width = gathered[0].shape
    out_shape = [jax.ShapeDtypeStruct((blocks * rows + tile_size, width), jnp.bfloat16)]
    scratch = []
    if packed:
        out_shape.append(jax.ShapeDtypeStruct((rows, width), jnp.bfloat16))
        scratch.append(pltpu.VMEM((blocks * rows, width), jnp.bfloat16))
    return pl.pallas_call(
        functools.partial(assemble_kernel, packed, blocks),
        out_shape=out_shape,
        in_specs=smem(1) + vmem(blocks) + anywhere(1),
        out_specs=vmem(len(out_shape)),
        scratch_shapes=scratch,
        compiler_params=pltpu.CompilerParams(vmem_limit_bytes=4 * 2**20),
        cost_estimate=pl.CostEstimate(flops=0, bytes_accessed=4 * 2**20, transcendentals=0),
        name="assemble",
    )(place, *gathered, after)


def product_kernel(
    half,
    rows,
    slot_ref,
    first_ref,
    second_ref,
    row_ref,
    go_on_ref,
    turns_ref,
    turned_ref,
    held_ref,
    weight_ref,
    out_ref,
):
    tile_max, tile_size, _ = turned_ref.shape
    chips, out_rows, width = out_ref.shape
    if out_rows > rows:
        for chip in range(chips):
            out_ref[chip, rows:, :] = weight_ref[2 * chip + half].astype(out_ref.dtype)

    def one_turn(turn, running):
        for step in range(UNROLL):
            at = turn * UNROLL + step
            slot = slot_ref[half, at]
            left = jnp.concatenate(
                [turned_ref[slot], turned_ref[jnp.minimum(slot + 1, tile_max - 1)]], axis=1
            )
            first = pl.multiple_of(first_ref[half, at], tile_size)
            second = pl.multiple_of(second_ref[half, at], tile_size)
            right = jnp.concatenate(
                [held_ref[pl.ds(first, tile_size), :], held_ref[pl.ds(second, tile_size), :]],
                axis=0,
            )
            term = jnp.dot(left, right, preferred_element_type=jnp.float32)
            running = running * go_on_ref[half, at].astype(jnp.float32) + term
            out_row = row_ref[half, at]
            chip = lax.div(out_row, rows)
            out_row = pl.multiple_of(out_row - chip * rows, tile_size)
            out_ref[chip, pl.ds(out_row, tile_size), :] = running.astype(out_ref.dtype)
        return running

    lax.fori_loop(0, turns_ref[half], one_turn, jnp.zeros((tile_size, width), jnp.float32))


def product(half, lists, turned, held, weights, rows, chips, extra):
    return pl.pallas_call(
        functools.partial(product_kernel, half, rows),
        out_shape=jax.ShapeDtypeStruct((chips, rows + extra, held.shape[1]), jnp.bfloat16),
        in_specs=smem(len(lists)) + vmem(3),
        out_specs=vmem(1)[0],
        compiler_params=pltpu.CompilerParams(vmem_limit_bytes=4 * 2**20),
        cost_estimate=pl.CostEstimate(
            flops=600000000, bytes_accessed=6000000, transcendentals=0
        ),
        name="product",
    )(*lists, turned, held, weights)


def update_kernel(kept_ref, *refs):
    *arrived_refs, iterate_ref, restart_ref, scale_ref, out_ref = refs
    rows = out_ref.shape[0]
    summed = kept_ref[:rows, :]
    for ref in arrived_refs:
        summed = summed + ref[:rows, :].astype(jnp.float32)
    out_ref[...] = (
        scale_ref[...] * (summed + iterate_ref[...].astype(jnp.float32))
        + TELEPORT * restart_ref[...].astype(jnp.float32)
    ).astype(out_ref.dtype)


def update(kept, arrived, iterate, restart, scale):
    return pl.pallas_call(
        update_kernel,
        out_shape=jax.ShapeDtypeStruct(iterate.shape, iterate.dtype),
        in_specs=vmem(len(arrived) + 4),
        out_specs=vmem(1)[0],
        compiler_params=pltpu.CompilerParams(vmem_limit_bytes=4 * 2**20),
        cost_estimate=pl.CostEstimate(flops=0, bytes_accessed=1, transcendentals=0),
        name="update",
    )(kept, *arrived, iterate, restart, scale)


def exchange(block, axis, mask, size):
    return lax.ppermute(block, axis, [(i, i ^ mask) for i in range(size)])


def gather_line(block, size):
    return [block] + [exchange(block, "col", mask, size) for mask in range(1, size)]


def reduce_chips(both, cut, chip_bits, row_size):
    kept, arrived = [], []
    for half in range(2):
        state = both[:, :cut] if half == 0 else both[:, cut:]
        state = state.reshape((2,) * len(chip_bits) + state.shape[1:])
        left = list(chip_bits)
        turn = half % len(chip_bits)
        got = None
        for bit in chip_bits[turn:] + chip_bits[:turn]:
            if got is not None:
                state = state + got.astype(jnp.float32)
            axis = left.index(bit)
            send = lax.index_in_dim(state, 1, axis, keepdims=False).astype(jnp.bfloat16)
            state = lax.index_in_dim(state, 0, axis, keepdims=False)
            got = exchange(send, "row", 1 << bit, row_size)
            left.remove(bit)
        kept.append(state)
        arrived.append(got)
    return jnp.concatenate(kept), jnp.concatenate(arrived)


def on_device(features, tile_vals, tile_src, row_counts):
    row_size = lax.axis_size("row")
    blocks = lax.axis_size("col")
    my_row = lax.axis_index("row").astype(jnp.int32)
    my_col = lax.axis_index("col").astype(jnp.int32)
    tile_size = tile_vals.shape[1]
    dest_count = row_counts.shape[1]
    rows = features.shape[0] // blocks
    source_tiles = features.shape[0] // tile_size
    width = features.shape[1] * blocks // CHUNKS
    piece = features.shape[1] // CHUNKS
    tiles_per_owner = dest_count // row_size
    chips = row_size // 2
    chip_bits = list(range(row_size.bit_length() - 2, 0, -1))
    place = jnp.stack([my_row, my_col, jnp.int32(source_tiles)])

    parts = features.reshape(blocks, rows, CHUNKS, piece).transpose(2, 1, 0, 3)
    parts = parts.reshape(CHUNKS, rows, blocks * piece)

    turned, weights, *lists = prepare(
        place, tile_src, row_counts, tile_vals, row_size, tiles_per_owner
    )

    gathered = [gather_line(parts[0], blocks), None]
    iterates = [None] * CHUNKS
    restarts = [None] * CHUNKS
    scale = None
    last = place
    for phase in range(ITERS * CHUNKS):
        chunk = phase % CHUNKS
        after = 1 - chunk
        first = phase < CHUNKS
        extra = EXTRA if phase == 0 else 0
        if phase > 0:
            iterates[after] = last = update(*pending)
        held, *own = assemble(place, gathered[chunk], last, tile_size, first)
        if first:
            iterates[chunk] = restarts[chunk] = own[0]
        if phase == 0:
            held, parts = lax.optimization_barrier((held, parts))
            gathered[after] = gather_line(parts[1], blocks)
        elif phase + 1 < ITERS * CHUNKS:
            gathered[after] = gather_line(iterates[after], blocks)
        sent = product(1, lists, turned, held, weights, rows, chips, extra)
        other = exchange(sent, "row", 1, row_size)
        kept = product(0, lists, turned, held, weights, rows, chips, extra)
        both = kept.astype(jnp.float32) + other.astype(jnp.float32)
        kept, arrived = reduce_chips(both, rows // 2, chip_bits, row_size)
        if phase == 0:
            weight_rows = slice(rows, rows + tiles_per_owner)
            total = 1.0 + kept[weight_rows] + arrived[weight_rows].astype(jnp.float32)
            scale = jnp.broadcast_to(
                ((1.0 - TELEPORT) / total).reshape(rows, 1), (rows, width)
            )
        pending = (kept, [arrived], iterates[chunk], restarts[chunk], scale)
    iterates[chunk] = update(*pending)
    out = jnp.stack(iterates).reshape(CHUNKS, rows, blocks, piece).transpose(1, 2, 0, 3)
    return out.reshape(rows, CHUNKS * width)


def solution(mesh):
    placed = (P("row", "col"), P("row", "col", None), P("row", "col"), P("row", "col"))
    return jax.shard_map(
        on_device, mesh=mesh, in_specs=placed, out_specs=P(("row", "col"), None), check_vma=False
    )
```

```python
import functools

import jax
import jax.numpy as jnp
from jax import lax
from jax.experimental import pallas as pl
from jax.experimental.pallas import tpu as pltpu
from jax.sharding import PartitionSpec as P

ITERS = 3


TELEPORT = 0.1


CHUNKS = 2


UNROLL = 8


EXTRA = 16


MOST = 8


def vmem(count):
    return [pl.BlockSpec(memory_space=pltpu.VMEM)] * count


def smem(count):
    return [pl.BlockSpec(memory_space=pltpu.SMEM)] * count


def anywhere(count):
    return [pl.BlockSpec(memory_space=pl.ANY)] * count


def hbm(count):
    return [pl.BlockSpec(memory_space=pltpu.HBM)] * count


def pair_capacity(tile_max, dest_count):
    most = (tile_max + dest_count // 2) // 2
    return -(-most // UNROLL) * UNROLL


SLOT, FIRST, SECOND, CHIP, ROW, GO_ON, TURNS, FIELDS = range(8)


def chip_place(relative, owner, chip_bits):
    place = jnp.int32(0)
    turned = jnp.int32(0)
    for bit in range(chip_bits):
        value = lax.bitwise_and(lax.shift_right_logical(relative, bit + 1), 1)
        place = place + value * (1 << bit)
        turned = turned + value * (1 << (chip_bits - 1 - bit))
    return jnp.where(lax.bitwise_and(owner, 1) == 0, place, turned)


def prepare_kernel(
    tiles_per_owner,
    chip_bits,
    place_ref,
    src_ref,
    count_ref,
    tile_ref,
    turned_ref,
    weight_ref,
    list_ref,
    held_ref,
    staged_ref,
    sum_ref,
    in_sems,
    out_sems,
):
    tile_max, tile_size, _ = tile_ref.shape
    dest_count = count_ref.shape[1]
    zero_tile = place_ref[2]
    my_row = place_ref[0]
    pieces = in_sems.shape[0]
    piece = tile_max // pieces
    spans = [pl.ds(index * piece, piece) for index in range(pieces)]
    copies_in = [
        pltpu.make_async_copy(tile_ref.at[span], held_ref.at[span], in_sems.at[index])
        for index, span in enumerate(spans)
    ]
    copies_out = [
        pltpu.make_async_copy(staged_ref.at[span], turned_ref.at[span], out_sems.at[index])
        for index, span in enumerate(spans)
    ]
    for copy in copies_in:
        copy.start()

    for half in range(2):
        base = half * FIELDS

        def one_dest(dest, carry, half=half, base=base):
            start, used = carry
            owner = lax.div(dest, tiles_per_owner)
            relative = lax.bitwise_xor(owner, my_row)
            count = count_ref[0, dest]
            mine = lax.bitwise_and(relative, 1) == half
            pairs = jnp.where(mine, lax.div(count + 1, 2), 0)
            chip = chip_place(relative, owner, chip_bits)
            out_row = (dest - owner * tiles_per_owner) * tile_size

            def one_pair(pair, carry):
                at = used + pair
                slot = start + 2 * pair
                next_slot = jnp.minimum(slot + 1, tile_max - 1)
                list_ref[base + SLOT, at] = slot
                list_ref[base + FIRST, at] = src_ref[0, slot] * tile_size
                list_ref[base + SECOND, at] = (
                    jnp.where(2 * pair + 1 < count, src_ref[0, next_slot], zero_tile) * tile_size
                )
                list_ref[base + CHIP, at] = chip
                list_ref[base + ROW, at] = out_row
                list_ref[base + GO_ON, at] = jnp.where(pair > 0, 1, 0)
                return carry

            lax.fori_loop(0, pairs, one_pair, 0)
            return start + count, used + pairs

        _, used = lax.fori_loop(0, dest_count, one_dest, (jnp.int32(0), jnp.int32(0)))
        turns = lax.div(used + UNROLL - 1, UNROLL)
        last_chip = list_ref[base + CHIP, used - 1]
        last_row = list_ref[base + ROW, used - 1]

        def one_pad(at, carry, base=base, last_chip=last_chip, last_row=last_row):
            list_ref[base + SLOT, at] = 0
            list_ref[base + FIRST, at] = zero_tile * tile_size
            list_ref[base + SECOND, at] = zero_tile * tile_size
            list_ref[base + CHIP, at] = last_chip
            list_ref[base + ROW, at] = last_row
            list_ref[base + GO_ON, at] = 1
            return carry

        lax.fori_loop(used, turns * UNROLL, one_pad, 0)
        list_ref[base + TURNS, 0] = turns

    group = min(8, piece)
    for index in range(pieces):
        copies_in[index].wait()

        def one_group(at, carry, index=index):
            for step in range(group):
                slot = index * piece + at * group + step
                tile = held_ref[slot]
                staged_ref[slot] = tile.T
                sum_ref[pl.ds(slot, 1), :] = jnp.sum(
                    tile.astype(jnp.float32), axis=0, keepdims=True
                )
            return carry

        lax.fori_loop(0, piece // group, one_group, 0)
        copies_out[index].start()

    sum_ref[tile_max:, :] = jnp.zeros((MOST, tile_size), jnp.float32)
    weight_ref[...] = jnp.zeros(weight_ref.shape, weight_ref.dtype)
    places = lax.broadcasted_iota(jnp.int32, (MOST, tile_size), 0)

    def weigh(owner, start):
        relative = lax.bitwise_xor(owner, my_row)
        chip = chip_place(relative, owner, chip_bits)
        for step in range(tiles_per_owner):
            count = count_ref[0, owner * tiles_per_owner + step]
            sums = jnp.where(places < count, sum_ref[pl.ds(start, MOST), :], 0.0)
            weight_ref[lax.bitwise_and(relative, 1), chip, step : step + 1, :] = jnp.sum(
                sums, axis=0, keepdims=True
            )
            start = start + count
        return start

    lax.fori_loop(0, dest_count // tiles_per_owner, weigh, jnp.int32(0))
    for copy in copies_out:
        copy.wait()


def prepare(place, tile_src, row_counts, tile_vals, row_size, tiles_per_owner):
    tile_max, tile_size, _ = tile_vals.shape
    capacity = pair_capacity(tile_max, row_counts.shape[1])
    chips = row_size // 2
    return pl.pallas_call(
        functools.partial(prepare_kernel, tiles_per_owner, chips.bit_length() - 1),
        out_shape=[
            jax.ShapeDtypeStruct(tile_vals.shape, tile_vals.dtype),
            jax.ShapeDtypeStruct((2, chips, EXTRA, tile_size), jnp.float32),
            jax.ShapeDtypeStruct((2 * FIELDS, capacity), jnp.int32),
        ],
        in_specs=smem(3) + hbm(1),
        out_specs=hbm(1) + vmem(1) + smem(1),
        scratch_shapes=[
            pltpu.VMEM(tile_vals.shape, tile_vals.dtype),
            pltpu.VMEM(tile_vals.shape, tile_vals.dtype),
            pltpu.VMEM((tile_max + MOST, tile_size), jnp.float32),
            pltpu.SemaphoreType.DMA((8,)),
            pltpu.SemaphoreType.DMA((8,)),
        ],
        compiler_params=pltpu.CompilerParams(vmem_limit_bytes=24 * 2**20),
        name="prepare",
    )(place, tile_src, row_counts, tile_vals)


def assemble_kernel(packed, blocks, *refs):
    block_refs = refs[:blocks]
    held_ref = refs[blocks + 1]
    staged_ref = refs[-1] if packed else held_ref
    col = lax.axis_index("col")
    rows, width = block_refs[0].shape

    def put(mask, ref):
        first = pl.multiple_of(lax.bitwise_xor(col, mask) * rows, rows)
        staged_ref[pl.ds(first, rows), :] = ref[...]

    for mask in range(blocks):
        put(mask, block_refs[mask])
    if packed:
        piece = width // blocks
        for group in range(blocks):
            lanes = slice(group * piece, (group + 1) * piece)
            held_ref[group * rows : (group + 1) * rows, :] = jnp.concatenate(
                [staged_ref[b * rows : (b + 1) * rows, lanes] for b in range(blocks)], axis=1
            )
        own_ref = refs[blocks + 2]
        own_ref[...] = held_ref[pl.ds(pl.multiple_of(col * rows, rows), rows), :]
    zeros = held_ref.shape[0] - blocks * rows
    held_ref[blocks * rows :, :] = jnp.zeros((zeros, width), held_ref.dtype)


def assemble(gathered, after, tile_size, packed):
    blocks = len(gathered)
    rows, width = gathered[0].shape
    out_shape = [jax.ShapeDtypeStruct((blocks * rows + tile_size, width), jnp.bfloat16)]
    scratch = []
    if packed:
        out_shape.append(jax.ShapeDtypeStruct((rows, width), jnp.bfloat16))
        scratch.append(pltpu.VMEM((blocks * rows, width), jnp.bfloat16))
    return pl.pallas_call(
        functools.partial(assemble_kernel, packed, blocks),
        out_shape=out_shape,
        in_specs=vmem(blocks) + anywhere(1),
        out_specs=vmem(len(out_shape)),
        scratch_shapes=scratch,
        compiler_params=pltpu.CompilerParams(vmem_limit_bytes=4 * 2**20),
        cost_estimate=pl.CostEstimate(flops=0, bytes_accessed=4 * 2**20, transcendentals=0),
        name="assemble",
    )(*gathered, after)


def product_kernel(half, rows, list_ref, turned_ref, held_ref, weight_ref, out_ref):
    tile_max, tile_size, _ = turned_ref.shape
    chips, out_rows, width = out_ref.shape
    base = half * FIELDS
    if out_rows > rows:
        out_ref[:, rows:, :] = weight_ref[half].astype(out_ref.dtype)

    def one_turn(turn, running):
        for step in range(UNROLL):
            at = turn * UNROLL + step
            slot = list_ref[base + SLOT, at]
            left = jnp.concatenate(
                [turned_ref[slot], turned_ref[jnp.minimum(slot + 1, tile_max - 1)]], axis=1
            )
            first = pl.multiple_of(list_ref[base + FIRST, at], tile_size)
            second = pl.multiple_of(list_ref[base + SECOND, at], tile_size)
            right = jnp.concatenate(
                [held_ref[pl.ds(first, tile_size), :], held_ref[pl.ds(second, tile_size), :]],
                axis=0,
            )
            term = jnp.dot(left, right, preferred_element_type=jnp.float32)
            running = running * list_ref[base + GO_ON, at].astype(jnp.float32) + term
            row = pl.multiple_of(list_ref[base + ROW, at], tile_size)
            out_ref[list_ref[base + CHIP, at], pl.ds(row, tile_size), :] = running.astype(
                out_ref.dtype
            )
        return running

    lax.fori_loop(
        0, list_ref[base + TURNS, 0], one_turn, jnp.zeros((tile_size, width), jnp.float32)
    )


def product(half, pairs, turned, held, weights, rows, chips, extra):
    return pl.pallas_call(
        functools.partial(product_kernel, half, rows),
        out_shape=jax.ShapeDtypeStruct((chips, rows + extra, held.shape[1]), jnp.bfloat16),
        in_specs=smem(1) + vmem(3),
        out_specs=vmem(1)[0],
        compiler_params=pltpu.CompilerParams(vmem_limit_bytes=4 * 2**20),
        cost_estimate=pl.CostEstimate(
            flops=600000000, bytes_accessed=6000000, transcendentals=0
        ),
        name="product",
    )(pairs, turned, held, weights)


def update_kernel(kept_ref, *refs):
    *arrived_refs, iterate_ref, restart_ref, scale_ref, out_ref = refs
    rows = out_ref.shape[0]
    summed = kept_ref[:rows, :]
    for ref in arrived_refs:
        summed = summed + ref[:rows, :].astype(jnp.float32)
    out_ref[...] = (
        scale_ref[...] * (summed + iterate_ref[...].astype(jnp.float32))
        + TELEPORT * restart_ref[...].astype(jnp.float32)
    ).astype(out_ref.dtype)


def update(kept, arrived, iterate, restart, scale):
    return pl.pallas_call(
        update_kernel,
        out_shape=jax.ShapeDtypeStruct(iterate.shape, iterate.dtype),
        in_specs=vmem(len(arrived) + 4),
        out_specs=vmem(1)[0],
        compiler_params=pltpu.CompilerParams(vmem_limit_bytes=4 * 2**20),
        cost_estimate=pl.CostEstimate(flops=0, bytes_accessed=1, transcendentals=0),
        name="update",
    )(kept, *arrived, iterate, restart, scale)


def exchange(block, axis, mask, size):
    return lax.ppermute(block, axis, [(i, i ^ mask) for i in range(size)])


def gather_line(block, size):
    return [block] + [exchange(block, "col", mask, size) for mask in range(1, size)]


def reduce_chips(state, chip_bits, row_size):
    arrived = None
    for step in range(chip_bits):
        if arrived is not None:
            state = state + arrived.astype(jnp.float32)
        cut = state.shape[0] // 2
        send = state[cut:].astype(jnp.bfloat16)
        state = state[:cut]
        bits = (chip_bits - step, 1 + step)
        arrived = lax.ppermute(
            send, "row", [(i, i ^ (1 << bits[i % 2])) for i in range(row_size)]
        )
    return state[0], arrived[0]


def on_device(features, tile_vals, tile_src, row_counts):
    row_size = lax.axis_size("row")
    blocks = lax.axis_size("col")
    my_row = lax.axis_index("row").astype(jnp.int32)
    my_col = lax.axis_index("col").astype(jnp.int32)
    tile_size = tile_vals.shape[1]
    dest_count = row_counts.shape[1]
    rows = features.shape[0] // blocks
    source_tiles = features.shape[0] // tile_size
    width = features.shape[1] * blocks // CHUNKS
    piece = features.shape[1] // CHUNKS
    tiles_per_owner = dest_count // row_size
    chips = row_size // 2
    place = jnp.stack([my_row, my_col, jnp.int32(source_tiles)])

    parts = features.reshape(blocks, rows, CHUNKS, piece).transpose(2, 1, 0, 3)
    parts = parts.reshape(CHUNKS, rows, blocks * piece)

    turned, weights, pairs = prepare(
        place, tile_src, row_counts, tile_vals, row_size, tiles_per_owner
    )

    gathered = [gather_line(parts[0], blocks), None]
    iterates = [None] * CHUNKS
    restarts = [None] * CHUNKS
    scale = None
    last = place
    for phase in range(ITERS * CHUNKS):
        chunk = phase % CHUNKS
        after = 1 - chunk
        first = phase < CHUNKS
        extra = EXTRA if phase == 0 else 0
        if phase > 0:
            iterates[after] = last = update(*pending)
        held, *own = assemble(gathered[chunk], last, tile_size, first)
        if first:
            iterates[chunk] = restarts[chunk] = own[0]
        if phase == 0:
            held, parts = lax.optimization_barrier((held, parts))
            gathered[after] = gather_line(parts[1], blocks)
        elif phase + 1 < ITERS * CHUNKS:
            gathered[after] = gather_line(iterates[after], blocks)
        sent = product(1, pairs, turned, held, weights, rows, chips, extra)
        other = exchange(sent, "row", 1, row_size)
        kept = product(0, pairs, turned, held, weights, rows, chips, extra)
        both = kept.astype(jnp.float32) + other.astype(jnp.float32)
        kept, arrived = reduce_chips(both, chips.bit_length() - 1, row_size)
        if phase == 0:
            weight_rows = slice(rows, rows + tiles_per_owner)
            total = 1.0 + kept[weight_rows] + arrived[weight_rows].astype(jnp.float32)
            scale = jnp.broadcast_to(
                ((1.0 - TELEPORT) / total).reshape(rows, 1), (rows, width)
            )
        pending = (kept, [arrived], iterates[chunk], restarts[chunk], scale)
    iterates[chunk] = update(*pending)
    out = jnp.stack(iterates).reshape(CHUNKS, rows, blocks, piece).transpose(1, 2, 0, 3)
    return out.reshape(rows, CHUNKS * width)


def solution(mesh):
    placed = (P("row", "col"), P("row", "col", None), P("row", "col"), P("row", "col"))
    return jax.shard_map(
        on_device, mesh=mesh, in_specs=placed, out_specs=P(("row", "col"), None), check_vma=False
    )
```

```python
import functools

import jax
import jax.numpy as jnp
from jax import lax
from jax.experimental import pallas as pl
from jax.experimental.pallas import tpu as pltpu
from jax.sharding import PartitionSpec as P

ITERS = 3


TELEPORT = 0.1


CHUNKS = 2


UNROLL = 8


EXTRA = 16


MOST = 8


def vmem(count):
    return [pl.BlockSpec(memory_space=pltpu.VMEM)] * count


def smem(count):
    return [pl.BlockSpec(memory_space=pltpu.SMEM)] * count


def anywhere(count):
    return [pl.BlockSpec(memory_space=pl.ANY)] * count


def hbm(count):
    return [pl.BlockSpec(memory_space=pltpu.HBM)] * count


def pair_capacity(tile_max, dest_count):
    most = (tile_max + dest_count // 2) // 2
    return -(-most // UNROLL) * UNROLL


def code_bits(tile_max, source_tiles, half_dests):
    sizes = (tile_max, source_tiles + 1, source_tiles + 1, half_dests, 2)
    widths = [(size - 1).bit_length() for size in sizes]
    assert sum(widths) < 32
    return [(sum(widths[at + 1 :]), (1 << width) - 1) for at, width in enumerate(widths)]


def encode(fields, bits):
    code = jnp.int32(0)
    for field, (shift, _) in zip(fields, bits):
        code = code + lax.shift_left(field, jnp.int32(shift))
    return code


def decode(code, bits):
    return [
        lax.bitwise_and(lax.shift_right_logical(code, jnp.int32(shift)), jnp.int32(mask))
        for shift, mask in bits
    ]


def chip_place(relative, owner, chip_bits):
    place = jnp.int32(0)
    turned = jnp.int32(0)
    for bit in range(chip_bits):
        value = lax.bitwise_and(lax.shift_right_logical(relative, bit + 1), 1)
        place = place + value * (1 << bit)
        turned = turned + value * (1 << (chip_bits - 1 - bit))
    return jnp.where(lax.bitwise_and(owner, 1) == 0, place, turned)


def prepare_kernel(
    tiles_per_owner,
    chip_bits,
    bits,
    place_ref,
    src_ref,
    count_ref,
    tile_ref,
    turned_ref,
    weight_ref,
    list_ref,
    held_ref,
    staged_ref,
    sum_ref,
    in_sems,
    out_sems,
):
    tile_max, tile_size, _ = tile_ref.shape
    dest_count = count_ref.shape[1]
    zero_tile = place_ref[2]
    my_row = place_ref[0]
    pieces = in_sems.shape[0]
    piece = tile_max // pieces
    spans = [pl.ds(index * piece, piece) for index in range(pieces)]
    copies_in = [
        pltpu.make_async_copy(tile_ref.at[span], held_ref.at[span], in_sems.at[index])
        for index, span in enumerate(spans)
    ]
    copies_out = [
        pltpu.make_async_copy(staged_ref.at[span], turned_ref.at[span], out_sems.at[index])
        for index, span in enumerate(spans)
    ]
    for copy in copies_in:
        copy.start()

    rows_each = (list_ref.shape[0] - 2) // 2

    for half in range(2):

        def put(at, fields, half=half):
            row = lax.div(at, UNROLL)
            list_ref[half * rows_each + row, at - row * UNROLL] = encode(fields, bits)

        def one_dest(dest, carry, half=half, put=put):
            start, used, _ = carry
            owner = lax.div(dest, tiles_per_owner)
            relative = lax.bitwise_xor(owner, my_row)
            count = count_ref[0, dest]
            mine = lax.bitwise_and(relative, 1) == half
            pairs = jnp.where(mine, lax.div(count + 1, 2), 0)
            chip = chip_place(relative, owner, chip_bits)
            target = chip * tiles_per_owner + dest - owner * tiles_per_owner

            def one_pair(pair, carry):
                slot = start + 2 * pair
                next_slot = jnp.minimum(slot + 1, tile_max - 1)
                second = jnp.where(2 * pair + 1 < count, src_ref[0, next_slot], zero_tile)
                go_on = jnp.where(pair > 0, 1, 0)
                put(used + pair, (slot, src_ref[0, slot], second, target, go_on))
                return carry

            lax.fori_loop(0, pairs, one_pair, 0)
            return start + count, used + pairs, jnp.where(mine, target, carry[2])

        zero = jnp.int32(0)
        _, used, last = lax.fori_loop(0, dest_count, one_dest, (zero, zero, zero))
        turns = lax.div(used + UNROLL - 1, UNROLL)

        def one_pad(at, carry, put=put, last=last):
            put(at, (jnp.int32(0), zero_tile, zero_tile, last, jnp.int32(1)))
            return carry

        lax.fori_loop(used, turns * UNROLL, one_pad, 0)
        for column in range(UNROLL):
            list_ref[2 * rows_each + half, column] = turns

    group = min(8, piece)
    for index in range(pieces):
        copies_in[index].wait()

        def one_group(at, carry, index=index):
            for step in range(group):
                slot = index * piece + at * group + step
                tile = held_ref[slot]
                staged_ref[slot] = tile.T
                sum_ref[pl.ds(slot, 1), :] = jnp.sum(
                    tile.astype(jnp.float32), axis=0, keepdims=True
                )
            return carry

        lax.fori_loop(0, piece // group, one_group, 0)
        copies_out[index].start()

    sum_ref[tile_max:, :] = jnp.zeros((MOST, tile_size), jnp.float32)
    weight_ref[...] = jnp.zeros(weight_ref.shape, weight_ref.dtype)
    places = lax.broadcasted_iota(jnp.int32, (MOST, tile_size), 0)

    def weigh(owner, start):
        relative = lax.bitwise_xor(owner, my_row)
        chip = chip_place(relative, owner, chip_bits)
        for step in range(tiles_per_owner):
            count = count_ref[0, owner * tiles_per_owner + step]
            sums = jnp.where(places < count, sum_ref[pl.ds(start, MOST), :], 0.0)
            weight_ref[lax.bitwise_and(relative, 1), chip, step : step + 1, :] = jnp.sum(
                sums, axis=0, keepdims=True
            )
            start = start + count
        return start

    lax.fori_loop(0, dest_count // tiles_per_owner, weigh, jnp.int32(0))
    for copy in copies_out:
        copy.wait()


def prepare(place, tile_src, row_counts, tile_vals, row_size, tiles_per_owner, bits):
    tile_max, tile_size, _ = tile_vals.shape
    capacity = pair_capacity(tile_max, row_counts.shape[1])
    chips = row_size // 2
    return pl.pallas_call(
        functools.partial(
            prepare_kernel, tiles_per_owner, chips.bit_length() - 1, bits
        ),
        out_shape=[
            jax.ShapeDtypeStruct(tile_vals.shape, tile_vals.dtype),
            jax.ShapeDtypeStruct((2, chips, EXTRA, tile_size), jnp.float32),
            jax.ShapeDtypeStruct((2 * (capacity // UNROLL) + 2, UNROLL), jnp.int32),
        ],
        in_specs=smem(3) + hbm(1),
        out_specs=hbm(1) + vmem(1) + smem(1),
        scratch_shapes=[
            pltpu.VMEM(tile_vals.shape, tile_vals.dtype),
            pltpu.VMEM(tile_vals.shape, tile_vals.dtype),
            pltpu.VMEM((tile_max + MOST, tile_size), jnp.float32),
            pltpu.SemaphoreType.DMA((8,)),
            pltpu.SemaphoreType.DMA((8,)),
        ],
        compiler_params=pltpu.CompilerParams(vmem_limit_bytes=24 * 2**20),
        name="prepare",
    )(place, tile_src, row_counts, tile_vals)


def assemble_kernel(packed, blocks, *refs):
    block_refs = refs[:blocks]
    held_ref = refs[blocks + 1]
    staged_ref = refs[-1] if packed else held_ref
    col = lax.axis_index("col")
    rows, width = block_refs[0].shape

    def put(mask, ref):
        first = pl.multiple_of(lax.bitwise_xor(col, mask) * rows, rows)
        staged_ref[pl.ds(first, rows), :] = ref[...]

    for mask in range(blocks):
        put(mask, block_refs[mask])
    if packed:
        piece = width // blocks
        for group in range(blocks):
            lanes = slice(group * piece, (group + 1) * piece)
            held_ref[group * rows : (group + 1) * rows, :] = jnp.concatenate(
                [staged_ref[b * rows : (b + 1) * rows, lanes] for b in range(blocks)], axis=1
            )
        own_ref = refs[blocks + 2]
        own_ref[...] = held_ref[pl.ds(pl.multiple_of(col * rows, rows), rows), :]
    zeros = held_ref.shape[0] - blocks * rows
    held_ref[blocks * rows :, :] = jnp.zeros((zeros, width), held_ref.dtype)


def assemble(gathered, after, tile_size, packed):
    blocks = len(gathered)
    rows, width = gathered[0].shape
    out_shape = [jax.ShapeDtypeStruct((blocks * rows + tile_size, width), jnp.bfloat16)]
    scratch = []
    if packed:
        out_shape.append(jax.ShapeDtypeStruct((rows, width), jnp.bfloat16))
        scratch.append(pltpu.VMEM((blocks * rows, width), jnp.bfloat16))
    return pl.pallas_call(
        functools.partial(assemble_kernel, packed, blocks),
        out_shape=out_shape,
        in_specs=vmem(blocks) + anywhere(1),
        out_specs=vmem(len(out_shape)),
        scratch_shapes=scratch,
        compiler_params=pltpu.CompilerParams(vmem_limit_bytes=4 * 2**20),
        cost_estimate=pl.CostEstimate(flops=0, bytes_accessed=4 * 2**20, transcendentals=0),
        name="assemble",
    )(*gathered, after)


def product_kernel(half, rows, bits, list_ref, turned_ref, held_ref, weight_ref, out_ref):
    tile_max, tile_size, _ = turned_ref.shape
    chips, out_rows, width = out_ref.shape
    rows_each = (list_ref.shape[0] - 2) // 2
    tiles = rows // tile_size
    if out_rows > rows:
        out_ref[:, rows:, :] = weight_ref[half].astype(out_ref.dtype)

    def codes_of(row):
        line = list_ref[pl.ds(row, 1), :]
        return tuple(line[0, step] for step in range(UNROLL))

    def one_turn(turn, carry):
        running, codes = carry
        later = codes_of(half * rows_each + turn + 1)
        for step in range(UNROLL):
            slot, first, second, target, go_on = decode(codes[step], bits)
            left = jnp.concatenate(
                [turned_ref[slot], turned_ref[jnp.minimum(slot + 1, tile_max - 1)]], axis=1
            )
            first = pl.multiple_of(first * tile_size, tile_size)
            second = pl.multiple_of(second * tile_size, tile_size)
            right = jnp.concatenate(
                [held_ref[pl.ds(first, tile_size), :], held_ref[pl.ds(second, tile_size), :]],
                axis=0,
            )
            term = jnp.dot(left, right, preferred_element_type=jnp.float32)
            running = running * go_on.astype(jnp.float32) + term
            chip = lax.div(target, tiles)
            row = pl.multiple_of((target - chip * tiles) * tile_size, tile_size)
            out_ref[chip, pl.ds(row, tile_size), :] = running.astype(out_ref.dtype)
        return running, later

    turns = list_ref[2 * rows_each + half : 2 * rows_each + half + 1, :][0, 0]
    zeros = jnp.zeros((tile_size, width), jnp.float32)
    lax.fori_loop(0, turns, one_turn, (zeros, codes_of(half * rows_each)))


def product(half, pairs, turned, held, weights, rows, chips, extra, bits):
    return pl.pallas_call(
        functools.partial(product_kernel, half, rows, bits),
        out_shape=jax.ShapeDtypeStruct((chips, rows + extra, held.shape[1]), jnp.bfloat16),
        in_specs=vmem(4),
        out_specs=vmem(1)[0],
        compiler_params=pltpu.CompilerParams(vmem_limit_bytes=4 * 2**20),
        cost_estimate=pl.CostEstimate(
            flops=600000000, bytes_accessed=6000000, transcendentals=0
        ),
        name="product",
    )(pairs, turned, held, weights)


def update_kernel(kept_ref, *refs):
    *arrived_refs, iterate_ref, restart_ref, scale_ref, out_ref = refs
    rows = out_ref.shape[0]
    summed = kept_ref[:rows, :]
    for ref in arrived_refs:
        summed = summed + ref[:rows, :].astype(jnp.float32)
    out_ref[...] = (
        scale_ref[...] * (summed + iterate_ref[...].astype(jnp.float32))
        + TELEPORT * restart_ref[...].astype(jnp.float32)
    ).astype(out_ref.dtype)


def update(kept, arrived, iterate, restart, scale):
    return pl.pallas_call(
        update_kernel,
        out_shape=jax.ShapeDtypeStruct(iterate.shape, iterate.dtype),
        in_specs=vmem(len(arrived) + 4),
        out_specs=vmem(1)[0],
        compiler_params=pltpu.CompilerParams(vmem_limit_bytes=4 * 2**20),
        cost_estimate=pl.CostEstimate(flops=0, bytes_accessed=1, transcendentals=0),
        name="update",
    )(kept, *arrived, iterate, restart, scale)


def exchange(block, axis, mask, size):
    return lax.ppermute(block, axis, [(i, i ^ mask) for i in range(size)])


def gather_line(block, size):
    return [block] + [exchange(block, "col", mask, size) for mask in range(1, size)]


def reduce_chips(state, chip_bits, row_size):
    arrived = None
    for step in range(chip_bits):
        if arrived is not None:
            state = state + arrived.astype(jnp.float32)
        cut = state.shape[0] // 2
        send = state[cut:].astype(jnp.bfloat16)
        state = state[:cut]
        bits = (chip_bits - step, 1 + step)
        arrived = lax.ppermute(
            send, "row", [(i, i ^ (1 << bits[i % 2])) for i in range(row_size)]
        )
    return state[0], arrived[0]


def on_device(features, tile_vals, tile_src, row_counts):
    row_size = lax.axis_size("row")
    blocks = lax.axis_size("col")
    my_row = lax.axis_index("row").astype(jnp.int32)
    my_col = lax.axis_index("col").astype(jnp.int32)
    tile_size = tile_vals.shape[1]
    dest_count = row_counts.shape[1]
    rows = features.shape[0] // blocks
    source_tiles = features.shape[0] // tile_size
    width = features.shape[1] * blocks // CHUNKS
    piece = features.shape[1] // CHUNKS
    tiles_per_owner = dest_count // row_size
    chips = row_size // 2
    bits = code_bits(tile_vals.shape[0], source_tiles, dest_count // 2)
    place = jnp.stack([my_row, my_col, jnp.int32(source_tiles)])

    parts = features.reshape(blocks, rows, CHUNKS, piece).transpose(2, 1, 0, 3)
    parts = parts.reshape(CHUNKS, rows, blocks * piece)

    turned, weights, pairs = prepare(
        place, tile_src, row_counts, tile_vals, row_size, tiles_per_owner, bits
    )

    gathered = [gather_line(parts[0], blocks), None]
    iterates = [None] * CHUNKS
    restarts = [None] * CHUNKS
    scale = None
    last = place
    for phase in range(ITERS * CHUNKS):
        chunk = phase % CHUNKS
        after = 1 - chunk
        first = phase < CHUNKS
        extra = EXTRA if phase == 0 else 0
        if phase > 0:
            iterates[after] = last = update(*pending)
        held, *own = assemble(gathered[chunk], last, tile_size, first)
        if first:
            iterates[chunk] = restarts[chunk] = own[0]
        if phase == 0:
            held, parts = lax.optimization_barrier((held, parts))
            gathered[after] = gather_line(parts[1], blocks)
        elif phase + 1 < ITERS * CHUNKS:
            gathered[after] = gather_line(iterates[after], blocks)
        sent = product(1, pairs, turned, held, weights, rows, chips, extra, bits)
        other = exchange(sent, "row", 1, row_size)
        kept = product(0, pairs, turned, held, weights, rows, chips, extra, bits)
        both = kept.astype(jnp.float32) + other.astype(jnp.float32)
        kept, arrived = reduce_chips(both, chips.bit_length() - 1, row_size)
        if phase == 0:
            weight_rows = slice(rows, rows + tiles_per_owner)
            total = 1.0 + kept[weight_rows] + arrived[weight_rows].astype(jnp.float32)
            scale = jnp.broadcast_to(
                ((1.0 - TELEPORT) / total).reshape(rows, 1), (rows, width)
            )
        pending = (kept, [arrived], iterates[chunk], restarts[chunk], scale)
    iterates[chunk] = update(*pending)
    out = jnp.stack(iterates).reshape(CHUNKS, rows, blocks, piece).transpose(1, 2, 0, 3)
    return out.reshape(rows, CHUNKS * width)


def solution(mesh):
    placed = (P("row", "col"), P("row", "col", None), P("row", "col"), P("row", "col"))
    return jax.shard_map(
        on_device, mesh=mesh, in_specs=placed, out_specs=P(("row", "col"), None), check_vma=False
    )
```

```python
import functools

import jax
import jax.numpy as jnp
from jax import lax
from jax.experimental import pallas as pl
from jax.experimental.pallas import tpu as pltpu
from jax.sharding import PartitionSpec as P

ITERS = 3


TELEPORT = 0.1


CHUNKS = 2


UNROLL = 8


EXTRA = 16


MOST = 8


def vmem(count):
    return [pl.BlockSpec(memory_space=pltpu.VMEM)] * count


def smem(count):
    return [pl.BlockSpec(memory_space=pltpu.SMEM)] * count


def anywhere(count):
    return [pl.BlockSpec(memory_space=pl.ANY)] * count


def hbm(count):
    return [pl.BlockSpec(memory_space=pltpu.HBM)] * count


def pair_capacity(tile_max, dest_count):
    most = (tile_max + dest_count // 2) // 2
    return -(-most // UNROLL) * UNROLL


def code_bits(tile_max, source_tiles, half_dests):
    sizes = (tile_max, source_tiles + 1, source_tiles + 1, half_dests, 2)
    widths = [(size - 1).bit_length() for size in sizes]
    assert sum(widths) < 32
    return [(sum(widths[at + 1 :]), (1 << width) - 1) for at, width in enumerate(widths)]


def encode(fields, bits):
    code = jnp.int32(0)
    for field, (shift, _) in zip(fields, bits):
        code = code + lax.shift_left(field, jnp.int32(shift))
    return code


def decode(code, bits):
    return [
        lax.bitwise_and(lax.shift_right_logical(code, jnp.int32(shift)), jnp.int32(mask))
        for shift, mask in bits
    ]


def prepare_kernel(
    tiles_per_owner,
    bits,
    place_ref,
    src_ref,
    count_ref,
    tile_ref,
    turned_ref,
    weight_ref,
    list_ref,
    held_ref,
    staged_ref,
    sum_ref,
    in_sems,
    out_sems,
):
    tile_max, tile_size, _ = tile_ref.shape
    dest_count = count_ref.shape[1]
    zero_tile = place_ref[2]
    my_row = place_ref[0]
    pieces = in_sems.shape[0]
    piece = tile_max // pieces
    spans = [pl.ds(index * piece, piece) for index in range(pieces)]
    copies_in = [
        pltpu.make_async_copy(tile_ref.at[span], held_ref.at[span], in_sems.at[index])
        for index, span in enumerate(spans)
    ]
    copies_out = [
        pltpu.make_async_copy(staged_ref.at[span], turned_ref.at[span], out_sems.at[index])
        for index, span in enumerate(spans)
    ]
    for copy in copies_in:
        copy.start()

    rows_each = (list_ref.shape[0] - 2) // 2

    for half in range(2):

        def put(at, fields, half=half):
            row = lax.div(at, UNROLL)
            list_ref[half * rows_each + row, at - row * UNROLL] = encode(fields, bits)

        def one_dest(dest, carry, half=half, put=put):
            start, used, _ = carry
            owner = lax.div(dest, tiles_per_owner)
            relative = lax.bitwise_xor(owner, my_row)
            count = count_ref[0, dest]
            mine = lax.bitwise_and(relative, 1) == half
            pairs = jnp.where(mine, lax.div(count + 1, 2), 0)
            chip = lax.div(relative, 2)
            target = chip * tiles_per_owner + dest - owner * tiles_per_owner

            def one_pair(pair, carry):
                slot = start + 2 * pair
                next_slot = jnp.minimum(slot + 1, tile_max - 1)
                second = jnp.where(2 * pair + 1 < count, src_ref[0, next_slot], zero_tile)
                go_on = jnp.where(pair > 0, 1, 0)
                put(used + pair, (slot, src_ref[0, slot], second, target, go_on))
                return carry

            lax.fori_loop(0, pairs, one_pair, 0)
            return start + count, used + pairs, jnp.where(mine, target, carry[2])

        zero = jnp.int32(0)
        _, used, last = lax.fori_loop(0, dest_count, one_dest, (zero, zero, zero))
        turns = lax.div(used + UNROLL - 1, UNROLL)

        def one_pad(at, carry, put=put, last=last):
            put(at, (jnp.int32(0), zero_tile, zero_tile, last, jnp.int32(1)))
            return carry

        lax.fori_loop(used, turns * UNROLL, one_pad, 0)
        for column in range(UNROLL):
            list_ref[2 * rows_each + half, column] = turns

    group = min(8, piece)
    for index in range(pieces):
        copies_in[index].wait()

        def one_group(at, carry, index=index):
            for step in range(group):
                slot = index * piece + at * group + step
                tile = held_ref[slot]
                staged_ref[slot] = tile.T
                sum_ref[pl.ds(slot, 1), :] = jnp.sum(
                    tile.astype(jnp.float32), axis=0, keepdims=True
                )
            return carry

        lax.fori_loop(0, piece // group, one_group, 0)
        copies_out[index].start()

    sum_ref[tile_max:, :] = jnp.zeros((MOST, tile_size), jnp.float32)
    weight_ref[...] = jnp.zeros(weight_ref.shape, weight_ref.dtype)
    places = lax.broadcasted_iota(jnp.int32, (MOST, tile_size), 0)

    def weigh(owner, start):
        relative = lax.bitwise_xor(owner, my_row)
        chip = lax.div(relative, 2)
        for step in range(tiles_per_owner):
            count = count_ref[0, owner * tiles_per_owner + step]
            sums = jnp.where(places < count, sum_ref[pl.ds(start, MOST), :], 0.0)
            weight_ref[lax.bitwise_and(relative, 1), chip, step : step + 1, :] = jnp.sum(
                sums, axis=0, keepdims=True
            )
            start = start + count
        return start

    lax.fori_loop(0, dest_count // tiles_per_owner, weigh, jnp.int32(0))
    for copy in copies_out:
        copy.wait()


def prepare(place, tile_src, row_counts, tile_vals, row_size, tiles_per_owner, bits):
    tile_max, tile_size, _ = tile_vals.shape
    capacity = pair_capacity(tile_max, row_counts.shape[1])
    chips = row_size // 2
    return pl.pallas_call(
        functools.partial(prepare_kernel, tiles_per_owner, bits),
        out_shape=[
            jax.ShapeDtypeStruct(tile_vals.shape, tile_vals.dtype),
            jax.ShapeDtypeStruct((2, chips, EXTRA, tile_size), jnp.float32),
            jax.ShapeDtypeStruct((2 * (capacity // UNROLL) + 2, UNROLL), jnp.int32),
        ],
        in_specs=smem(3) + hbm(1),
        out_specs=hbm(1) + vmem(1) + smem(1),
        scratch_shapes=[
            pltpu.VMEM(tile_vals.shape, tile_vals.dtype),
            pltpu.VMEM(tile_vals.shape, tile_vals.dtype),
            pltpu.VMEM((tile_max + MOST, tile_size), jnp.float32),
            pltpu.SemaphoreType.DMA((8,)),
            pltpu.SemaphoreType.DMA((8,)),
        ],
        compiler_params=pltpu.CompilerParams(vmem_limit_bytes=24 * 2**20),
        name="prepare",
    )(place, tile_src, row_counts, tile_vals)


def assemble_kernel(packed, blocks, *refs):
    block_refs = refs[:blocks]
    held_ref = refs[blocks + 1]
    staged_ref = refs[-1] if packed else held_ref
    col = lax.axis_index("col")
    rows, width = block_refs[0].shape

    def put(mask, ref):
        first = pl.multiple_of(lax.bitwise_xor(col, mask) * rows, rows)
        staged_ref[pl.ds(first, rows), :] = ref[...]

    for mask in range(blocks):
        put(mask, block_refs[mask])
    if packed:
        piece = width // blocks
        for group in range(blocks):
            lanes = slice(group * piece, (group + 1) * piece)
            held_ref[group * rows : (group + 1) * rows, :] = jnp.concatenate(
                [staged_ref[b * rows : (b + 1) * rows, lanes] for b in range(blocks)], axis=1
            )
        own_ref = refs[blocks + 2]
        own_ref[...] = held_ref[pl.ds(pl.multiple_of(col * rows, rows), rows), :]
    zeros = held_ref.shape[0] - blocks * rows
    held_ref[blocks * rows :, :] = jnp.zeros((zeros, width), held_ref.dtype)


def assemble(gathered, after, tile_size, packed):
    blocks = len(gathered)
    rows, width = gathered[0].shape
    out_shape = [jax.ShapeDtypeStruct((blocks * rows + tile_size, width), jnp.bfloat16)]
    scratch = []
    if packed:
        out_shape.append(jax.ShapeDtypeStruct((rows, width), jnp.bfloat16))
        scratch.append(pltpu.VMEM((blocks * rows, width), jnp.bfloat16))
    return pl.pallas_call(
        functools.partial(assemble_kernel, packed, blocks),
        out_shape=out_shape,
        in_specs=vmem(blocks) + anywhere(1),
        out_specs=vmem(len(out_shape)),
        scratch_shapes=scratch,
        compiler_params=pltpu.CompilerParams(vmem_limit_bytes=4 * 2**20),
        cost_estimate=pl.CostEstimate(flops=0, bytes_accessed=4 * 2**20, transcendentals=0),
        name="assemble",
    )(*gathered, after)


def product_kernel(half, rows, bits, list_ref, turned_ref, held_ref, weight_ref, out_ref):
    tile_max, tile_size, _ = turned_ref.shape
    chips, out_rows, width = out_ref.shape
    rows_each = (list_ref.shape[0] - 2) // 2
    tiles = rows // tile_size
    if out_rows > rows:
        out_ref[:, rows:, :] = weight_ref[half].astype(out_ref.dtype)

    def codes_of(row):
        line = list_ref[pl.ds(row, 1), :]
        return tuple(line[0, step] for step in range(UNROLL))

    def one_turn(turn, carry):
        running, codes = carry
        later = codes_of(half * rows_each + turn + 1)
        for step in range(UNROLL):
            slot, first, second, target, go_on = decode(codes[step], bits)
            left = jnp.concatenate(
                [turned_ref[slot], turned_ref[jnp.minimum(slot + 1, tile_max - 1)]], axis=1
            )
            first = pl.multiple_of(first * tile_size, tile_size)
            second = pl.multiple_of(second * tile_size, tile_size)
            right = jnp.concatenate(
                [held_ref[pl.ds(first, tile_size), :], held_ref[pl.ds(second, tile_size), :]],
                axis=0,
            )
            term = jnp.dot(left, right, preferred_element_type=jnp.float32)
            running = running * go_on.astype(jnp.float32) + term
            chip = lax.div(target, tiles)
            row = pl.multiple_of((target - chip * tiles) * tile_size, tile_size)
            out_ref[chip, pl.ds(row, tile_size), :] = running.astype(out_ref.dtype)
        return running, later

    turns = list_ref[2 * rows_each + half : 2 * rows_each + half + 1, :][0, 0]
    zeros = jnp.zeros((tile_size, width), jnp.float32)
    lax.fori_loop(0, turns, one_turn, (zeros, codes_of(half * rows_each)))


def product(half, pairs, turned, held, weights, rows, chips, extra, bits):
    return pl.pallas_call(
        functools.partial(product_kernel, half, rows, bits),
        out_shape=jax.ShapeDtypeStruct((chips, rows + extra, held.shape[1]), jnp.bfloat16),
        in_specs=vmem(4),
        out_specs=vmem(1)[0],
        compiler_params=pltpu.CompilerParams(vmem_limit_bytes=4 * 2**20),
        cost_estimate=pl.CostEstimate(
            flops=600000000, bytes_accessed=6000000, transcendentals=0
        ),
        name="product",
    )(pairs, turned, held, weights)


def update_kernel(kept_ref, *refs):
    *arrived_refs, iterate_ref, restart_ref, scale_ref, out_ref = refs
    rows = out_ref.shape[0]
    summed = kept_ref[:rows, :]
    for ref in arrived_refs:
        summed = summed + ref[:rows, :].astype(jnp.float32)
    out_ref[...] = (
        scale_ref[...] * (summed + iterate_ref[...].astype(jnp.float32))
        + TELEPORT * restart_ref[...].astype(jnp.float32)
    ).astype(out_ref.dtype)


def update(kept, arrived, iterate, restart, scale):
    return pl.pallas_call(
        update_kernel,
        out_shape=jax.ShapeDtypeStruct(iterate.shape, iterate.dtype),
        in_specs=vmem(len(arrived) + 4),
        out_specs=vmem(1)[0],
        compiler_params=pltpu.CompilerParams(vmem_limit_bytes=4 * 2**20),
        cost_estimate=pl.CostEstimate(flops=0, bytes_accessed=1, transcendentals=0),
        name="update",
    )(kept, *arrived, iterate, restart, scale)


def exchange(block, axis, mask, size):
    return lax.ppermute(block, axis, [(i, i ^ mask) for i in range(size)])


def gather_line(block, size, masks):
    return {mask: exchange(block, "col", mask, size) for mask in masks}


def reduce_chips(both, cut, chip_bits, row_size):
    kept, arrived = [], []
    for half in range(2):
        state = both[:, :cut] if half == 0 else both[:, cut:]
        state = state.reshape((2,) * len(chip_bits) + state.shape[1:])
        left = list(chip_bits)
        turn = half % len(chip_bits)
        got = None
        for bit in chip_bits[turn:] + chip_bits[:turn]:
            if got is not None:
                state = state + got.astype(jnp.float32)
            axis = left.index(bit)
            send = lax.index_in_dim(state, 1, axis, keepdims=False).astype(jnp.bfloat16)
            state = lax.index_in_dim(state, 0, axis, keepdims=False)
            got = exchange(send, "row", 1 << bit, row_size)
            left.remove(bit)
        kept.append(state)
        arrived.append(got)
    return jnp.concatenate(kept), jnp.concatenate(arrived)


def on_device(features, tile_vals, tile_src, row_counts):
    row_size = lax.axis_size("row")
    blocks = lax.axis_size("col")
    my_row = lax.axis_index("row").astype(jnp.int32)
    my_col = lax.axis_index("col").astype(jnp.int32)
    tile_size = tile_vals.shape[1]
    dest_count = row_counts.shape[1]
    rows = features.shape[0] // blocks
    source_tiles = features.shape[0] // tile_size
    width = features.shape[1] * blocks // CHUNKS
    piece = features.shape[1] // CHUNKS
    tiles_per_owner = dest_count // row_size
    chips = row_size // 2
    chip_bits = list(range(row_size.bit_length() - 2, 0, -1))
    bits = code_bits(tile_vals.shape[0], source_tiles, dest_count // 2)
    place = jnp.stack([my_row, my_col, jnp.int32(source_tiles)])

    parts = features.reshape(blocks, rows, CHUNKS, piece).transpose(2, 1, 0, 3)
    parts = parts.reshape(CHUNKS, rows, blocks * piece)

    turned, weights, pairs = prepare(
        place, tile_src, row_counts, tile_vals, row_size, tiles_per_owner, bits
    )

    gathered = [{0: parts[0], **gather_line(parts[0], blocks, range(1, blocks))}, None]
    early = [mask for mask in range(1, blocks) if 2 * mask >= blocks]
    late = [mask for mask in range(1, blocks) if mask not in early]
    iterates = [None] * CHUNKS
    restarts = [None] * CHUNKS
    scale = None
    last = place
    for phase in range(ITERS * CHUNKS):
        chunk = phase % CHUNKS
        after = 1 - chunk
        first = phase < CHUNKS
        extra = EXTRA if phase == 0 else 0
        if phase > 0:
            iterates[after] = last = update(*pending)
        held, *own = assemble([gathered[chunk][m] for m in range(blocks)], last, tile_size, first)
        if first:
            iterates[chunk] = restarts[chunk] = own[0]
        if phase == 0:
            held, parts = lax.optimization_barrier((held, parts))
            coming = parts[1]
        elif phase + 1 < ITERS * CHUNKS:
            coming = iterates[after]
        else:
            coming = None
        if coming is not None:
            gathered[after] = {0: coming, **gather_line(coming, blocks, early)}
        sent = product(1, pairs, turned, held, weights, rows, chips, extra, bits)
        other = exchange(sent, "row", 1, row_size)
        kept = product(0, pairs, turned, held, weights, rows, chips, extra, bits)
        both = kept.astype(jnp.float32) + other.astype(jnp.float32)
        if coming is not None:
            coming, both = lax.optimization_barrier((coming, both))
            gathered[after].update(gather_line(coming, blocks, late))
        kept, arrived = reduce_chips(both, rows // 2, chip_bits, row_size)
        if phase == 0:
            weight_rows = slice(rows, rows + tiles_per_owner)
            total = 1.0 + kept[weight_rows] + arrived[weight_rows].astype(jnp.float32)
            scale = jnp.broadcast_to(
                ((1.0 - TELEPORT) / total).reshape(rows, 1), (rows, width)
            )
        pending = (kept, [arrived], iterates[chunk], restarts[chunk], scale)
    iterates[chunk] = update(*pending)
    out = jnp.stack(iterates).reshape(CHUNKS, rows, blocks, piece).transpose(1, 2, 0, 3)
    return out.reshape(rows, CHUNKS * width)


def solution(mesh):
    placed = (P("row", "col"), P("row", "col", None), P("row", "col"), P("row", "col"))
    return jax.shard_map(
        on_device, mesh=mesh, in_specs=placed, out_specs=P(("row", "col"), None), check_vma=False
    )
```

```python
import functools

import jax
import jax.numpy as jnp
from jax import lax
from jax.experimental import pallas as pl
from jax.experimental.pallas import tpu as pltpu
from jax.sharding import PartitionSpec as P

ITERS = 3


TELEPORT = 0.1


CHUNKS = 2


UNROLL = 8


EXTRA = 16


MOST = 8


def vmem(count):
    return [pl.BlockSpec(memory_space=pltpu.VMEM)] * count


def smem(count):
    return [pl.BlockSpec(memory_space=pltpu.SMEM)] * count


def anywhere(count):
    return [pl.BlockSpec(memory_space=pl.ANY)] * count


def hbm(count):
    return [pl.BlockSpec(memory_space=pltpu.HBM)] * count


def pair_capacity(tile_max, dest_count):
    most = (tile_max + dest_count // 2) // 2
    return -(-most // UNROLL) * UNROLL


def code_bits(tile_max, source_tiles, half_dests):
    sizes = (tile_max, source_tiles + 1, source_tiles + 1, half_dests, 2)
    widths = [(size - 1).bit_length() for size in sizes]
    assert sum(widths) < 32
    return [(sum(widths[at + 1 :]), (1 << width) - 1) for at, width in enumerate(widths)]


def encode(fields, bits):
    code = jnp.int32(0)
    for field, (shift, _) in zip(fields, bits):
        code = code + lax.shift_left(field, jnp.int32(shift))
    return code


def decode(code, bits):
    return [
        lax.bitwise_and(lax.shift_right_logical(code, jnp.int32(shift)), jnp.int32(mask))
        for shift, mask in bits
    ]


def prepare_kernel(
    tiles_per_owner,
    bits,
    place_ref,
    src_ref,
    count_ref,
    tile_ref,
    turned_ref,
    weight_ref,
    list_ref,
    held_ref,
    staged_ref,
    sum_ref,
    in_sems,
    out_sems,
):
    tile_max, tile_size, _ = tile_ref.shape
    dest_count = count_ref.shape[1]
    zero_tile = place_ref[2]
    my_row = place_ref[0]
    pieces = in_sems.shape[0]
    piece = tile_max // pieces
    spans = [pl.ds(index * piece, piece) for index in range(pieces)]
    copies_in = [
        pltpu.make_async_copy(tile_ref.at[span], held_ref.at[span], in_sems.at[index])
        for index, span in enumerate(spans)
    ]
    copies_out = [
        pltpu.make_async_copy(staged_ref.at[span], turned_ref.at[span], out_sems.at[index])
        for index, span in enumerate(spans)
    ]
    for copy in copies_in:
        copy.start()

    rows_each = (list_ref.shape[0] - 2) // 2

    for half in range(2):

        def put(at, fields, half=half):
            row = lax.div(at, UNROLL)
            list_ref[half * rows_each + row, at - row * UNROLL] = encode(fields, bits)

        def one_dest(dest, carry, half=half, put=put):
            start, used, _ = carry
            owner = lax.div(dest, tiles_per_owner)
            relative = lax.bitwise_xor(owner, my_row)
            count = count_ref[0, dest]
            mine = lax.bitwise_and(relative, 1) == half
            pairs = jnp.where(mine, lax.div(count + 1, 2), 0)
            chip = lax.div(relative, 2)
            target = chip * tiles_per_owner + dest - owner * tiles_per_owner

            def one_pair(pair, carry):
                slot = start + 2 * pair
                next_slot = jnp.minimum(slot + 1, tile_max - 1)
                second = jnp.where(2 * pair + 1 < count, src_ref[0, next_slot], zero_tile)
                go_on = jnp.where(pair > 0, 1, 0)
                put(used + pair, (slot, src_ref[0, slot], second, target, go_on))
                return carry

            lax.fori_loop(0, pairs, one_pair, 0)
            return start + count, used + pairs, jnp.where(mine, target, carry[2])

        zero = jnp.int32(0)
        _, used, last = lax.fori_loop(0, dest_count, one_dest, (zero, zero, zero))
        turns = lax.div(used + UNROLL - 1, UNROLL)

        def one_pad(at, carry, put=put, last=last):
            put(at, (jnp.int32(0), zero_tile, zero_tile, last, jnp.int32(1)))
            return carry

        lax.fori_loop(used, turns * UNROLL, one_pad, 0)
        for column in range(UNROLL):
            list_ref[2 * rows_each + half, column] = turns

    group = min(8, piece)
    for index in range(pieces):
        copies_in[index].wait()

        def one_group(at, carry, index=index):
            for step in range(group):
                slot = index * piece + at * group + step
                tile = held_ref[slot]
                staged_ref[slot] = tile.T
                sum_ref[pl.ds(slot, 1), :] = jnp.sum(
                    tile.astype(jnp.float32), axis=0, keepdims=True
                )
            return carry

        lax.fori_loop(0, piece // group, one_group, 0)
        copies_out[index].start()

    sum_ref[tile_max:, :] = jnp.zeros((MOST, tile_size), jnp.float32)
    weight_ref[...] = jnp.zeros(weight_ref.shape, weight_ref.dtype)
    places = lax.broadcasted_iota(jnp.int32, (MOST, tile_size), 0)

    def weigh(owner, start):
        relative = lax.bitwise_xor(owner, my_row)
        chip = lax.div(relative, 2)
        for step in range(tiles_per_owner):
            count = count_ref[0, owner * tiles_per_owner + step]
            sums = jnp.where(places < count, sum_ref[pl.ds(start, MOST), :], 0.0)
            weight_ref[lax.bitwise_and(relative, 1), chip, step : step + 1, :] = jnp.sum(
                sums, axis=0, keepdims=True
            )
            start = start + count
        return start

    lax.fori_loop(0, dest_count // tiles_per_owner, weigh, jnp.int32(0))
    for copy in copies_out:
        copy.wait()


def prepare(place, tile_src, row_counts, tile_vals, row_size, tiles_per_owner, bits):
    tile_max, tile_size, _ = tile_vals.shape
    capacity = pair_capacity(tile_max, row_counts.shape[1])
    chips = row_size // 2
    return pl.pallas_call(
        functools.partial(prepare_kernel, tiles_per_owner, bits),
        out_shape=[
            jax.ShapeDtypeStruct(tile_vals.shape, tile_vals.dtype),
            jax.ShapeDtypeStruct((2, chips, EXTRA, tile_size), jnp.float32),
            jax.ShapeDtypeStruct((2 * (capacity // UNROLL) + 2, UNROLL), jnp.int32),
        ],
        in_specs=smem(3) + hbm(1),
        out_specs=hbm(1) + vmem(1) + smem(1),
        scratch_shapes=[
            pltpu.VMEM(tile_vals.shape, tile_vals.dtype),
            pltpu.VMEM(tile_vals.shape, tile_vals.dtype),
            pltpu.VMEM((tile_max + MOST, tile_size), jnp.float32),
            pltpu.SemaphoreType.DMA((8,)),
            pltpu.SemaphoreType.DMA((8,)),
        ],
        compiler_params=pltpu.CompilerParams(
            vmem_limit_bytes=2 * tile_vals.size * tile_vals.dtype.itemsize + 2 * 2**20
        ),
        name="prepare",
    )(place, tile_src, row_counts, tile_vals)


def assemble_kernel(packed, blocks, *refs):
    block_refs = refs[:blocks]
    held_ref = refs[blocks + 1]
    staged_ref = refs[-1] if packed else held_ref
    col = lax.axis_index("col")
    rows, width = block_refs[0].shape

    def put(mask, ref):
        first = pl.multiple_of(lax.bitwise_xor(col, mask) * rows, rows)
        staged_ref[pl.ds(first, rows), :] = ref[...]

    for mask in range(blocks):
        put(mask, block_refs[mask])
    if packed:
        piece = width // blocks
        for group in range(blocks):
            lanes = slice(group * piece, (group + 1) * piece)
            held_ref[group * rows : (group + 1) * rows, :] = jnp.concatenate(
                [staged_ref[b * rows : (b + 1) * rows, lanes] for b in range(blocks)], axis=1
            )
        own_ref = refs[blocks + 2]
        own_ref[...] = held_ref[pl.ds(pl.multiple_of(col * rows, rows), rows), :]
    zeros = held_ref.shape[0] - blocks * rows
    held_ref[blocks * rows :, :] = jnp.zeros((zeros, width), held_ref.dtype)


def assemble(gathered, after, tile_size, packed):
    blocks = len(gathered)
    rows, width = gathered[0].shape
    out_shape = [jax.ShapeDtypeStruct((blocks * rows + tile_size, width), jnp.bfloat16)]
    scratch = []
    if packed:
        out_shape.append(jax.ShapeDtypeStruct((rows, width), jnp.bfloat16))
        scratch.append(pltpu.VMEM((blocks * rows, width), jnp.bfloat16))
    return pl.pallas_call(
        functools.partial(assemble_kernel, packed, blocks),
        out_shape=out_shape,
        in_specs=vmem(blocks) + anywhere(1),
        out_specs=vmem(len(out_shape)),
        scratch_shapes=scratch,
        compiler_params=pltpu.CompilerParams(vmem_limit_bytes=4 * 2**20),
        cost_estimate=pl.CostEstimate(flops=0, bytes_accessed=4 * 2**20, transcendentals=0),
        name="assemble",
    )(*gathered, after)


def product_kernel(half, rows, bits, list_ref, turned_ref, held_ref, weight_ref, out_ref):
    tile_max, tile_size, _ = turned_ref.shape
    chips, out_rows, width = out_ref.shape
    rows_each = (list_ref.shape[0] - 2) // 2
    tiles = rows // tile_size
    if out_rows > rows:
        out_ref[:, rows:, :] = weight_ref[half].astype(out_ref.dtype)

    def codes_of(row):
        line = list_ref[pl.ds(row, 1), :]
        return tuple(line[0, step] for step in range(UNROLL))

    def one_turn(turn, carry):
        running, codes = carry
        later = codes_of(half * rows_each + turn + 1)
        for step in range(UNROLL):
            slot, first, second, target, go_on = decode(codes[step], bits)
            left = jnp.concatenate(
                [turned_ref[slot], turned_ref[jnp.minimum(slot + 1, tile_max - 1)]], axis=1
            )
            first = pl.multiple_of(first * tile_size, tile_size)
            second = pl.multiple_of(second * tile_size, tile_size)
            right = jnp.concatenate(
                [held_ref[pl.ds(first, tile_size), :], held_ref[pl.ds(second, tile_size), :]],
                axis=0,
            )
            term = jnp.dot(left, right, preferred_element_type=jnp.float32)
            running = running * go_on.astype(jnp.float32) + term
            chip = lax.div(target, tiles)
            row = pl.multiple_of((target - chip * tiles) * tile_size, tile_size)
            out_ref[chip, pl.ds(row, tile_size), :] = running.astype(out_ref.dtype)
        return running, later

    turns = list_ref[2 * rows_each + half : 2 * rows_each + half + 1, :][0, 0]
    zeros = jnp.zeros((tile_size, width), jnp.float32)
    lax.fori_loop(0, turns, one_turn, (zeros, codes_of(half * rows_each)))


def product(half, pairs, turned, held, weights, rows, chips, extra, bits):
    return pl.pallas_call(
        functools.partial(product_kernel, half, rows, bits),
        out_shape=jax.ShapeDtypeStruct((chips, rows + extra, held.shape[1]), jnp.bfloat16),
        in_specs=vmem(4),
        out_specs=vmem(1)[0],
        compiler_params=pltpu.CompilerParams(vmem_limit_bytes=4 * 2**20),
        cost_estimate=pl.CostEstimate(
            flops=600000000, bytes_accessed=6000000, transcendentals=0
        ),
        name="product",
    )(pairs, turned, held, weights)


def update_kernel(kept_ref, *refs):
    *arrived_refs, iterate_ref, restart_ref, scale_ref, out_ref = refs
    rows = out_ref.shape[0]
    summed = kept_ref[:rows, :]
    for ref in arrived_refs:
        summed = summed + ref[:rows, :].astype(jnp.float32)
    out_ref[...] = (
        scale_ref[...] * (summed + iterate_ref[...].astype(jnp.float32))
        + TELEPORT * restart_ref[...].astype(jnp.float32)
    ).astype(out_ref.dtype)


def update(kept, arrived, iterate, restart, scale):
    return pl.pallas_call(
        update_kernel,
        out_shape=jax.ShapeDtypeStruct(iterate.shape, iterate.dtype),
        in_specs=vmem(len(arrived) + 4),
        out_specs=vmem(1)[0],
        compiler_params=pltpu.CompilerParams(vmem_limit_bytes=4 * 2**20),
        cost_estimate=pl.CostEstimate(flops=0, bytes_accessed=1, transcendentals=0),
        name="update",
    )(kept, *arrived, iterate, restart, scale)


def exchange(block, axis, mask, size):
    return lax.ppermute(block, axis, [(i, i ^ mask) for i in range(size)])


def gather_line(block, size, masks):
    return {mask: exchange(block, "col", mask, size) for mask in masks}


def reduce_chips(both, cut, chip_bits, row_size):
    kept, arrived = [], []
    for half in range(2):
        state = both[:, :cut] if half == 0 else both[:, cut:]
        state = state.reshape((2,) * len(chip_bits) + state.shape[1:])
        left = list(chip_bits)
        turn = half % len(chip_bits)
        got = None
        for bit in chip_bits[turn:] + chip_bits[:turn]:
            if got is not None:
                state = state + got.astype(jnp.float32)
            axis = left.index(bit)
            send = lax.index_in_dim(state, 1, axis, keepdims=False).astype(jnp.bfloat16)
            state = lax.index_in_dim(state, 0, axis, keepdims=False)
            got = exchange(send, "row", 1 << bit, row_size)
            left.remove(bit)
        kept.append(state)
        arrived.append(got)
    return jnp.concatenate(kept), jnp.concatenate(arrived)


def on_device(features, tile_vals, tile_src, row_counts):
    row_size = lax.axis_size("row")
    blocks = lax.axis_size("col")
    my_row = lax.axis_index("row").astype(jnp.int32)
    my_col = lax.axis_index("col").astype(jnp.int32)
    tile_size = tile_vals.shape[1]
    dest_count = row_counts.shape[1]
    rows = features.shape[0] // blocks
    source_tiles = features.shape[0] // tile_size
    width = features.shape[1] * blocks // CHUNKS
    piece = features.shape[1] // CHUNKS
    tiles_per_owner = dest_count // row_size
    chips = row_size // 2
    chip_bits = list(range(row_size.bit_length() - 2, 0, -1))
    bits = code_bits(tile_vals.shape[0], source_tiles, dest_count // 2)
    place = jnp.stack([my_row, my_col, jnp.int32(source_tiles)])

    parts = features.reshape(blocks, rows, CHUNKS, piece).transpose(2, 1, 0, 3)
    parts = parts.reshape(CHUNKS, rows, blocks * piece)

    turned, weights, pairs = prepare(
        place, tile_src, row_counts, tile_vals, row_size, tiles_per_owner, bits
    )

    gathered = [{0: parts[0], **gather_line(parts[0], blocks, range(1, blocks))}, None]
    early = [mask for mask in range(1, blocks) if 2 * mask >= blocks]
    late = [mask for mask in range(1, blocks) if mask not in early]
    iterates = [None] * CHUNKS
    restarts = [None] * CHUNKS
    scale = None
    last = place
    for phase in range(ITERS * CHUNKS):
        chunk = phase % CHUNKS
        after = 1 - chunk
        first = phase < CHUNKS
        extra = EXTRA if phase == 0 else 0
        if phase > 0:
            iterates[after] = last = update(*pending)
        held, *own = assemble([gathered[chunk][m] for m in range(blocks)], last, tile_size, first)
        if first:
            iterates[chunk] = restarts[chunk] = own[0]
        if phase == 0:
            held, parts = lax.optimization_barrier((held, parts))
            coming = parts[1]
        elif phase + 1 < ITERS * CHUNKS:
            coming = iterates[after]
        else:
            coming = None
        if coming is not None:
            gathered[after] = {0: coming, **gather_line(coming, blocks, early)}
        sent = product(1, pairs, turned, held, weights, rows, chips, extra, bits)
        other = exchange(sent, "row", 1, row_size)
        kept = product(0, pairs, turned, held, weights, rows, chips, extra, bits)
        both = kept.astype(jnp.float32) + other.astype(jnp.float32)
        if coming is not None:
            coming, both = lax.optimization_barrier((coming, both))
            gathered[after].update(gather_line(coming, blocks, late))
        kept, arrived = reduce_chips(both, rows // 2, chip_bits, row_size)
        if phase == 0:
            weight_rows = slice(rows, rows + tiles_per_owner)
            total = 1.0 + kept[weight_rows] + arrived[weight_rows].astype(jnp.float32)
            scale = jnp.broadcast_to(
                ((1.0 - TELEPORT) / total).reshape(rows, 1), (rows, width)
            )
        pending = (kept, [arrived], iterates[chunk], restarts[chunk], scale)
    iterates[chunk] = update(*pending)
    out = jnp.stack(iterates).reshape(CHUNKS, rows, blocks, piece).transpose(1, 2, 0, 3)
    return out.reshape(rows, CHUNKS * width)


def solution(mesh):
    placed = (P("row", "col"), P("row", "col", None), P("row", "col"), P("row", "col"))
    return jax.shard_map(
        on_device, mesh=mesh, in_specs=placed, out_specs=P(("row", "col"), None), check_vma=False
    )
```

```python
import functools

import jax
import jax.numpy as jnp
from jax import lax
from jax.experimental import pallas as pl
from jax.experimental.pallas import tpu as pltpu
from jax.sharding import PartitionSpec as P

ITERS = 3


TELEPORT = 0.1


CHUNKS = 2


UNROLL = 8


EXTRA = 16


MOST = 8


def vmem(count):
    return [pl.BlockSpec(memory_space=pltpu.VMEM)] * count


def smem(count):
    return [pl.BlockSpec(memory_space=pltpu.SMEM)] * count


def anywhere(count):
    return [pl.BlockSpec(memory_space=pl.ANY)] * count


def hbm(count):
    return [pl.BlockSpec(memory_space=pltpu.HBM)] * count


def pair_capacity(tile_max, dest_count):
    most = (tile_max + dest_count // 2) // 2
    return -(-most // UNROLL) * UNROLL


def code_bits(tile_max, source_tiles, half_dests):
    sizes = (tile_max, source_tiles + 1, source_tiles + 1, half_dests, 2)
    widths = [(size - 1).bit_length() for size in sizes]
    assert sum(widths) < 32
    return [(sum(widths[at + 1 :]), (1 << width) - 1) for at, width in enumerate(widths)]


def encode(fields, bits):
    code = jnp.int32(0)
    for field, (shift, _) in zip(fields, bits):
        code = code + lax.shift_left(field, jnp.int32(shift))
    return code


def decode(code, bits):
    return [
        lax.bitwise_and(lax.shift_right_logical(code, jnp.int32(shift)), jnp.int32(mask))
        for shift, mask in bits
    ]


def prepare_kernel(
    tiles_per_owner,
    bits,
    place_ref,
    src_ref,
    count_ref,
    tile_ref,
    turned_ref,
    weight_ref,
    list_ref,
    held_ref,
    sum_ref,
    in_sems,
):
    tile_max, tile_size, _ = tile_ref.shape
    dest_count = count_ref.shape[1]
    zero_tile = place_ref[2]
    my_row = place_ref[0]
    pieces = in_sems.shape[0]
    piece = tile_max // pieces
    spans = [pl.ds(index * piece, piece) for index in range(pieces)]
    copies_in = [
        pltpu.make_async_copy(tile_ref.at[span], held_ref.at[span], in_sems.at[index])
        for index, span in enumerate(spans)
    ]
    for copy in copies_in:
        copy.start()

    rows_each = (list_ref.shape[0] - 2) // 2

    for half in range(2):

        def put(at, fields, half=half):
            row = lax.div(at, UNROLL)
            list_ref[half * rows_each + row, at - row * UNROLL] = encode(fields, bits)

        def one_dest(dest, carry, half=half, put=put):
            start, used, _ = carry
            owner = lax.div(dest, tiles_per_owner)
            relative = lax.bitwise_xor(owner, my_row)
            count = count_ref[0, dest]
            mine = lax.bitwise_and(relative, 1) == half
            pairs = jnp.where(mine, lax.div(count + 1, 2), 0)
            chip = lax.div(relative, 2)
            target = chip * tiles_per_owner + dest - owner * tiles_per_owner

            def one_pair(pair, carry):
                slot = start + 2 * pair
                next_slot = jnp.minimum(slot + 1, tile_max - 1)
                second = jnp.where(2 * pair + 1 < count, src_ref[0, next_slot], zero_tile)
                go_on = jnp.where(pair > 0, 1, 0)
                put(used + pair, (slot, src_ref[0, slot], second, target, go_on))
                return carry

            lax.fori_loop(0, pairs, one_pair, 0)
            return start + count, used + pairs, jnp.where(mine, target, carry[2])

        zero = jnp.int32(0)
        _, used, last = lax.fori_loop(0, dest_count, one_dest, (zero, zero, zero))
        turns = lax.div(used + UNROLL - 1, UNROLL)

        def one_pad(at, carry, put=put, last=last):
            put(at, (jnp.int32(0), zero_tile, zero_tile, last, jnp.int32(1)))
            return carry

        lax.fori_loop(used, turns * UNROLL, one_pad, 0)
        for column in range(UNROLL):
            list_ref[2 * rows_each + half, column] = turns

    group = min(8, piece)
    for index in range(pieces):
        copies_in[index].wait()

        def one_group(at, carry, index=index):
            for step in range(group):
                slot = index * piece + at * group + step
                tile = held_ref[slot]
                turned_ref[slot] = tile.T
                sum_ref[pl.ds(slot, 1), :] = jnp.sum(
                    tile.astype(jnp.float32), axis=0, keepdims=True
                )
            return carry

        lax.fori_loop(0, piece // group, one_group, 0)

    sum_ref[tile_max:, :] = jnp.zeros((MOST, tile_size), jnp.float32)
    weight_ref[...] = jnp.zeros(weight_ref.shape, weight_ref.dtype)
    places = lax.broadcasted_iota(jnp.int32, (MOST, tile_size), 0)

    def weigh(owner, start):
        relative = lax.bitwise_xor(owner, my_row)
        chip = lax.div(relative, 2)
        for step in range(tiles_per_owner):
            count = count_ref[0, owner * tiles_per_owner + step]
            sums = jnp.where(places < count, sum_ref[pl.ds(start, MOST), :], 0.0)
            weight_ref[lax.bitwise_and(relative, 1), chip, step : step + 1, :] = jnp.sum(
                sums, axis=0, keepdims=True
            )
            start = start + count
        return start

    lax.fori_loop(0, dest_count // tiles_per_owner, weigh, jnp.int32(0))


def prepare(place, tile_src, row_counts, tile_vals, row_size, tiles_per_owner, bits):
    tile_max, tile_size, _ = tile_vals.shape
    capacity = pair_capacity(tile_max, row_counts.shape[1])
    chips = row_size // 2
    return pl.pallas_call(
        functools.partial(prepare_kernel, tiles_per_owner, bits),
        out_shape=[
            pltpu.VMEM(tile_vals.shape, tile_vals.dtype),
            jax.ShapeDtypeStruct((2, chips, EXTRA, tile_size), jnp.float32),
            jax.ShapeDtypeStruct((2 * (capacity // UNROLL) + 2, UNROLL), jnp.int32),
        ],
        in_specs=smem(3) + hbm(1),
        out_specs=vmem(2) + smem(1),
        scratch_shapes=[
            pltpu.VMEM(tile_vals.shape, tile_vals.dtype),
            pltpu.VMEM((tile_max + MOST, tile_size), jnp.float32),
            pltpu.SemaphoreType.DMA((8,)),
        ],
        compiler_params=pltpu.CompilerParams(vmem_limit_bytes=24 * 2**20),
        name="prepare",
    )(place, tile_src, row_counts, tile_vals)


def assemble_kernel(packed, blocks, *refs):
    block_refs = refs[:blocks]
    held_ref = refs[blocks + 1]
    staged_ref = refs[-1] if packed else held_ref
    col = lax.axis_index("col")
    rows, width = block_refs[0].shape

    def put(mask, ref):
        first = pl.multiple_of(lax.bitwise_xor(col, mask) * rows, rows)
        staged_ref[pl.ds(first, rows), :] = ref[...]

    for mask in range(blocks):
        put(mask, block_refs[mask])
    if packed:
        piece = width // blocks
        for group in range(blocks):
            lanes = slice(group * piece, (group + 1) * piece)
            held_ref[group * rows : (group + 1) * rows, :] = jnp.concatenate(
                [staged_ref[b * rows : (b + 1) * rows, lanes] for b in range(blocks)], axis=1
            )
        own_ref = refs[blocks + 2]
        own_ref[...] = held_ref[pl.ds(pl.multiple_of(col * rows, rows), rows), :]
    zeros = held_ref.shape[0] - blocks * rows
    held_ref[blocks * rows :, :] = jnp.zeros((zeros, width), held_ref.dtype)


def assemble(gathered, after, tile_size, packed):
    blocks = len(gathered)
    rows, width = gathered[0].shape
    out_shape = [jax.ShapeDtypeStruct((blocks * rows + tile_size, width), jnp.bfloat16)]
    scratch = []
    if packed:
        out_shape.append(jax.ShapeDtypeStruct((rows, width), jnp.bfloat16))
        scratch.append(pltpu.VMEM((blocks * rows, width), jnp.bfloat16))
    return pl.pallas_call(
        functools.partial(assemble_kernel, packed, blocks),
        out_shape=out_shape,
        in_specs=vmem(blocks) + anywhere(1),
        out_specs=vmem(len(out_shape)),
        scratch_shapes=scratch,
        compiler_params=pltpu.CompilerParams(vmem_limit_bytes=4 * 2**20),
        cost_estimate=pl.CostEstimate(flops=0, bytes_accessed=4 * 2**20, transcendentals=0),
        name="assemble",
    )(*gathered, after)


def product_kernel(
    half, rows, bits, list_ref, turned_ref, held_ref, weight_ref, out_ref, passed_ref
):
    tile_max, tile_size, _ = turned_ref.shape
    chips, out_rows, width = out_ref.shape
    rows_each = (list_ref.shape[0] - 2) // 2
    tiles = rows // tile_size
    if out_rows > rows:
        out_ref[:, rows:, :] = weight_ref[half].astype(out_ref.dtype)

    def codes_of(row):
        line = list_ref[pl.ds(row, 1), :]
        return tuple(line[0, step] for step in range(UNROLL))

    def one_turn(turn, carry):
        running, codes = carry
        later = codes_of(half * rows_each + turn + 1)
        for step in range(UNROLL):
            slot, first, second, target, go_on = decode(codes[step], bits)
            left = jnp.concatenate(
                [turned_ref[slot], turned_ref[jnp.minimum(slot + 1, tile_max - 1)]], axis=1
            )
            first = pl.multiple_of(first * tile_size, tile_size)
            second = pl.multiple_of(second * tile_size, tile_size)
            right = jnp.concatenate(
                [held_ref[pl.ds(first, tile_size), :], held_ref[pl.ds(second, tile_size), :]],
                axis=0,
            )
            term = jnp.dot(left, right, preferred_element_type=jnp.float32)
            running = running * go_on.astype(jnp.float32) + term
            chip = lax.div(target, tiles)
            row = pl.multiple_of((target - chip * tiles) * tile_size, tile_size)
            out_ref[chip, pl.ds(row, tile_size), :] = running.astype(out_ref.dtype)
        return running, later

    turns = list_ref[2 * rows_each + half : 2 * rows_each + half + 1, :][0, 0]
    zeros = jnp.zeros((tile_size, width), jnp.float32)
    lax.fori_loop(0, turns, one_turn, (zeros, codes_of(half * rows_each)))


def product(half, pairs, turned, held, weights, rows, chips, extra, bits):
    return pl.pallas_call(
        functools.partial(product_kernel, half, rows, bits),
        out_shape=[
            jax.ShapeDtypeStruct((chips, rows + extra, held.shape[1]), jnp.bfloat16),
            jax.ShapeDtypeStruct(turned.shape, turned.dtype),
        ],
        in_specs=vmem(4),
        out_specs=vmem(2),
        input_output_aliases={1: 1},
        compiler_params=pltpu.CompilerParams(vmem_limit_bytes=4 * 2**20),
        cost_estimate=pl.CostEstimate(
            flops=600000000, bytes_accessed=6000000, transcendentals=0
        ),
        name="product",
    )(pairs, turned, held, weights)


def update_kernel(kept_ref, *refs):
    *arrived_refs, iterate_ref, restart_ref, scale_ref, out_ref = refs
    rows = out_ref.shape[0]
    summed = kept_ref[:rows, :]
    for ref in arrived_refs:
        summed = summed + ref[:rows, :].astype(jnp.float32)
    out_ref[...] = (
        scale_ref[...] * (summed + iterate_ref[...].astype(jnp.float32))
        + TELEPORT * restart_ref[...].astype(jnp.float32)
    ).astype(out_ref.dtype)


def update(kept, arrived, iterate, restart, scale):
    return pl.pallas_call(
        update_kernel,
        out_shape=jax.ShapeDtypeStruct(iterate.shape, iterate.dtype),
        in_specs=vmem(len(arrived) + 4),
        out_specs=vmem(1)[0],
        compiler_params=pltpu.CompilerParams(vmem_limit_bytes=4 * 2**20),
        cost_estimate=pl.CostEstimate(flops=0, bytes_accessed=1, transcendentals=0),
        name="update",
    )(kept, *arrived, iterate, restart, scale)


def exchange(block, axis, mask, size):
    return lax.ppermute(block, axis, [(i, i ^ mask) for i in range(size)])


def gather_line(block, size, masks):
    return {mask: exchange(block, "col", mask, size) for mask in masks}


def reduce_chips(both, cut, chip_bits, row_size):
    kept, arrived = [], []
    for half in range(2):
        state = both[:, :cut] if half == 0 else both[:, cut:]
        state = state.reshape((2,) * len(chip_bits) + state.shape[1:])
        left = list(chip_bits)
        turn = half % len(chip_bits)
        got = None
        for bit in chip_bits[turn:] + chip_bits[:turn]:
            if got is not None:
                state = state + got.astype(jnp.float32)
            axis = left.index(bit)
            send = lax.index_in_dim(state, 1, axis, keepdims=False).astype(jnp.bfloat16)
            state = lax.index_in_dim(state, 0, axis, keepdims=False)
            got = exchange(send, "row", 1 << bit, row_size)
            left.remove(bit)
        kept.append(state)
        arrived.append(got)
    return jnp.concatenate(kept), jnp.concatenate(arrived)


def on_device(features, tile_vals, tile_src, row_counts):
    row_size = lax.axis_size("row")
    blocks = lax.axis_size("col")
    my_row = lax.axis_index("row").astype(jnp.int32)
    my_col = lax.axis_index("col").astype(jnp.int32)
    tile_size = tile_vals.shape[1]
    dest_count = row_counts.shape[1]
    rows = features.shape[0] // blocks
    source_tiles = features.shape[0] // tile_size
    width = features.shape[1] * blocks // CHUNKS
    piece = features.shape[1] // CHUNKS
    tiles_per_owner = dest_count // row_size
    chips = row_size // 2
    chip_bits = list(range(row_size.bit_length() - 2, 0, -1))
    bits = code_bits(tile_vals.shape[0], source_tiles, dest_count // 2)
    place = jnp.stack([my_row, my_col, jnp.int32(source_tiles)])

    parts = features.reshape(blocks, rows, CHUNKS, piece).transpose(2, 1, 0, 3)
    parts = parts.reshape(CHUNKS, rows, blocks * piece)

    turned, weights, pairs = prepare(
        place, tile_src, row_counts, tile_vals, row_size, tiles_per_owner, bits
    )

    gathered = [{0: parts[0], **gather_line(parts[0], blocks, range(1, blocks))}, None]
    early = [mask for mask in range(1, blocks) if 2 * mask >= blocks]
    late = [mask for mask in range(1, blocks) if mask not in early]
    iterates = [None] * CHUNKS
    restarts = [None] * CHUNKS
    scale = None
    last = place
    for phase in range(ITERS * CHUNKS):
        chunk = phase % CHUNKS
        after = 1 - chunk
        first = phase < CHUNKS
        extra = EXTRA if phase == 0 else 0
        if phase > 0:
            iterates[after] = last = update(*pending)
        held, *own = assemble([gathered[chunk][m] for m in range(blocks)], last, tile_size, first)
        if first:
            iterates[chunk] = restarts[chunk] = own[0]
        if phase == 0:
            held, parts = lax.optimization_barrier((held, parts))
            coming = parts[1]
        elif phase + 1 < ITERS * CHUNKS:
            coming = iterates[after]
        else:
            coming = None
        if coming is not None:
            gathered[after] = {0: coming, **gather_line(coming, blocks, early)}
        sent, turned = product(1, pairs, turned, held, weights, rows, chips, extra, bits)
        other = exchange(sent, "row", 1, row_size)
        kept, turned = product(0, pairs, turned, held, weights, rows, chips, extra, bits)
        both = kept.astype(jnp.float32) + other.astype(jnp.float32)
        if coming is not None:
            coming, both = lax.optimization_barrier((coming, both))
            gathered[after].update(gather_line(coming, blocks, late))
        kept, arrived = reduce_chips(both, rows // 2, chip_bits, row_size)
        if phase == 0:
            weight_rows = slice(rows, rows + tiles_per_owner)
            total = 1.0 + kept[weight_rows] + arrived[weight_rows].astype(jnp.float32)
            scale = jnp.broadcast_to(
                ((1.0 - TELEPORT) / total).reshape(rows, 1), (rows, width)
            )
        pending = (kept, [arrived], iterates[chunk], restarts[chunk], scale)
    iterates[chunk] = update(*pending)
    out = jnp.stack(iterates).reshape(CHUNKS, rows, blocks, piece).transpose(1, 2, 0, 3)
    return out.reshape(rows, CHUNKS * width)


def solution(mesh):
    placed = (P("row", "col"), P("row", "col", None), P("row", "col"), P("row", "col"))
    return jax.shard_map(
        on_device, mesh=mesh, in_specs=placed, out_specs=P(("row", "col"), None), check_vma=False
    )
```

```python
import functools

import jax
import jax.numpy as jnp
from jax import lax
from jax.experimental import pallas as pl
from jax.experimental.pallas import tpu as pltpu
from jax.sharding import PartitionSpec as P

ITERS = 3


TELEPORT = 0.1


CHUNKS = 2


UNROLL = 8


EXTRA = 16


MOST = 8


def vmem(count):
    return [pl.BlockSpec(memory_space=pltpu.VMEM)] * count


def smem(count):
    return [pl.BlockSpec(memory_space=pltpu.SMEM)] * count


def anywhere(count):
    return [pl.BlockSpec(memory_space=pl.ANY)] * count


def hbm(count):
    return [pl.BlockSpec(memory_space=pltpu.HBM)] * count


def pair_capacity(tile_max, dest_count):
    most = (tile_max + dest_count // 2) // 2
    return -(-most // UNROLL) * UNROLL


def code_bits(tile_max, source_tiles, half_dests):
    sizes = (tile_max, source_tiles + 1, source_tiles + 1, half_dests, 2)
    widths = [(size - 1).bit_length() for size in sizes]
    assert sum(widths) < 32
    return [(sum(widths[at + 1 :]), (1 << width) - 1) for at, width in enumerate(widths)]


def encode(fields, bits):
    code = jnp.int32(0)
    for field, (shift, _) in zip(fields, bits):
        code = code + lax.shift_left(field, jnp.int32(shift))
    return code


def decode(code, bits):
    return [
        lax.bitwise_and(lax.shift_right_logical(code, jnp.int32(shift)), jnp.int32(mask))
        for shift, mask in bits
    ]


def prepare_kernel(
    tiles_per_owner,
    bits,
    place_ref,
    src_ref,
    count_ref,
    tile_ref,
    turned_ref,
    weight_ref,
    list_ref,
    held_ref,
    staged_ref,
    sum_ref,
    in_sems,
    out_sems,
):
    tile_max, tile_size, _ = tile_ref.shape
    dest_count = count_ref.shape[1]
    zero_tile = place_ref[2]
    my_row = place_ref[0]
    pieces = in_sems.shape[0]
    piece = tile_max // pieces
    spans = [pl.ds(index * piece, piece) for index in range(pieces)]
    copies_in = [
        pltpu.make_async_copy(tile_ref.at[span], held_ref.at[span], in_sems.at[index])
        for index, span in enumerate(spans)
    ]
    copies_out = [
        pltpu.make_async_copy(staged_ref.at[span], turned_ref.at[span], out_sems.at[index])
        for index, span in enumerate(spans)
    ]
    for copy in copies_in:
        copy.start()

    rows_each = (list_ref.shape[0] - 2) // 2

    for half in range(2):

        def put(at, fields, half=half):
            row = lax.div(at, UNROLL)
            list_ref[half * rows_each + row, at - row * UNROLL] = encode(fields, bits)

        def one_dest(dest, carry, half=half, put=put):
            start, used, _ = carry
            owner = lax.div(dest, tiles_per_owner)
            relative = lax.bitwise_xor(owner, my_row)
            count = count_ref[0, dest]
            mine = lax.bitwise_and(relative, 1) == half
            pairs = jnp.where(mine, lax.div(count + 1, 2), 0)
            chip = lax.div(relative, 2)
            target = chip * tiles_per_owner + dest - owner * tiles_per_owner

            def one_pair(pair, carry):
                slot = start + 2 * pair
                next_slot = jnp.minimum(slot + 1, tile_max - 1)
                second = jnp.where(2 * pair + 1 < count, src_ref[0, next_slot], zero_tile)
                go_on = jnp.where(pair > 0, 1, 0)
                put(used + pair, (slot, src_ref[0, slot], second, target, go_on))
                return carry

            lax.fori_loop(0, pairs, one_pair, 0)
            return start + count, used + pairs, jnp.where(mine, target, carry[2])

        zero = jnp.int32(0)
        _, used, last = lax.fori_loop(0, dest_count, one_dest, (zero, zero, zero))
        turns = lax.div(used + UNROLL - 1, UNROLL)

        def one_pad(at, carry, put=put, last=last):
            put(at, (jnp.int32(0), zero_tile, zero_tile, last, jnp.int32(1)))
            return carry

        lax.fori_loop(used, turns * UNROLL, one_pad, 0)
        for column in range(UNROLL):
            list_ref[2 * rows_each + half, column] = turns

    group = min(8, piece)
    for index in range(pieces):
        copies_in[index].wait()

        def one_group(at, carry, index=index):
            for step in range(group):
                slot = index * piece + at * group + step
                tile = held_ref[slot]
                staged_ref[slot] = tile.T
                sum_ref[pl.ds(slot, 1), :] = jnp.sum(
                    tile.astype(jnp.float32), axis=0, keepdims=True
                )
            return carry

        lax.fori_loop(0, piece // group, one_group, 0)
        copies_out[index].start()

    sum_ref[tile_max:, :] = jnp.zeros((MOST, tile_size), jnp.float32)
    weight_ref[...] = jnp.zeros(weight_ref.shape, weight_ref.dtype)
    places = lax.broadcasted_iota(jnp.int32, (MOST, tile_size), 0)

    def weigh(owner, start):
        relative = lax.bitwise_xor(owner, my_row)
        chip = lax.div(relative, 2)
        for step in range(tiles_per_owner):
            count = count_ref[0, owner * tiles_per_owner + step]
            sums = jnp.where(places < count, sum_ref[pl.ds(start, MOST), :], 0.0)
            weight_ref[lax.bitwise_and(relative, 1), chip, step : step + 1, :] = jnp.sum(
                sums, axis=0, keepdims=True
            )
            start = start + count
        return start

    lax.fori_loop(0, dest_count // tiles_per_owner, weigh, jnp.int32(0))
    for copy in copies_out:
        copy.wait()


def prepare(place, tile_src, row_counts, tile_vals, row_size, tiles_per_owner, bits):
    tile_max, tile_size, _ = tile_vals.shape
    capacity = pair_capacity(tile_max, row_counts.shape[1])
    chips = row_size // 2
    return pl.pallas_call(
        functools.partial(prepare_kernel, tiles_per_owner, bits),
        out_shape=[
            jax.ShapeDtypeStruct(tile_vals.shape, tile_vals.dtype),
            jax.ShapeDtypeStruct((2, chips, EXTRA, tile_size), jnp.float32),
            jax.ShapeDtypeStruct((2 * (capacity // UNROLL) + 2, UNROLL), jnp.int32),
        ],
        in_specs=smem(3) + hbm(1),
        out_specs=hbm(1) + vmem(1) + smem(1),
        scratch_shapes=[
            pltpu.VMEM(tile_vals.shape, tile_vals.dtype),
            pltpu.VMEM(tile_vals.shape, tile_vals.dtype),
            pltpu.VMEM((tile_max + MOST, tile_size), jnp.float32),
            pltpu.SemaphoreType.DMA((8,)),
            pltpu.SemaphoreType.DMA((8,)),
        ],
        compiler_params=pltpu.CompilerParams(vmem_limit_bytes=24 * 2**20),
        name="prepare",
    )(place, tile_src, row_counts, tile_vals)


def pack_kernel(blocks, features_ref, *part_refs):
    rows = features_ref.shape[0] // blocks
    piece = features_ref.shape[1] // len(part_refs)
    for chunk, part_ref in enumerate(part_refs):
        lanes = slice(chunk * piece, (chunk + 1) * piece)
        part_ref[...] = jnp.concatenate(
            [features_ref[b * rows : (b + 1) * rows, lanes] for b in range(blocks)], axis=1
        )


def pack(features, blocks):
    rows = features.shape[0] // blocks
    width = features.shape[1] // CHUNKS * blocks
    return pl.pallas_call(
        functools.partial(pack_kernel, blocks),
        out_shape=[jax.ShapeDtypeStruct((rows, width), features.dtype)] * CHUNKS,
        in_specs=vmem(1),
        out_specs=vmem(CHUNKS),
        compiler_params=pltpu.CompilerParams(vmem_limit_bytes=4 * 2**20),
        name="pack",
    )(features)


def assemble_kernel(packed, blocks, *refs):
    block_refs = refs[:blocks]
    held_ref = refs[blocks + 1]
    staged_ref = refs[-1] if packed else held_ref
    col = lax.axis_index("col")
    rows, width = block_refs[0].shape

    def put(mask, ref):
        first = pl.multiple_of(lax.bitwise_xor(col, mask) * rows, rows)
        staged_ref[pl.ds(first, rows), :] = ref[...]

    for mask in range(blocks):
        put(mask, block_refs[mask])
    if packed:
        piece = width // blocks
        for group in range(blocks):
            lanes = slice(group * piece, (group + 1) * piece)
            held_ref[group * rows : (group + 1) * rows, :] = jnp.concatenate(
                [staged_ref[b * rows : (b + 1) * rows, lanes] for b in range(blocks)], axis=1
            )
        own_ref = refs[blocks + 2]
        own_ref[...] = held_ref[pl.ds(pl.multiple_of(col * rows, rows), rows), :]
    zeros = held_ref.shape[0] - blocks * rows
    held_ref[blocks * rows :, :] = jnp.zeros((zeros, width), held_ref.dtype)


def assemble(gathered, after, tile_size, packed):
    blocks = len(gathered)
    rows, width = gathered[0].shape
    out_shape = [jax.ShapeDtypeStruct((blocks * rows + tile_size, width), jnp.bfloat16)]
    scratch = []
    if packed:
        out_shape.append(jax.ShapeDtypeStruct((rows, width), jnp.bfloat16))
        scratch.append(pltpu.VMEM((blocks * rows, width), jnp.bfloat16))
    return pl.pallas_call(
        functools.partial(assemble_kernel, packed, blocks),
        out_shape=out_shape,
        in_specs=vmem(blocks) + anywhere(1),
        out_specs=vmem(len(out_shape)),
        scratch_shapes=scratch,
        compiler_params=pltpu.CompilerParams(vmem_limit_bytes=4 * 2**20),
        cost_estimate=pl.CostEstimate(flops=0, bytes_accessed=4 * 2**20, transcendentals=0),
        name="assemble",
    )(*gathered, after)


def product_kernel(half, rows, bits, list_ref, turned_ref, held_ref, weight_ref, out_ref):
    tile_max, tile_size, _ = turned_ref.shape
    chips, out_rows, width = out_ref.shape
    rows_each = (list_ref.shape[0] - 2) // 2
    tiles = rows // tile_size
    if out_rows > rows:
        out_ref[:, rows:, :] = weight_ref[half].astype(out_ref.dtype)

    def codes_of(row):
        line = list_ref[pl.ds(row, 1), :]
        return tuple(line[0, step] for step in range(UNROLL))

    def one_turn(turn, carry):
        running, codes = carry
        later = codes_of(half * rows_each + turn + 1)
        for step in range(UNROLL):
            slot, first, second, target, go_on = decode(codes[step], bits)
            left = jnp.concatenate(
                [turned_ref[slot], turned_ref[jnp.minimum(slot + 1, tile_max - 1)]], axis=1
            )
            first = pl.multiple_of(first * tile_size, tile_size)
            second = pl.multiple_of(second * tile_size, tile_size)
            right = jnp.concatenate(
                [held_ref[pl.ds(first, tile_size), :], held_ref[pl.ds(second, tile_size), :]],
                axis=0,
            )
            term = jnp.dot(left, right, preferred_element_type=jnp.float32)
            running = running * go_on.astype(jnp.float32) + term
            chip = lax.div(target, tiles)
            row = pl.multiple_of((target - chip * tiles) * tile_size, tile_size)
            out_ref[chip, pl.ds(row, tile_size), :] = running.astype(out_ref.dtype)
        return running, later

    turns = list_ref[2 * rows_each + half : 2 * rows_each + half + 1, :][0, 0]
    zeros = jnp.zeros((tile_size, width), jnp.float32)
    lax.fori_loop(0, turns, one_turn, (zeros, codes_of(half * rows_each)))


def product(half, pairs, turned, held, weights, rows, chips, extra, bits):
    return pl.pallas_call(
        functools.partial(product_kernel, half, rows, bits),
        out_shape=jax.ShapeDtypeStruct((chips, rows + extra, held.shape[1]), jnp.bfloat16),
        in_specs=vmem(4),
        out_specs=vmem(1)[0],
        compiler_params=pltpu.CompilerParams(vmem_limit_bytes=4 * 2**20),
        cost_estimate=pl.CostEstimate(
            flops=600000000, bytes_accessed=6000000, transcendentals=0
        ),
        name="product",
    )(pairs, turned, held, weights)


def update_kernel(kept_ref, *refs):
    *arrived_refs, iterate_ref, restart_ref, scale_ref, out_ref = refs
    rows = out_ref.shape[0]
    summed = kept_ref[:rows, :]
    for ref in arrived_refs:
        summed = summed + ref[:rows, :].astype(jnp.float32)
    out_ref[...] = (
        scale_ref[...] * (summed + iterate_ref[...].astype(jnp.float32))
        + TELEPORT * restart_ref[...].astype(jnp.float32)
    ).astype(out_ref.dtype)


def update(kept, arrived, iterate, restart, scale):
    return pl.pallas_call(
        update_kernel,
        out_shape=jax.ShapeDtypeStruct(iterate.shape, iterate.dtype),
        in_specs=vmem(len(arrived) + 4),
        out_specs=vmem(1)[0],
        compiler_params=pltpu.CompilerParams(vmem_limit_bytes=4 * 2**20),
        cost_estimate=pl.CostEstimate(flops=0, bytes_accessed=1, transcendentals=0),
        name="update",
    )(kept, *arrived, iterate, restart, scale)


def exchange(block, axis, mask, size):
    return lax.ppermute(block, axis, [(i, i ^ mask) for i in range(size)])


def gather_line(block, size, masks):
    return {mask: exchange(block, "col", mask, size) for mask in masks}


def reduce_chips(both, cut, chip_bits, row_size):
    kept, arrived = [], []
    for half in range(2):
        state = both[:, :cut] if half == 0 else both[:, cut:]
        state = state.reshape((2,) * len(chip_bits) + state.shape[1:])
        left = list(chip_bits)
        turn = half % len(chip_bits)
        got = None
        for bit in chip_bits[turn:] + chip_bits[:turn]:
            if got is not None:
                state = state + got.astype(jnp.float32)
            axis = left.index(bit)
            send = lax.index_in_dim(state, 1, axis, keepdims=False).astype(jnp.bfloat16)
            state = lax.index_in_dim(state, 0, axis, keepdims=False)
            got = exchange(send, "row", 1 << bit, row_size)
            left.remove(bit)
        kept.append(state)
        arrived.append(got)
    return jnp.concatenate(kept), jnp.concatenate(arrived)


def on_device(features, tile_vals, tile_src, row_counts):
    row_size = lax.axis_size("row")
    blocks = lax.axis_size("col")
    my_row = lax.axis_index("row").astype(jnp.int32)
    my_col = lax.axis_index("col").astype(jnp.int32)
    tile_size = tile_vals.shape[1]
    dest_count = row_counts.shape[1]
    rows = features.shape[0] // blocks
    source_tiles = features.shape[0] // tile_size
    width = features.shape[1] * blocks // CHUNKS
    piece = features.shape[1] // CHUNKS
    tiles_per_owner = dest_count // row_size
    chips = row_size // 2
    chip_bits = list(range(row_size.bit_length() - 2, 0, -1))
    bits = code_bits(tile_vals.shape[0], source_tiles, dest_count // 2)
    place = jnp.stack([my_row, my_col, jnp.int32(source_tiles)])

    parts = pack(features, blocks)

    turned, weights, pairs = prepare(
        place, tile_src, row_counts, tile_vals, row_size, tiles_per_owner, bits
    )

    gathered = [{0: parts[0], **gather_line(parts[0], blocks, range(1, blocks))}, None]
    early = [mask for mask in range(1, blocks) if 2 * mask >= blocks]
    late = [mask for mask in range(1, blocks) if mask not in early]
    iterates = [None] * CHUNKS
    restarts = [None] * CHUNKS
    scale = None
    last = place
    for phase in range(ITERS * CHUNKS):
        chunk = phase % CHUNKS
        after = 1 - chunk
        first = phase < CHUNKS
        extra = EXTRA if phase == 0 else 0
        if phase > 0:
            iterates[after] = last = update(*pending)
        held, *own = assemble([gathered[chunk][m] for m in range(blocks)], last, tile_size, first)
        if first:
            iterates[chunk] = restarts[chunk] = own[0]
        if phase == 0:
            held, coming = lax.optimization_barrier((held, parts[1]))
        elif phase + 1 < ITERS * CHUNKS:
            coming = iterates[after]
        else:
            coming = None
        if coming is not None:
            gathered[after] = {0: coming, **gather_line(coming, blocks, early)}
        sent = product(1, pairs, turned, held, weights, rows, chips, extra, bits)
        other = exchange(sent, "row", 1, row_size)
        kept = product(0, pairs, turned, held, weights, rows, chips, extra, bits)
        both = kept.astype(jnp.float32) + other.astype(jnp.float32)
        if coming is not None:
            coming, both = lax.optimization_barrier((coming, both))
            gathered[after].update(gather_line(coming, blocks, late))
        kept, arrived = reduce_chips(both, rows // 2, chip_bits, row_size)
        if phase == 0:
            weight_rows = slice(rows, rows + tiles_per_owner)
            total = 1.0 + kept[weight_rows] + arrived[weight_rows].astype(jnp.float32)
            scale = jnp.broadcast_to(
                ((1.0 - TELEPORT) / total).reshape(rows, 1), (rows, width)
            )
        pending = (kept, [arrived], iterates[chunk], restarts[chunk], scale)
    iterates[chunk] = update(*pending)
    iterates = lax.optimization_barrier(iterates)
    out = jnp.stack(iterates).reshape(CHUNKS, rows, blocks, piece).transpose(1, 2, 0, 3)
    return out.reshape(rows, CHUNKS * width)


def solution(mesh):
    placed = (P("row", "col"), P("row", "col", None), P("row", "col"), P("row", "col"))
    return jax.shard_map(
        on_device, mesh=mesh, in_specs=placed, out_specs=P(("row", "col"), None), check_vma=False
    )
```

```python
import functools

import jax
import jax.numpy as jnp
from jax import lax
from jax.experimental import pallas as pl
from jax.experimental.pallas import tpu as pltpu
from jax.sharding import PartitionSpec as P

ITERS = 3


TELEPORT = 0.1


CHUNKS = 2


UNROLL = 8


EXTRA = 16


MOST = 8


def vmem(count):
    return [pl.BlockSpec(memory_space=pltpu.VMEM)] * count


def smem(count):
    return [pl.BlockSpec(memory_space=pltpu.SMEM)] * count


def anywhere(count):
    return [pl.BlockSpec(memory_space=pl.ANY)] * count


def hbm(count):
    return [pl.BlockSpec(memory_space=pltpu.HBM)] * count


def pair_capacity(tile_max, dest_count):
    most = (tile_max + dest_count // 2) // 2
    return -(-most // UNROLL) * UNROLL


def code_bits(tile_max, source_tiles, half_dests):
    sizes = (tile_max, source_tiles + 1, source_tiles + 1, half_dests, 2)
    widths = [(size - 1).bit_length() for size in sizes]
    assert sum(widths) < 32
    return [(sum(widths[at + 1 :]), (1 << width) - 1) for at, width in enumerate(widths)]


def encode(fields, bits):
    code = jnp.int32(0)
    for field, (shift, _) in zip(fields, bits):
        code = code + lax.shift_left(field, jnp.int32(shift))
    return code


def decode(code, bits):
    return [
        lax.bitwise_and(lax.shift_right_logical(code, jnp.int32(shift)), jnp.int32(mask))
        for shift, mask in bits
    ]


def prepare_kernel(
    tiles_per_owner,
    bits,
    place_ref,
    src_ref,
    count_ref,
    tile_ref,
    turned_ref,
    weight_ref,
    list_ref,
    held_ref,
    staged_ref,
    sum_ref,
    in_sems,
    out_sems,
):
    tile_max, tile_size, _ = tile_ref.shape
    dest_count = count_ref.shape[1]
    zero_tile = place_ref[2]
    my_row = place_ref[0]
    pieces = in_sems.shape[0]
    piece = tile_max // pieces
    spans = [pl.ds(index * piece, piece) for index in range(pieces)]
    copies_in = [
        pltpu.make_async_copy(tile_ref.at[span], held_ref.at[span], in_sems.at[index])
        for index, span in enumerate(spans)
    ]
    copies_out = [
        pltpu.make_async_copy(staged_ref.at[span], turned_ref.at[span], out_sems.at[index])
        for index, span in enumerate(spans)
    ]
    for copy in copies_in:
        copy.start()

    rows_each = (list_ref.shape[0] - 2) // 2

    for half in range(2):

        def put(at, fields, half=half):
            row = lax.div(at, UNROLL)
            list_ref[half * rows_each + row, at - row * UNROLL] = encode(fields, bits)

        def one_dest(dest, carry, half=half, put=put):
            start, used, _ = carry
            owner = lax.div(dest, tiles_per_owner)
            relative = lax.bitwise_xor(owner, my_row)
            count = count_ref[0, dest]
            mine = lax.bitwise_and(relative, 1) == half
            pairs = jnp.where(mine, lax.div(count + 1, 2), 0)
            chip = lax.div(relative, 2)
            target = chip * tiles_per_owner + dest - owner * tiles_per_owner

            def one_pair(pair, carry):
                slot = start + 2 * pair
                next_slot = jnp.minimum(slot + 1, tile_max - 1)
                second = jnp.where(2 * pair + 1 < count, src_ref[0, next_slot], zero_tile)
                go_on = jnp.where(pair > 0, 1, 0)
                put(used + pair, (slot, src_ref[0, slot], second, target, go_on))
                return carry

            lax.fori_loop(0, pairs, one_pair, 0)
            return start + count, used + pairs, jnp.where(mine, target, carry[2])

        zero = jnp.int32(0)
        _, used, last = lax.fori_loop(0, dest_count, one_dest, (zero, zero, zero))
        turns = lax.div(used + UNROLL - 1, UNROLL)

        def one_pad(at, carry, put=put, last=last):
            put(at, (jnp.int32(0), zero_tile, zero_tile, last, jnp.int32(1)))
            return carry

        lax.fori_loop(used, turns * UNROLL, one_pad, 0)
        for column in range(UNROLL):
            list_ref[2 * rows_each + half, column] = turns

    group = min(8, piece)
    for index in range(pieces):
        copies_in[index].wait()

        def one_group(at, carry, index=index):
            for step in range(group):
                slot = index * piece + at * group + step
                tile = held_ref[slot]
                staged_ref[slot] = tile.T
                sum_ref[pl.ds(slot, 1), :] = jnp.sum(
                    tile.astype(jnp.float32), axis=0, keepdims=True
                )
            return carry

        lax.fori_loop(0, piece // group, one_group, 0)
        copies_out[index].start()

    sum_ref[tile_max:, :] = jnp.zeros((MOST, tile_size), jnp.float32)
    weight_ref[...] = jnp.zeros(weight_ref.shape, weight_ref.dtype)
    places = lax.broadcasted_iota(jnp.int32, (MOST, tile_size), 0)

    def weigh(owner, start):
        relative = lax.bitwise_xor(owner, my_row)
        chip = lax.div(relative, 2)
        for step in range(tiles_per_owner):
            count = count_ref[0, owner * tiles_per_owner + step]
            sums = jnp.where(places < count, sum_ref[pl.ds(start, MOST), :], 0.0)
            weight_ref[lax.bitwise_and(relative, 1), chip, step : step + 1, :] = jnp.sum(
                sums, axis=0, keepdims=True
            )
            start = start + count
        return start

    lax.fori_loop(0, dest_count // tiles_per_owner, weigh, jnp.int32(0))
    for copy in copies_out:
        copy.wait()


def prepare(place, tile_src, row_counts, tile_vals, row_size, tiles_per_owner, bits):
    tile_max, tile_size, _ = tile_vals.shape
    capacity = pair_capacity(tile_max, row_counts.shape[1])
    chips = row_size // 2
    return pl.pallas_call(
        functools.partial(prepare_kernel, tiles_per_owner, bits),
        out_shape=[
            jax.ShapeDtypeStruct(tile_vals.shape, tile_vals.dtype),
            jax.ShapeDtypeStruct((2, chips, EXTRA, tile_size), jnp.float32),
            jax.ShapeDtypeStruct((2 * (capacity // UNROLL) + 2, UNROLL), jnp.int32),
        ],
        in_specs=smem(3) + hbm(1),
        out_specs=hbm(1) + vmem(1) + smem(1),
        scratch_shapes=[
            pltpu.VMEM(tile_vals.shape, tile_vals.dtype),
            pltpu.VMEM(tile_vals.shape, tile_vals.dtype),
            pltpu.VMEM((tile_max + MOST, tile_size), jnp.float32),
            pltpu.SemaphoreType.DMA((8,)),
            pltpu.SemaphoreType.DMA((8,)),
        ],
        compiler_params=pltpu.CompilerParams(vmem_limit_bytes=24 * 2**20),
        name="prepare",
    )(place, tile_src, row_counts, tile_vals)


def pack_kernel(blocks, features_ref, *part_refs):
    rows = features_ref.shape[0] // blocks
    piece = features_ref.shape[1] // len(part_refs)
    for chunk, part_ref in enumerate(part_refs):
        lanes = slice(chunk * piece, (chunk + 1) * piece)
        part_ref[...] = jnp.concatenate(
            [features_ref[b * rows : (b + 1) * rows, lanes] for b in range(blocks)], axis=1
        )


def pack(features, blocks):
    rows = features.shape[0] // blocks
    width = features.shape[1] // CHUNKS * blocks
    return pl.pallas_call(
        functools.partial(pack_kernel, blocks),
        out_shape=[jax.ShapeDtypeStruct((rows, width), features.dtype)] * CHUNKS,
        in_specs=vmem(1),
        out_specs=vmem(CHUNKS),
        compiler_params=pltpu.CompilerParams(vmem_limit_bytes=4 * 2**20),
        name="pack",
    )(features)


def assemble_kernel(packed, masks, *refs):
    blocks = len(masks)
    block_refs = refs[:blocks]
    held_ref = refs[blocks + 1]
    staged_ref = refs[-1] if packed else held_ref
    col = lax.axis_index("col")
    rows, width = block_refs[0].shape

    def put(mask, ref):
        first = pl.multiple_of(lax.bitwise_xor(col, mask) * rows, rows)
        staged_ref[pl.ds(first, rows), :] = ref[...]

    for mask, ref in zip(masks, block_refs):
        put(mask, ref)
    if packed:
        piece = width // blocks
        for group in range(blocks):
            lanes = slice(group * piece, (group + 1) * piece)
            held_ref[group * rows : (group + 1) * rows, :] = jnp.concatenate(
                [staged_ref[b * rows : (b + 1) * rows, lanes] for b in range(blocks)], axis=1
            )
        own_ref = refs[blocks + 2]
        own_ref[...] = held_ref[pl.ds(pl.multiple_of(col * rows, rows), rows), :]
    zeros = held_ref.shape[0] - blocks * rows
    held_ref[blocks * rows :, :] = jnp.zeros((zeros, width), held_ref.dtype)


def assemble(gathered, after, tile_size, packed):
    blocks = len(gathered)
    masks = sorted(gathered, key=lambda mask: (2 * mask < blocks, mask))
    rows, width = gathered[0].shape
    out_shape = [jax.ShapeDtypeStruct((blocks * rows + tile_size, width), jnp.bfloat16)]
    scratch = []
    if packed:
        out_shape.append(jax.ShapeDtypeStruct((rows, width), jnp.bfloat16))
        scratch.append(pltpu.VMEM((blocks * rows, width), jnp.bfloat16))
    return pl.pallas_call(
        functools.partial(assemble_kernel, packed, masks),
        out_shape=out_shape,
        in_specs=vmem(blocks) + anywhere(1),
        out_specs=vmem(len(out_shape)),
        scratch_shapes=scratch,
        compiler_params=pltpu.CompilerParams(vmem_limit_bytes=4 * 2**20),
        cost_estimate=pl.CostEstimate(flops=0, bytes_accessed=4 * 2**20, transcendentals=0),
        name="assemble",
    )(*[gathered[mask] for mask in masks], after)


def product_kernel(half, rows, bits, list_ref, turned_ref, held_ref, weight_ref, out_ref):
    tile_max, tile_size, _ = turned_ref.shape
    chips, out_rows, width = out_ref.shape
    rows_each = (list_ref.shape[0] - 2) // 2
    tiles = rows // tile_size
    if out_rows > rows:
        out_ref[:, rows:, :] = weight_ref[half].astype(out_ref.dtype)

    def codes_of(row):
        line = list_ref[pl.ds(row, 1), :]
        return tuple(line[0, step] for step in range(UNROLL))

    def one_turn(turn, carry):
        running, codes = carry
        later = codes_of(half * rows_each + turn + 1)
        for step in range(UNROLL):
            slot, first, second, target, go_on = decode(codes[step], bits)
            left = jnp.concatenate(
                [turned_ref[slot], turned_ref[jnp.minimum(slot + 1, tile_max - 1)]], axis=1
            )
            first = pl.multiple_of(first * tile_size, tile_size)
            second = pl.multiple_of(second * tile_size, tile_size)
            right = jnp.concatenate(
                [held_ref[pl.ds(first, tile_size), :], held_ref[pl.ds(second, tile_size), :]],
                axis=0,
            )
            term = jnp.dot(left, right, preferred_element_type=jnp.float32)
            running = running * go_on.astype(jnp.float32) + term
            chip = lax.div(target, tiles)
            row = pl.multiple_of((target - chip * tiles) * tile_size, tile_size)
            out_ref[chip, pl.ds(row, tile_size), :] = running.astype(out_ref.dtype)
        return running, later

    turns = list_ref[2 * rows_each + half : 2 * rows_each + half + 1, :][0, 0]
    zeros = jnp.zeros((tile_size, width), jnp.float32)
    lax.fori_loop(0, turns, one_turn, (zeros, codes_of(half * rows_each)))


def product(half, pairs, turned, held, weights, rows, chips, extra, bits):
    return pl.pallas_call(
        functools.partial(product_kernel, half, rows, bits),
        out_shape=jax.ShapeDtypeStruct((chips, rows + extra, held.shape[1]), jnp.bfloat16),
        in_specs=vmem(4),
        out_specs=vmem(1)[0],
        compiler_params=pltpu.CompilerParams(vmem_limit_bytes=4 * 2**20),
        cost_estimate=pl.CostEstimate(
            flops=600000000, bytes_accessed=6000000, transcendentals=0
        ),
        name="product",
    )(pairs, turned, held, weights)


def update_kernel(kept_ref, *refs):
    *arrived_refs, iterate_ref, restart_ref, scale_ref, out_ref = refs
    rows = out_ref.shape[0]
    summed = kept_ref[:rows, :]
    for ref in arrived_refs:
        summed = summed + ref[:rows, :].astype(jnp.float32)
    out_ref[...] = (
        scale_ref[...] * (summed + iterate_ref[...].astype(jnp.float32))
        + TELEPORT * restart_ref[...].astype(jnp.float32)
    ).astype(out_ref.dtype)


def update(kept, arrived, iterate, restart, scale):
    return pl.pallas_call(
        update_kernel,
        out_shape=jax.ShapeDtypeStruct(iterate.shape, iterate.dtype),
        in_specs=vmem(len(arrived) + 4),
        out_specs=vmem(1)[0],
        compiler_params=pltpu.CompilerParams(vmem_limit_bytes=4 * 2**20),
        cost_estimate=pl.CostEstimate(flops=0, bytes_accessed=1, transcendentals=0),
        name="update",
    )(kept, *arrived, iterate, restart, scale)


def exchange(block, axis, mask, size):
    return lax.ppermute(block, axis, [(i, i ^ mask) for i in range(size)])


def gather_line(block, size, masks):
    return {mask: exchange(block, "col", mask, size) for mask in masks}


def reduce_chips(both, cut, chip_bits, row_size):
    kept, arrived = [], []
    for half in range(2):
        state = both[:, :cut] if half == 0 else both[:, cut:]
        state = state.reshape((2,) * len(chip_bits) + state.shape[1:])
        left = list(chip_bits)
        turn = half % len(chip_bits)
        got = None
        for bit in chip_bits[turn:] + chip_bits[:turn]:
            if got is not None:
                state = state + got.astype(jnp.float32)
            axis = left.index(bit)
            send = lax.index_in_dim(state, 1, axis, keepdims=False).astype(jnp.bfloat16)
            state = lax.index_in_dim(state, 0, axis, keepdims=False)
            got = exchange(send, "row", 1 << bit, row_size)
            left.remove(bit)
        kept.append(state)
        arrived.append(got)
    return jnp.concatenate(kept), jnp.concatenate(arrived)


def on_device(features, tile_vals, tile_src, row_counts):
    row_size = lax.axis_size("row")
    blocks = lax.axis_size("col")
    my_row = lax.axis_index("row").astype(jnp.int32)
    my_col = lax.axis_index("col").astype(jnp.int32)
    tile_size = tile_vals.shape[1]
    dest_count = row_counts.shape[1]
    rows = features.shape[0] // blocks
    source_tiles = features.shape[0] // tile_size
    width = features.shape[1] * blocks // CHUNKS
    piece = features.shape[1] // CHUNKS
    tiles_per_owner = dest_count // row_size
    chips = row_size // 2
    chip_bits = list(range(row_size.bit_length() - 2, 0, -1))
    bits = code_bits(tile_vals.shape[0], source_tiles, dest_count // 2)
    place = jnp.stack([my_row, my_col, jnp.int32(source_tiles)])

    parts = pack(features, blocks)

    turned, weights, pairs = prepare(
        place, tile_src, row_counts, tile_vals, row_size, tiles_per_owner, bits
    )

    gathered = [{0: parts[0], **gather_line(parts[0], blocks, range(1, blocks))}, None]
    early = [mask for mask in range(1, blocks) if 2 * mask >= blocks]
    late = [mask for mask in range(1, blocks) if mask not in early]
    iterates = [None] * CHUNKS
    restarts = [None] * CHUNKS
    scale = None
    last = place
    for phase in range(ITERS * CHUNKS):
        chunk = phase % CHUNKS
        after = 1 - chunk
        first = phase < CHUNKS
        extra = EXTRA if phase == 0 else 0
        if phase > 0:
            iterates[after] = last = update(*pending)
        held, *own = assemble(gathered[chunk], last, tile_size, first)
        if first:
            iterates[chunk] = restarts[chunk] = own[0]
        if phase == 0:
            held, coming = lax.optimization_barrier((held, parts[1]))
        elif phase + 1 < ITERS * CHUNKS:
            coming = iterates[after]
        else:
            coming = None
        if coming is not None:
            gathered[after] = {0: coming, **gather_line(coming, blocks, early)}
        sent = product(1, pairs, turned, held, weights, rows, chips, extra, bits)
        other = exchange(sent, "row", 1, row_size)
        kept = product(0, pairs, turned, held, weights, rows, chips, extra, bits)
        both = kept.astype(jnp.float32) + other.astype(jnp.float32)
        if coming is not None:
            coming, both = lax.optimization_barrier((coming, both))
            gathered[after].update(gather_line(coming, blocks, late))
        if phase + 1 < ITERS * CHUNKS:
            kept, arrived = reduce_chips(both, rows // 2, chip_bits, row_size)
            arrived = [arrived]
        else:
            kept = both[0]
            arrived = [
                exchange(both[mask].astype(jnp.bfloat16), "row", 2 * mask, row_size)
                for mask in range(chips - 1, 0, -1)
            ]
        if phase == 0:
            weight_rows = slice(rows, rows + tiles_per_owner)
            total = 1.0 + kept[weight_rows] + arrived[0][weight_rows].astype(jnp.float32)
            scale = jnp.broadcast_to(
                ((1.0 - TELEPORT) / total).reshape(rows, 1), (rows, width)
            )
        pending = (kept, arrived, iterates[chunk], restarts[chunk], scale)
    iterates[chunk] = update(*pending)
    iterates = lax.optimization_barrier(iterates)
    out = jnp.stack(iterates).reshape(CHUNKS, rows, blocks, piece).transpose(1, 2, 0, 3)
    return out.reshape(rows, CHUNKS * width)


def solution(mesh):
    placed = (P("row", "col"), P("row", "col", None), P("row", "col"), P("row", "col"))
    return jax.shard_map(
        on_device, mesh=mesh, in_specs=placed, out_specs=P(("row", "col"), None), check_vma=False
    )
```

```python
import functools

import jax
import jax.numpy as jnp
from jax import lax
from jax.experimental import pallas as pl
from jax.experimental.pallas import tpu as pltpu
from jax.sharding import PartitionSpec as P

ITERS = 3


TELEPORT = 0.1


CHUNKS = 2


UNROLL = 12


EXTRA = 16


MOST = 8


def vmem(count):
    return [pl.BlockSpec(memory_space=pltpu.VMEM)] * count


def smem(count):
    return [pl.BlockSpec(memory_space=pltpu.SMEM)] * count


def anywhere(count):
    return [pl.BlockSpec(memory_space=pl.ANY)] * count


def hbm(count):
    return [pl.BlockSpec(memory_space=pltpu.HBM)] * count


def pair_capacity(tile_max, dest_count):
    most = (tile_max + dest_count // 2) // 2
    return -(-most // UNROLL) * UNROLL


def code_bits(tile_max, source_tiles, half_dests):
    sizes = (tile_max, source_tiles + 1, source_tiles + 1, half_dests, 2)
    widths = [(size - 1).bit_length() for size in sizes]
    assert sum(widths) < 32
    return [(sum(widths[at + 1 :]), (1 << width) - 1) for at, width in enumerate(widths)]


def encode(fields, bits):
    code = jnp.int32(0)
    for field, (shift, _) in zip(fields, bits):
        code = code + lax.shift_left(field, jnp.int32(shift))
    return code


def decode(code, bits):
    return [
        lax.bitwise_and(lax.shift_right_logical(code, jnp.int32(shift)), jnp.int32(mask))
        for shift, mask in bits
    ]


def prepare_kernel(
    tiles_per_owner,
    bits,
    place_ref,
    src_ref,
    count_ref,
    tile_ref,
    turned_ref,
    weight_ref,
    list_ref,
    held_ref,
    staged_ref,
    sum_ref,
    in_sems,
    out_sems,
):
    tile_max, tile_size, _ = tile_ref.shape
    dest_count = count_ref.shape[1]
    zero_tile = place_ref[2]
    my_row = place_ref[0]
    pieces = in_sems.shape[0]
    piece = tile_max // pieces
    spans = [pl.ds(index * piece, piece) for index in range(pieces)]
    copies_in = [
        pltpu.make_async_copy(tile_ref.at[span], held_ref.at[span], in_sems.at[index])
        for index, span in enumerate(spans)
    ]
    copies_out = [
        pltpu.make_async_copy(staged_ref.at[span], turned_ref.at[span], out_sems.at[index])
        for index, span in enumerate(spans)
    ]
    for copy in copies_in:
        copy.start()

    rows_each = (list_ref.shape[0] - 2) // 2

    for half in range(2):

        def put(at, fields, half=half):
            row = lax.div(at, UNROLL)
            list_ref[half * rows_each + row, at - row * UNROLL] = encode(fields, bits)

        def one_dest(dest, carry, half=half, put=put):
            start, used, _ = carry
            owner = lax.div(dest, tiles_per_owner)
            relative = lax.bitwise_xor(owner, my_row)
            count = count_ref[0, dest]
            mine = lax.bitwise_and(relative, 1) == half
            pairs = jnp.where(mine, lax.div(count + 1, 2), 0)
            chip = lax.div(relative, 2)
            target = chip * tiles_per_owner + dest - owner * tiles_per_owner

            def one_pair(pair, carry):
                slot = start + 2 * pair
                next_slot = jnp.minimum(slot + 1, tile_max - 1)
                second = jnp.where(2 * pair + 1 < count, src_ref[0, next_slot], zero_tile)
                go_on = jnp.where(pair > 0, 1, 0)
                put(used + pair, (slot, src_ref[0, slot], second, target, go_on))
                return carry

            lax.fori_loop(0, pairs, one_pair, 0)
            return start + count, used + pairs, jnp.where(mine, target, carry[2])

        zero = jnp.int32(0)
        _, used, last = lax.fori_loop(0, dest_count, one_dest, (zero, zero, zero))
        turns = lax.div(used + UNROLL - 1, UNROLL)

        def one_pad(at, carry, put=put, last=last):
            put(at, (jnp.int32(0), zero_tile, zero_tile, last, jnp.int32(1)))
            return carry

        lax.fori_loop(used, turns * UNROLL, one_pad, 0)
        for column in range(UNROLL):
            list_ref[2 * rows_each + half, column] = turns

    group = min(8, piece)
    for index in range(pieces):
        copies_in[index].wait()

        def one_group(at, carry, index=index):
            for step in range(group):
                slot = index * piece + at * group + step
                tile = held_ref[slot]
                staged_ref[slot] = tile.T
                sum_ref[pl.ds(slot, 1), :] = jnp.sum(
                    tile.astype(jnp.float32), axis=0, keepdims=True
                )
            return carry

        lax.fori_loop(0, piece // group, one_group, 0)
        copies_out[index].start()

    sum_ref[tile_max:, :] = jnp.zeros((MOST, tile_size), jnp.float32)
    weight_ref[...] = jnp.zeros(weight_ref.shape, weight_ref.dtype)
    places = lax.broadcasted_iota(jnp.int32, (MOST, tile_size), 0)

    def weigh(owner, start):
        relative = lax.bitwise_xor(owner, my_row)
        chip = lax.div(relative, 2)
        for step in range(tiles_per_owner):
            count = count_ref[0, owner * tiles_per_owner + step]
            sums = jnp.where(places < count, sum_ref[pl.ds(start, MOST), :], 0.0)
            weight_ref[lax.bitwise_and(relative, 1), chip, step : step + 1, :] = jnp.sum(
                sums, axis=0, keepdims=True
            )
            start = start + count
        return start

    lax.fori_loop(0, dest_count // tiles_per_owner, weigh, jnp.int32(0))
    for copy in copies_out:
        copy.wait()


def prepare(place, tile_src, row_counts, tile_vals, row_size, tiles_per_owner, bits):
    tile_max, tile_size, _ = tile_vals.shape
    capacity = pair_capacity(tile_max, row_counts.shape[1])
    chips = row_size // 2
    return pl.pallas_call(
        functools.partial(prepare_kernel, tiles_per_owner, bits),
        out_shape=[
            jax.ShapeDtypeStruct(tile_vals.shape, tile_vals.dtype),
            jax.ShapeDtypeStruct((2, chips, EXTRA, tile_size), jnp.float32),
            jax.ShapeDtypeStruct((2 * (capacity // UNROLL) + 2, UNROLL), jnp.int32),
        ],
        in_specs=smem(3) + hbm(1),
        out_specs=hbm(1) + vmem(1) + smem(1),
        scratch_shapes=[
            pltpu.VMEM(tile_vals.shape, tile_vals.dtype),
            pltpu.VMEM(tile_vals.shape, tile_vals.dtype),
            pltpu.VMEM((tile_max + MOST, tile_size), jnp.float32),
            pltpu.SemaphoreType.DMA((8,)),
            pltpu.SemaphoreType.DMA((8,)),
        ],
        compiler_params=pltpu.CompilerParams(vmem_limit_bytes=24 * 2**20),
        name="prepare",
    )(place, tile_src, row_counts, tile_vals)


def pack_kernel(blocks, features_ref, *part_refs):
    rows = features_ref.shape[0] // blocks
    piece = features_ref.shape[1] // len(part_refs)
    for chunk, part_ref in enumerate(part_refs):
        lanes = slice(chunk * piece, (chunk + 1) * piece)
        part_ref[...] = jnp.concatenate(
            [features_ref[b * rows : (b + 1) * rows, lanes] for b in range(blocks)], axis=1
        )


def pack(features, blocks):
    rows = features.shape[0] // blocks
    width = features.shape[1] // CHUNKS * blocks
    return pl.pallas_call(
        functools.partial(pack_kernel, blocks),
        out_shape=[jax.ShapeDtypeStruct((rows, width), features.dtype)] * CHUNKS,
        in_specs=vmem(1),
        out_specs=vmem(CHUNKS),
        compiler_params=pltpu.CompilerParams(vmem_limit_bytes=4 * 2**20),
        name="pack",
    )(features)


def assemble_kernel(packed, masks, *refs):
    blocks = len(masks)
    block_refs = refs[:blocks]
    held_ref = refs[blocks + 1]
    staged_ref = refs[-1] if packed else held_ref
    col = lax.axis_index("col")
    rows, width = block_refs[0].shape

    def put(mask, ref):
        first = pl.multiple_of(lax.bitwise_xor(col, mask) * rows, rows)
        staged_ref[pl.ds(first, rows), :] = ref[...]

    for mask, ref in zip(masks, block_refs):
        put(mask, ref)
    if packed:
        piece = width // blocks
        for group in range(blocks):
            lanes = slice(group * piece, (group + 1) * piece)
            held_ref[group * rows : (group + 1) * rows, :] = jnp.concatenate(
                [staged_ref[b * rows : (b + 1) * rows, lanes] for b in range(blocks)], axis=1
            )
        own_ref = refs[blocks + 2]
        own_ref[...] = held_ref[pl.ds(pl.multiple_of(col * rows, rows), rows), :]
    zeros = held_ref.shape[0] - blocks * rows
    held_ref[blocks * rows :, :] = jnp.zeros((zeros, width), held_ref.dtype)


def assemble(gathered, after, tile_size, packed):
    blocks = len(gathered)
    masks = sorted(gathered, key=lambda mask: (2 * mask < blocks, mask))
    rows, width = gathered[0].shape
    out_shape = [jax.ShapeDtypeStruct((blocks * rows + tile_size, width), jnp.bfloat16)]
    scratch = []
    if packed:
        out_shape.append(jax.ShapeDtypeStruct((rows, width), jnp.bfloat16))
        scratch.append(pltpu.VMEM((blocks * rows, width), jnp.bfloat16))
    return pl.pallas_call(
        functools.partial(assemble_kernel, packed, masks),
        out_shape=out_shape,
        in_specs=vmem(blocks) + anywhere(1),
        out_specs=vmem(len(out_shape)),
        scratch_shapes=scratch,
        compiler_params=pltpu.CompilerParams(vmem_limit_bytes=4 * 2**20),
        cost_estimate=pl.CostEstimate(flops=0, bytes_accessed=4 * 2**20, transcendentals=0),
        name="assemble",
    )(*[gathered[mask] for mask in masks], after)


def product_kernel(half, rows, bits, list_ref, turned_ref, held_ref, weight_ref, out_ref):
    tile_max, tile_size, _ = turned_ref.shape
    chips, out_rows, width = out_ref.shape
    rows_each = (list_ref.shape[0] - 2) // 2
    tiles = rows // tile_size
    if out_rows > rows:
        out_ref[:, rows:, :] = weight_ref[half].astype(out_ref.dtype)

    def codes_of(row):
        line = list_ref[pl.ds(row, 1), :]
        return tuple(line[0, step] for step in range(UNROLL))

    def one_turn(turn, carry):
        running, codes = carry
        later = codes_of(half * rows_each + turn + 1)
        for step in range(UNROLL):
            slot, first, second, target, go_on = decode(codes[step], bits)
            left = jnp.concatenate(
                [turned_ref[slot], turned_ref[jnp.minimum(slot + 1, tile_max - 1)]], axis=1
            )
            first = pl.multiple_of(first * tile_size, tile_size)
            second = pl.multiple_of(second * tile_size, tile_size)
            right = jnp.concatenate(
                [held_ref[pl.ds(first, tile_size), :], held_ref[pl.ds(second, tile_size), :]],
                axis=0,
            )
            term = jnp.dot(left, right, preferred_element_type=jnp.float32)
            running = running * go_on.astype(jnp.float32) + term
            chip = lax.div(target, tiles)
            row = pl.multiple_of((target - chip * tiles) * tile_size, tile_size)
            out_ref[chip, pl.ds(row, tile_size), :] = running.astype(out_ref.dtype)
        return running, later

    turns = list_ref[2 * rows_each + half : 2 * rows_each + half + 1, :][0, 0]
    zeros = jnp.zeros((tile_size, width), jnp.float32)
    lax.fori_loop(0, turns, one_turn, (zeros, codes_of(half * rows_each)))


def product(half, pairs, turned, held, weights, rows, chips, extra, bits):
    return pl.pallas_call(
        functools.partial(product_kernel, half, rows, bits),
        out_shape=jax.ShapeDtypeStruct((chips, rows + extra, held.shape[1]), jnp.bfloat16),
        in_specs=vmem(4),
        out_specs=vmem(1)[0],
        compiler_params=pltpu.CompilerParams(vmem_limit_bytes=4 * 2**20),
        cost_estimate=pl.CostEstimate(
            flops=600000000, bytes_accessed=6000000, transcendentals=0
        ),
        name="product",
    )(pairs, turned, held, weights)


def update_kernel(kept_ref, *refs):
    *arrived_refs, iterate_ref, restart_ref, scale_ref, out_ref = refs
    rows = out_ref.shape[0]
    summed = kept_ref[:rows, :]
    for ref in arrived_refs:
        summed = summed + ref[:rows, :].astype(jnp.float32)
    out_ref[...] = (
        scale_ref[...] * (summed + iterate_ref[...].astype(jnp.float32))
        + TELEPORT * restart_ref[...].astype(jnp.float32)
    ).astype(out_ref.dtype)


def update(kept, arrived, iterate, restart, scale):
    return pl.pallas_call(
        update_kernel,
        out_shape=jax.ShapeDtypeStruct(iterate.shape, iterate.dtype),
        in_specs=vmem(len(arrived) + 4),
        out_specs=vmem(1)[0],
        compiler_params=pltpu.CompilerParams(vmem_limit_bytes=4 * 2**20),
        cost_estimate=pl.CostEstimate(flops=0, bytes_accessed=1, transcendentals=0),
        name="update",
    )(kept, *arrived, iterate, restart, scale)


def exchange(block, axis, mask, size):
    return lax.ppermute(block, axis, [(i, i ^ mask) for i in range(size)])


def gather_line(block, size, masks):
    return {mask: exchange(block, "col", mask, size) for mask in masks}


def reduce_chips(both, cut, chip_bits, row_size):
    kept, arrived = [], []
    for half in range(2):
        state = both[:, :cut] if half == 0 else both[:, cut:]
        state = state.reshape((2,) * len(chip_bits) + state.shape[1:])
        left = list(chip_bits)
        turn = half % len(chip_bits)
        got = None
        for bit in chip_bits[turn:] + chip_bits[:turn]:
            if got is not None:
                state = state + got.astype(jnp.float32)
            axis = left.index(bit)
            send = lax.index_in_dim(state, 1, axis, keepdims=False).astype(jnp.bfloat16)
            state = lax.index_in_dim(state, 0, axis, keepdims=False)
            got = exchange(send, "row", 1 << bit, row_size)
            left.remove(bit)
        kept.append(state)
        arrived.append(got)
    return jnp.concatenate(kept), jnp.concatenate(arrived)


def on_device(features, tile_vals, tile_src, row_counts):
    row_size = lax.axis_size("row")
    blocks = lax.axis_size("col")
    my_row = lax.axis_index("row").astype(jnp.int32)
    my_col = lax.axis_index("col").astype(jnp.int32)
    tile_size = tile_vals.shape[1]
    dest_count = row_counts.shape[1]
    rows = features.shape[0] // blocks
    source_tiles = features.shape[0] // tile_size
    width = features.shape[1] * blocks // CHUNKS
    piece = features.shape[1] // CHUNKS
    tiles_per_owner = dest_count // row_size
    chips = row_size // 2
    chip_bits = list(range(row_size.bit_length() - 2, 0, -1))
    bits = code_bits(tile_vals.shape[0], source_tiles, dest_count // 2)
    place = jnp.stack([my_row, my_col, jnp.int32(source_tiles)])

    parts = pack(features, blocks)

    turned, weights, pairs = prepare(
        place, tile_src, row_counts, tile_vals, row_size, tiles_per_owner, bits
    )

    gathered = [{0: parts[0], **gather_line(parts[0], blocks, range(1, blocks))}, None]
    early = [mask for mask in range(1, blocks) if 2 * mask >= blocks]
    late = [mask for mask in range(1, blocks) if mask not in early]
    iterates = [None] * CHUNKS
    restarts = [None] * CHUNKS
    scale = None
    last = place
    for phase in range(ITERS * CHUNKS):
        chunk = phase % CHUNKS
        after = 1 - chunk
        first = phase < CHUNKS
        extra = EXTRA if phase == 0 else 0
        if phase > 0:
            iterates[after] = last = update(*pending)
        held, *own = assemble(gathered[chunk], last, tile_size, first)
        if first:
            iterates[chunk] = restarts[chunk] = own[0]
        if phase == 0:
            held, coming = lax.optimization_barrier((held, parts[1]))
        elif phase + 1 < ITERS * CHUNKS:
            coming = iterates[after]
        else:
            coming = None
        if coming is not None:
            gathered[after] = {0: coming, **gather_line(coming, blocks, early)}
        sent = product(1, pairs, turned, held, weights, rows, chips, extra, bits)
        other = exchange(sent, "row", 1, row_size)
        kept = product(0, pairs, turned, held, weights, rows, chips, extra, bits)
        both = kept.astype(jnp.float32) + other.astype(jnp.float32)
        if coming is not None:
            coming, both = lax.optimization_barrier((coming, both))
            gathered[after].update(gather_line(coming, blocks, late))
        if phase + 1 < ITERS * CHUNKS:
            kept, arrived = reduce_chips(both, rows // 2, chip_bits, row_size)
            arrived = [arrived]
        else:
            kept = both[0]
            arrived = [
                exchange(both[mask].astype(jnp.bfloat16), "row", 2 * mask, row_size)
                for mask in range(chips - 1, 0, -1)
            ]
        if phase == 0:
            weight_rows = slice(rows, rows + tiles_per_owner)
            total = 1.0 + kept[weight_rows] + arrived[0][weight_rows].astype(jnp.float32)
            scale = jnp.broadcast_to(
                ((1.0 - TELEPORT) / total).reshape(rows, 1), (rows, width)
            )
        pending = (kept, arrived, iterates[chunk], restarts[chunk], scale)
    iterates[chunk] = update(*pending)
    iterates = lax.optimization_barrier(iterates)
    out = jnp.stack(iterates).reshape(CHUNKS, rows, blocks, piece).transpose(1, 2, 0, 3)
    return out.reshape(rows, CHUNKS * width)


def solution(mesh):
    placed = (P("row", "col"), P("row", "col", None), P("row", "col"), P("row", "col"))
    return jax.shard_map(
        on_device, mesh=mesh, in_specs=placed, out_specs=P(("row", "col"), None), check_vma=False
    )
```

```python
import functools

import jax
import jax.numpy as jnp
from jax import lax
from jax.experimental import pallas as pl
from jax.experimental.pallas import tpu as pltpu
from jax.sharding import PartitionSpec as P

ITERS = 3


TELEPORT = 0.1


CHUNKS = 2


UNROLL = 24


EXTRA = 16


MOST = 8


def vmem(count):
    return [pl.BlockSpec(memory_space=pltpu.VMEM)] * count


def smem(count):
    return [pl.BlockSpec(memory_space=pltpu.SMEM)] * count


def anywhere(count):
    return [pl.BlockSpec(memory_space=pl.ANY)] * count


def hbm(count):
    return [pl.BlockSpec(memory_space=pltpu.HBM)] * count


def pair_capacity(tile_max, dest_count):
    most = (tile_max + dest_count // 2) // 2
    return -(-most // UNROLL) * UNROLL


def code_bits(tile_max, source_tiles, half_dests):
    sizes = (tile_max, source_tiles + 1, source_tiles + 1, half_dests, 2)
    widths = [(size - 1).bit_length() for size in sizes]
    assert sum(widths) < 32
    return [(sum(widths[at + 1 :]), (1 << width) - 1) for at, width in enumerate(widths)]


def encode(fields, bits):
    code = jnp.int32(0)
    for field, (shift, _) in zip(fields, bits):
        code = code + lax.shift_left(field, jnp.int32(shift))
    return code


def decode(code, bits):
    return [
        lax.bitwise_and(lax.shift_right_logical(code, jnp.int32(shift)), jnp.int32(mask))
        for shift, mask in bits
    ]


def prepare_kernel(
    tiles_per_owner,
    bits,
    place_ref,
    src_ref,
    count_ref,
    tile_ref,
    turned_ref,
    weight_ref,
    list_ref,
    held_ref,
    staged_ref,
    sum_ref,
    in_sems,
    out_sems,
):
    tile_max, tile_size, _ = tile_ref.shape
    dest_count = count_ref.shape[1]
    zero_tile = place_ref[2]
    my_row = place_ref[0]
    pieces = in_sems.shape[0]
    piece = tile_max // pieces
    spans = [pl.ds(index * piece, piece) for index in range(pieces)]
    copies_in = [
        pltpu.make_async_copy(tile_ref.at[span], held_ref.at[span], in_sems.at[index])
        for index, span in enumerate(spans)
    ]
    copies_out = [
        pltpu.make_async_copy(staged_ref.at[span], turned_ref.at[span], out_sems.at[index])
        for index, span in enumerate(spans)
    ]
    for copy in copies_in:
        copy.start()

    rows_each = (list_ref.shape[0] - 2) // 2

    for half in range(2):

        def put(at, fields, half=half):
            row = lax.div(at, UNROLL)
            list_ref[half * rows_each + row, at - row * UNROLL] = encode(fields, bits)

        def one_dest(dest, carry, half=half, put=put):
            start, used, _ = carry
            owner = lax.div(dest, tiles_per_owner)
            relative = lax.bitwise_xor(owner, my_row)
            count = count_ref[0, dest]
            mine = lax.bitwise_and(relative, 1) == half
            pairs = jnp.where(mine, lax.div(count + 1, 2), 0)
            chip = lax.div(relative, 2)
            target = chip * tiles_per_owner + dest - owner * tiles_per_owner

            def one_pair(pair, carry):
                slot = start + 2 * pair
                next_slot = jnp.minimum(slot + 1, tile_max - 1)
                second = jnp.where(2 * pair + 1 < count, src_ref[0, next_slot], zero_tile)
                go_on = jnp.where(pair > 0, 1, 0)
                put(used + pair, (slot, src_ref[0, slot], second, target, go_on))
                return carry

            lax.fori_loop(0, pairs, one_pair, 0)
            return start + count, used + pairs, jnp.where(mine, target, carry[2])

        zero = jnp.int32(0)
        _, used, last = lax.fori_loop(0, dest_count, one_dest, (zero, zero, zero))
        turns = lax.div(used + UNROLL - 1, UNROLL)

        def one_pad(at, carry, put=put, last=last):
            put(at, (jnp.int32(0), zero_tile, zero_tile, last, jnp.int32(1)))
            return carry

        lax.fori_loop(used, turns * UNROLL, one_pad, 0)
        for column in range(UNROLL):
            list_ref[2 * rows_each + half, column] = turns

    group = min(8, piece)
    for index in range(pieces):
        copies_in[index].wait()

        def one_group(at, carry, index=index):
            for step in range(group):
                slot = index * piece + at * group + step
                tile = held_ref[slot]
                staged_ref[slot] = tile.T
                sum_ref[pl.ds(slot, 1), :] = jnp.sum(
                    tile.astype(jnp.float32), axis=0, keepdims=True
                )
            return carry

        lax.fori_loop(0, piece // group, one_group, 0)
        copies_out[index].start()

    sum_ref[tile_max:, :] = jnp.zeros((MOST, tile_size), jnp.float32)
    weight_ref[...] = jnp.zeros(weight_ref.shape, weight_ref.dtype)
    places = lax.broadcasted_iota(jnp.int32, (MOST, tile_size), 0)

    def weigh(owner, start):
        relative = lax.bitwise_xor(owner, my_row)
        chip = lax.div(relative, 2)
        for step in range(tiles_per_owner):
            count = count_ref[0, owner * tiles_per_owner + step]
            sums = jnp.where(places < count, sum_ref[pl.ds(start, MOST), :], 0.0)
            weight_ref[lax.bitwise_and(relative, 1), chip, step : step + 1, :] = jnp.sum(
                sums, axis=0, keepdims=True
            )
            start = start + count
        return start

    lax.fori_loop(0, dest_count // tiles_per_owner, weigh, jnp.int32(0))
    for copy in copies_out:
        copy.wait()


def prepare(place, tile_src, row_counts, tile_vals, row_size, tiles_per_owner, bits):
    tile_max, tile_size, _ = tile_vals.shape
    capacity = pair_capacity(tile_max, row_counts.shape[1])
    chips = row_size // 2
    return pl.pallas_call(
        functools.partial(prepare_kernel, tiles_per_owner, bits),
        out_shape=[
            jax.ShapeDtypeStruct(tile_vals.shape, tile_vals.dtype),
            jax.ShapeDtypeStruct((2, chips, EXTRA, tile_size), jnp.float32),
            jax.ShapeDtypeStruct((2 * (capacity // UNROLL) + 2, UNROLL), jnp.int32),
        ],
        in_specs=smem(3) + hbm(1),
        out_specs=hbm(1) + vmem(1) + smem(1),
        scratch_shapes=[
            pltpu.VMEM(tile_vals.shape, tile_vals.dtype),
            pltpu.VMEM(tile_vals.shape, tile_vals.dtype),
            pltpu.VMEM((tile_max + MOST, tile_size), jnp.float32),
            pltpu.SemaphoreType.DMA((8,)),
            pltpu.SemaphoreType.DMA((8,)),
        ],
        compiler_params=pltpu.CompilerParams(vmem_limit_bytes=24 * 2**20),
        name="prepare",
    )(place, tile_src, row_counts, tile_vals)


def pack_kernel(blocks, features_ref, *part_refs):
    rows = features_ref.shape[0] // blocks
    piece = features_ref.shape[1] // len(part_refs)
    for chunk, part_ref in enumerate(part_refs):
        lanes = slice(chunk * piece, (chunk + 1) * piece)
        part_ref[...] = jnp.concatenate(
            [features_ref[b * rows : (b + 1) * rows, lanes] for b in range(blocks)], axis=1
        )


def pack(features, blocks):
    rows = features.shape[0] // blocks
    width = features.shape[1] // CHUNKS * blocks
    return pl.pallas_call(
        functools.partial(pack_kernel, blocks),
        out_shape=[jax.ShapeDtypeStruct((rows, width), features.dtype)] * CHUNKS,
        in_specs=vmem(1),
        out_specs=vmem(CHUNKS),
        compiler_params=pltpu.CompilerParams(vmem_limit_bytes=4 * 2**20),
        name="pack",
    )(features)


def assemble_kernel(packed, masks, *refs):
    blocks = len(masks)
    block_refs = refs[:blocks]
    held_ref = refs[blocks + 1]
    staged_ref = refs[-1] if packed else held_ref
    col = lax.axis_index("col")
    rows, width = block_refs[0].shape

    def put(mask, ref):
        first = pl.multiple_of(lax.bitwise_xor(col, mask) * rows, rows)
        staged_ref[pl.ds(first, rows), :] = ref[...]

    for mask, ref in zip(masks, block_refs):
        put(mask, ref)
    if packed:
        piece = width // blocks
        for group in range(blocks):
            lanes = slice(group * piece, (group + 1) * piece)
            held_ref[group * rows : (group + 1) * rows, :] = jnp.concatenate(
                [staged_ref[b * rows : (b + 1) * rows, lanes] for b in range(blocks)], axis=1
            )
        own_ref = refs[blocks + 2]
        own_ref[...] = held_ref[pl.ds(pl.multiple_of(col * rows, rows), rows), :]
    zeros = held_ref.shape[0] - blocks * rows
    held_ref[blocks * rows :, :] = jnp.zeros((zeros, width), held_ref.dtype)


def assemble(gathered, after, tile_size, packed):
    blocks = len(gathered)
    masks = sorted(gathered, key=lambda mask: (2 * mask < blocks, mask))
    rows, width = gathered[0].shape
    out_shape = [jax.ShapeDtypeStruct((blocks * rows + tile_size, width), jnp.bfloat16)]
    scratch = []
    if packed:
        out_shape.append(jax.ShapeDtypeStruct((rows, width), jnp.bfloat16))
        scratch.append(pltpu.VMEM((blocks * rows, width), jnp.bfloat16))
    return pl.pallas_call(
        functools.partial(assemble_kernel, packed, masks),
        out_shape=out_shape,
        in_specs=vmem(blocks) + anywhere(1),
        out_specs=vmem(len(out_shape)),
        scratch_shapes=scratch,
        compiler_params=pltpu.CompilerParams(vmem_limit_bytes=4 * 2**20),
        cost_estimate=pl.CostEstimate(flops=0, bytes_accessed=4 * 2**20, transcendentals=0),
        name="assemble",
    )(*[gathered[mask] for mask in masks], after)


def product_kernel(half, rows, bits, list_ref, turned_ref, held_ref, weight_ref, out_ref):
    tile_max, tile_size, _ = turned_ref.shape
    chips, out_rows, width = out_ref.shape
    rows_each = (list_ref.shape[0] - 2) // 2
    tiles = rows // tile_size
    if out_rows > rows:
        out_ref[:, rows:, :] = weight_ref[half].astype(out_ref.dtype)

    def codes_of(row):
        line = list_ref[pl.ds(row, 1), :]
        return tuple(line[0, step] for step in range(UNROLL))

    def one_turn(turn, carry):
        running, codes = carry
        later = codes_of(half * rows_each + turn + 1)
        for step in range(UNROLL):
            slot, first, second, target, go_on = decode(codes[step], bits)
            left = jnp.concatenate(
                [turned_ref[slot], turned_ref[jnp.minimum(slot + 1, tile_max - 1)]], axis=1
            )
            first = pl.multiple_of(first * tile_size, tile_size)
            second = pl.multiple_of(second * tile_size, tile_size)
            right = jnp.concatenate(
                [held_ref[pl.ds(first, tile_size), :], held_ref[pl.ds(second, tile_size), :]],
                axis=0,
            )
            term = jnp.dot(left, right, preferred_element_type=jnp.float32)
            running = running * go_on.astype(jnp.float32) + term
            chip = lax.div(target, tiles)
            row = pl.multiple_of((target - chip * tiles) * tile_size, tile_size)
            out_ref[chip, pl.ds(row, tile_size), :] = running.astype(out_ref.dtype)
        return running, later

    turns = list_ref[2 * rows_each + half : 2 * rows_each + half + 1, :][0, 0]
    zeros = jnp.zeros((tile_size, width), jnp.float32)
    lax.fori_loop(0, turns, one_turn, (zeros, codes_of(half * rows_each)))


def product(half, pairs, turned, held, weights, rows, chips, extra, bits):
    return pl.pallas_call(
        functools.partial(product_kernel, half, rows, bits),
        out_shape=jax.ShapeDtypeStruct((chips, rows + extra, held.shape[1]), jnp.bfloat16),
        in_specs=vmem(4),
        out_specs=vmem(1)[0],
        compiler_params=pltpu.CompilerParams(vmem_limit_bytes=4 * 2**20),
        cost_estimate=pl.CostEstimate(
            flops=600000000, bytes_accessed=6000000, transcendentals=0
        ),
        name="product",
    )(pairs, turned, held, weights)


def update_kernel(kept_ref, *refs):
    *arrived_refs, iterate_ref, restart_ref, scale_ref, out_ref = refs
    rows = out_ref.shape[0]
    summed = kept_ref[:rows, :]
    for ref in arrived_refs:
        summed = summed + ref[:rows, :].astype(jnp.float32)
    out_ref[...] = (
        scale_ref[...] * (summed + iterate_ref[...].astype(jnp.float32))
        + TELEPORT * restart_ref[...].astype(jnp.float32)
    ).astype(out_ref.dtype)


def update(kept, arrived, iterate, restart, scale):
    return pl.pallas_call(
        update_kernel,
        out_shape=jax.ShapeDtypeStruct(iterate.shape, iterate.dtype),
        in_specs=vmem(len(arrived) + 4),
        out_specs=vmem(1)[0],
        compiler_params=pltpu.CompilerParams(vmem_limit_bytes=4 * 2**20),
        cost_estimate=pl.CostEstimate(flops=0, bytes_accessed=1, transcendentals=0),
        name="update",
    )(kept, *arrived, iterate, restart, scale)


def exchange(block, axis, mask, size):
    return lax.ppermute(block, axis, [(i, i ^ mask) for i in range(size)])


def gather_line(block, size, masks):
    return {mask: exchange(block, "col", mask, size) for mask in masks}


def reduce_chips(both, cut, chip_bits, row_size):
    kept, arrived = [], []
    for half in range(2):
        state = both[:, :cut] if half == 0 else both[:, cut:]
        state = state.reshape((2,) * len(chip_bits) + state.shape[1:])
        left = list(chip_bits)
        turn = half % len(chip_bits)
        got = None
        for bit in chip_bits[turn:] + chip_bits[:turn]:
            if got is not None:
                state = state + got.astype(jnp.float32)
            axis = left.index(bit)
            send = lax.index_in_dim(state, 1, axis, keepdims=False).astype(jnp.bfloat16)
            state = lax.index_in_dim(state, 0, axis, keepdims=False)
            got = exchange(send, "row", 1 << bit, row_size)
            left.remove(bit)
        kept.append(state)
        arrived.append(got)
    return jnp.concatenate(kept), jnp.concatenate(arrived)


def on_device(features, tile_vals, tile_src, row_counts):
    row_size = lax.axis_size("row")
    blocks = lax.axis_size("col")
    my_row = lax.axis_index("row").astype(jnp.int32)
    my_col = lax.axis_index("col").astype(jnp.int32)
    tile_size = tile_vals.shape[1]
    dest_count = row_counts.shape[1]
    rows = features.shape[0] // blocks
    source_tiles = features.shape[0] // tile_size
    width = features.shape[1] * blocks // CHUNKS
    piece = features.shape[1] // CHUNKS
    tiles_per_owner = dest_count // row_size
    chips = row_size // 2
    chip_bits = list(range(row_size.bit_length() - 2, 0, -1))
    bits = code_bits(tile_vals.shape[0], source_tiles, dest_count // 2)
    place = jnp.stack([my_row, my_col, jnp.int32(source_tiles)])

    parts = pack(features, blocks)

    turned, weights, pairs = prepare(
        place, tile_src, row_counts, tile_vals, row_size, tiles_per_owner, bits
    )

    gathered = [{0: parts[0], **gather_line(parts[0], blocks, range(1, blocks))}, None]
    early = [mask for mask in range(1, blocks) if 2 * mask >= blocks]
    late = [mask for mask in range(1, blocks) if mask not in early]
    iterates = [None] * CHUNKS
    restarts = [None] * CHUNKS
    scale = None
    last = place
    for phase in range(ITERS * CHUNKS):
        chunk = phase % CHUNKS
        after = 1 - chunk
        first = phase < CHUNKS
        extra = EXTRA if phase == 0 else 0
        if phase > 0:
            iterates[after] = last = update(*pending)
        held, *own = assemble(gathered[chunk], last, tile_size, first)
        if first:
            iterates[chunk] = restarts[chunk] = own[0]
        if phase == 0:
            held, coming = lax.optimization_barrier((held, parts[1]))
        elif phase + 1 < ITERS * CHUNKS:
            coming = iterates[after]
        else:
            coming = None
        if coming is not None:
            gathered[after] = {0: coming, **gather_line(coming, blocks, early)}
        sent = product(1, pairs, turned, held, weights, rows, chips, extra, bits)
        other = exchange(sent, "row", 1, row_size)
        kept = product(0, pairs, turned, held, weights, rows, chips, extra, bits)
        both = kept.astype(jnp.float32) + other.astype(jnp.float32)
        if coming is not None:
            coming, both = lax.optimization_barrier((coming, both))
            gathered[after].update(gather_line(coming, blocks, late))
        if phase + 1 < ITERS * CHUNKS:
            kept, arrived = reduce_chips(both, rows // 2, chip_bits, row_size)
            arrived = [arrived]
        else:
            kept = both[0]
            arrived = [
                exchange(both[mask].astype(jnp.bfloat16), "row", 2 * mask, row_size)
                for mask in range(chips - 1, 0, -1)
            ]
        if phase == 0:
            weight_rows = slice(rows, rows + tiles_per_owner)
            total = 1.0 + kept[weight_rows] + arrived[0][weight_rows].astype(jnp.float32)
            scale = jnp.broadcast_to(
                ((1.0 - TELEPORT) / total).reshape(rows, 1), (rows, width)
            )
        pending = (kept, arrived, iterates[chunk], restarts[chunk], scale)
    iterates[chunk] = update(*pending)
    iterates = lax.optimization_barrier(iterates)
    out = jnp.stack(iterates).reshape(CHUNKS, rows, blocks, piece).transpose(1, 2, 0, 3)
    return out.reshape(rows, CHUNKS * width)


def solution(mesh):
    placed = (P("row", "col"), P("row", "col", None), P("row", "col"), P("row", "col"))
    return jax.shard_map(
        on_device, mesh=mesh, in_specs=placed, out_specs=P(("row", "col"), None), check_vma=False
    )
```
